32 devices in a mesh: pipe: 2 (over x), dp: 4 (over z), tensor: 4 (over y, core).
Axes of the slice: x: 2, y: 2, z: 4, core: 2. Of those that a mesh axis runs over, the one named last changes fastest.
Arguments:
- section_input: bfloat16 [2, 24, 512, 768], P('pipe', 'dp', 'tensor'), may hold values from -6 to 6
- lengths: int32 [24, 2], P('dp'), may hold values from 32 to 512, as said below
- norm_gain: float32 [2, 3, 768], P('pipe'), may hold values from 0.5 to 1.5
- attn_in: bfloat16 [2, 3, 768, 768], P('pipe', None, None, 'tensor'), may hold values from -0.21875 to 0.21875
- attn_out: bfloat16 [2, 768, 768], P('pipe', 'tensor'), may hold values from -2.5 to 2.5
- cross_first: bfloat16 [2, 768, 768], P('pipe', None, 'tensor'), may hold values from -0.21875 to 0.21875
- cross_second: bfloat16 [2, 768, 768], P('pipe', None, 'tensor')
- ffn_in: bfloat16 [2, 768, 3072], P('pipe', None, 'tensor'), may hold values from -0.21875 to 0.21875
- ffn_out: bfloat16 [2, 3072, 768], P('pipe', 'tensor'), may hold values from -0.109375 to 0.109375
- rel_bias: bfloat16 [2, 32, 12], P('pipe', None, 'tensor'), may hold values from -4 to 4
- out_grad: bfloat16 [2, 24, 512, 768], P('pipe', 'dp', 'tensor'), may hold values from -6 to 6
Outputs:
- section_output: bfloat16 [2, 24, 512, 768], P('pipe', 'dp', 'tensor')
- input_grad: float32 [2, 24, 512, 768], P('pipe', 'dp', 'tensor')
- attn_in_grad: float32 [2, 3, 768, 768], P('pipe', None, 'dp', 'tensor')
- attn_out_grad: float32 [2, 768, 768], P('pipe', 'tensor', 'dp')
- cross_first_grad: float32 [2, 768, 768], P('pipe', 'dp', 'tensor')
- cross_second_grad: float32 [2, 768, 768], P('pipe', 'dp', 'tensor')
- ffn_in_grad: float32 [2, 768, 3072], P('pipe', 'dp', 'tensor')
- ffn_out_grad: float32 [2, 3072, 768], P('pipe', 'tensor', 'dp')
- rel_bias_grad: float32 [2, 32, 12], P('pipe', 'dp', 'tensor')
- norm_gain_grad: float32 [2, 3, 768], P('pipe', None, ('dp', 'tensor'))
The draws below stay inside these ranges and needn't reach their ends.
Inputs may be any that keep to these rules, and one draw needn't show every extreme that they name: `lengths`: in each block of 6 rows (one data index) one row, drawn from the seed, has length 512 in both columns.
All inputs are finite; a program needn't handle non-finite values.
Results may differ from the reference program's by a relative error of at most 0.03.
Values may be sent and summed in bfloat16 or wider, within the bound.
A program may use at most 320 MiB of HBM per device.

```python
import math
import jax
import jax.numpy as jnp
from jax import lax

D = 768
H = 12
DK = 64
FF = 3072
NB = 32
MAX_DIST = 128
SEQ = 512
MB = 6
EX = 1
HD = 768
BATCH = 24


def draw_lengths(key, part):
    key = jax.random.fold_in(key, 11)
    first_key, second_key = jax.random.split(key)
    block_rows = MB * EX
    drawn = jax.random.randint(first_key, (BATCH, 2), SEQ // 16, SEQ + 1, dtype=jnp.int32)
    chosen = jax.random.randint(second_key, (BATCH // block_rows,), 0, block_rows, dtype=jnp.int32)
    row_ids = jnp.arange(BATCH, dtype=jnp.int32)
    longest = row_ids % block_rows == jnp.repeat(chosen, block_rows)
    return jnp.where(longest[:, None], SEQ, drawn).astype(jnp.int32)


def draw_cross_second(key, part):
    key = jax.random.fold_in(key, 5)
    noise = jax.random.normal(key, (2, D, HD), jnp.float32)
    scales = jnp.array([D ** (-0.5), max(HD // 128, 1) ** (-0.5)], jnp.float32)
    return (noise * scales[:, None, None]).astype(jnp.bfloat16)


def block_scale(stream_key, extent, pieces, smallest, largest):
    level = 1.0
    for position, shards_of in pieces:
        heights = jax.random.uniform(jax.random.fold_in(jax.random.fold_in(stream_key, 6), position), (shards_of,), jnp.float32, smallest / len(pieces), largest / len(pieces))
        level = level * jnp.repeat(jnp.exp(heights), extent[position] // shards_of).reshape((-1,) + (1,) * (len(extent) - 1 - position))
    return level


def bell_draw(key, shape, deviation, most, shards=(), kind=jnp.bfloat16):
    values = deviation * jax.random.normal(key, shape, jnp.float32)
    if shards:
        values = values * block_scale(key, shape, shards, -0.22, 0.18)
    return jnp.clip(values, -most, most).astype(kind)


def setup_inputs(seed: int = 0) -> dict:
    streams_of = jax.random.split(jax.random.key(seed), 12)
    section_input = bell_draw(streams_of[0], (2, BATCH, SEQ, D), 1.0, 6.0, ((0, 2), (1, 4), (2, 4)))
    lengths = draw_lengths(jax.random.fold_in(streams_of[11], 71), 0)
    norm_gain = jnp.clip(1.0 + 0.1 * jax.random.normal(streams_of[2], (2, 3, D), jnp.float32), 0.5, 1.5)
    attn_in = bell_draw(streams_of[3], (2, 3, D, HD), D ** -0.5, 0.21875, ((0, 2), (3, 4)))
    attn_out = bell_draw(streams_of[4], (2, HD, D), (max(HD // 128, 1)) ** -0.5, 2.5, ((0, 2), (1, 4)))
    cross_first = bell_draw(streams_of[5], (2, D, HD), D ** -0.5, 0.21875, ((0, 2), (2, 4)))
    cross_second = draw_cross_second(jax.random.fold_in(streams_of[11], 71), 0)
    ffn_in = bell_draw(streams_of[7], (2, D, FF), D ** -0.5, 0.21875, ((0, 2), (2, 4)))
    ffn_out = bell_draw(streams_of[8], (2, FF, D), FF ** -0.5, 0.109375, ((0, 2), (1, 4)))
    rel_bias = bell_draw(streams_of[9], (2, NB, H), 1.0, 4.0, ((0, 2), (2, 4)))
    out_grad = bell_draw(streams_of[10], (2, BATCH, SEQ, D), 1.0, 6.0, ((0, 2), (1, 4), (2, 4)))
    return {"section_input": section_input, "lengths": lengths, "norm_gain": norm_gain, "attn_in": attn_in, "attn_out": attn_out, "cross_first": cross_first, "cross_second": cross_second, "ffn_in": ffn_in, "ffn_out": ffn_out, "rel_bias": rel_bias, "out_grad": out_grad}


@jax.custom_vjp
def low(v):
    return lax.optimization_barrier(v.astype(jnp.bfloat16)).astype(jnp.float32)

@jax.custom_vjp
def low_back(v):
    return v

def low_keep(v):
    return (low(v), None)

def low_pass(kept, grad):
    return (grad,)

def back_keep(v):
    return (v, None)

def back_low(kept, grad):
    return (low(grad),)
low.defvjp(low_keep, low_pass)
low_back.defvjp(back_keep, back_low)
norm_epsilon = 1e-06
masked_score = -1000000000.0

def bucket_map(rows_in, cols_in, both_ways):
    offset = cols_in - rows_in
    if both_ways:
        half_span = NB // 2
        sign_base = jnp.where(offset > 0, half_span, 0).astype(jnp.int32)
        distance = jnp.abs(offset)
    else:
        half_span = NB
        sign_base = jnp.zeros_like(offset)
        distance = jnp.maximum(-offset, 0)
    exact_span = half_span // 2
    count_n = jnp.zeros_like(offset)
    for level_id in range(exact_span + 1, half_span):
        found_at = 8 * MAX_DIST + 1
        for dist_n in range(exact_span, 8 * MAX_DIST + 1):
            level_at = exact_span + math.floor(math.log(dist_n / exact_span) / math.log(MAX_DIST / exact_span) * (half_span - exact_span))
            if level_at >= level_id:
                found_at = dist_n
                break
        count_n = count_n + (distance >= found_at).astype(jnp.int32)
    return sign_base + jnp.where(distance < exact_span, distance, exact_span + count_n)

def normalize(values, gain_row):
    return values * lax.rsqrt(lax.optimization_barrier(jnp.mean(values * values, axis=-1, keepdims=True)) + norm_epsilon) * gain_row

def project(left, right):
    return jnp.dot(left, right, precision=lax.Precision.HIGHEST, preferred_element_type=jnp.float32)

def attend(queries, keys_in, values_in, bias_term, allowed):
    query_heads = queries.reshape(SEQ, H, DK)
    key_heads = keys_in.reshape(SEQ, H, DK)
    value_heads = values_in.reshape(SEQ, H, DK)
    scores = jnp.einsum('ihd,jhd->hij', query_heads, key_heads, precision=lax.Precision.HIGHEST) * 0.125 + bias_term
    scores = low_back(jnp.where(allowed[None], scores, masked_score))
    shifted = scores - lax.optimization_barrier(jnp.max(scores, axis=-1, keepdims=True))
    expo = jnp.exp(shifted)
    soft_probs = low(expo / lax.optimization_barrier(jnp.sum(expo, axis=-1, keepdims=True)))
    context = jnp.einsum('hij,jhd->ihd', soft_probs, value_heads, precision=lax.Precision.HIGHEST).reshape(SEQ, HD)
    return low(low_back(context))

def self_block(normed, w_in, w_out, bias_term, allowed):
    queries = low(low_back(project(normed, w_in[0])))
    keys_in = low(low_back(project(normed, w_in[1])))
    values_in = low(low_back(project(normed, w_in[2])))
    context = attend(queries, keys_in, values_in, bias_term, allowed)
    return low_back(project(context, w_out))

def feed(hidden, gain_row, f_in, f_out):
    normed = low(normalize(hidden, gain_row))
    pre_act = low_back(project(normed, f_in))
    activated = low(jax.nn.gelu(pre_act, approximate=True))
    return low_back(project(activated, f_out))

def reference(section_input, lengths, norm_gain, attn_in, attn_out, cross_first, cross_second, ffn_in, ffn_out, rel_bias, out_grad):
    params = tuple((item.astype(jnp.float32) for item in (norm_gain, attn_in, attn_out, cross_first, cross_second, ffn_in, ffn_out, rel_bias)))
    enc_x = section_input[0].astype(jnp.float32)
    dec_x = section_input[1].astype(jnp.float32)
    positions = jnp.arange(SEQ, dtype=jnp.int32)
    rows_idx = positions[:, None]
    cols_idx = positions[None, :]
    enc_hot = (bucket_map(rows_idx, cols_idx, True)[:, :, None] == jnp.arange(NB, dtype=jnp.int32)).astype(jnp.float32)
    dec_hot = (bucket_map(rows_idx, cols_idx, False)[:, :, None] == jnp.arange(NB, dtype=jnp.int32)).astype(jnp.float32)

    def forward(weights, enc_all, dec_all):
        gain_rows, w_in, w_out, c_first, c_second, f_in, f_out, bias_table = weights
        enc_bias = jnp.einsum('ijb,bh->hij', enc_hot, bias_table[0], precision=lax.Precision.HIGHEST)
        dec_bias = jnp.einsum('ijb,bh->hij', dec_hot, bias_table[1], precision=lax.Precision.HIGHEST)

        def one_example(example_items):
            src_x, tgt_x, length_row = example_items
            src_len = length_row[0]
            tgt_len = length_row[1]
            enc_allowed = jnp.broadcast_to(cols_idx < src_len, (SEQ, SEQ))
            h_one = src_x + self_block(low(normalize(src_x, gain_rows[0, 0])), w_in[0], w_out[0], enc_bias, enc_allowed)
            enc_out = h_one + feed(h_one, gain_rows[0, 2], f_in[0], f_out[0])
            memory = low(normalize(enc_out, gain_rows[0, 1]))
            mem_keys = low(low_back(project(memory, c_first[0])))
            mem_values = low(low_back(project(memory, c_second[0])))
            dec_allowed = (cols_idx < tgt_len) & (cols_idx <= rows_idx)
            d_one = tgt_x + self_block(low(normalize(tgt_x, gain_rows[1, 0])), w_in[1], w_out[1], dec_bias, dec_allowed)
            cross_normed = low(normalize(d_one, gain_rows[1, 1]))
            cross_query = low(low_back(project(cross_normed, c_first[1])))
            cross_context = attend(cross_query, mem_keys, mem_values, 0.0, enc_allowed)
            d_two = d_one + low_back(project(cross_context, c_second[1].T))
            dec_out = d_two + feed(d_two, gain_rows[1, 2], f_in[1], f_out[1])
            return (memory, dec_out)
        return lax.map(jax.checkpoint(one_example), (enc_all, dec_all, lengths))
    results, pullback = jax.vjp(forward, params, enc_x, dec_x)
    gradients, enc_grad, dec_grad = pullback((out_grad[0].astype(jnp.float32), out_grad[1].astype(jnp.float32)))
    section_output = jnp.stack([results[0], results[1]]).astype(jnp.bfloat16)
    input_grad = jnp.stack([enc_grad, dec_grad])
    gain_grad, w_in_grad, w_out_grad, first_grad, second_grad, f_in_grad, f_out_grad, bias_grad = gradients
    return (section_output, input_grad, w_in_grad, w_out_grad, first_grad, second_grad, f_in_grad, f_out_grad, bias_grad, gain_grad)
```

```python
import math
from functools import partial

import jax
import jax.numpy as jnp
from jax import lax
from jax.experimental import pallas as pl
from jax.experimental.pallas import tpu as pltpu
from jax.sharding import PartitionSpec as P

NB = 32
MAX_DIST = 128
DK = 64
EPS = 1e-06
MASKED = -1000000000.0
MESH = pl.DeviceIdType.MESH
bf16, f32 = jnp.bfloat16, jnp.float32
PAIR = 128
G_IN, G_MID, G_FFN, G_DFFN, G_DMID, G_DATT = range(6)
S_ATT, S_MID, S_FFN, S_DMEM, S_DFFN, S_DMID, S_DIN = range(7)


def bucket_list(offsets, both_ways):
    half = NB // 2 if both_ways else NB
    exact = half // 2
    out = []
    for r in offsets:
        base = half if both_ways and r > 0 else 0
        n = abs(r) if both_ways else max(-r, 0)
        if n < exact:
            out.append(base + n)
        else:
            at = exact + math.floor(
                math.log(n / exact) / math.log(MAX_DIST / exact) * (half - exact)
            )
            out.append(base + min(half - 1, at))
    return out


def nt(a, b):
    return lax.dot_general(a, b, (((1,), (1,)), ((), ())), preferred_element_type=f32)


def nn(a, b):
    return lax.dot_general(a, b, (((1,), (0,)), ((), ())), preferred_element_type=f32)


def tn(a, b):
    return lax.dot_general(a, b, (((0,), (0,)), ((), ())), preferred_element_type=f32)


def section_kernel(
    x_ref, cot_ref, wown, wpeer, gain_ref, len_ref, diag_ref,
    sec_ref, ing_ref, gown, gpeer, dbias_ref, dgain_ref,
    wqkv, wo, w1, w2, wf1, wf2, bias,
    fin, qkv, ctx, lse, h1, fatt, mid, kvs, kvr, cq, cctx, clse, fmid,
    r2, ffnf, fffn, dctx, rsa, rss, rsr, stage,
    wsem, gs, gr, ss, sr, ps, pr, osem,
):
    ex = x_ref.shape[0]
    tb, width = x_ref.shape[2], x_ref.shape[3]
    rows = 2 * tb
    kq = wo.shape[0] // 2
    kc = wo.shape[0]
    fq = wf1.shape[0] // 2
    fc = wf1.shape[0]
    seq = 2 * rows
    heads = kc // DK
    pairs = kc // PAIR

    tensor = lax.axis_index("tensor")
    pipe = lax.axis_index("pipe")
    core = lax.rem(tensor, 2)
    partner = {"tensor": tensor + 1 - 2 * core}
    other = {"pipe": 1 - pipe}

    barrier = pltpu.get_barrier_semaphore()
    pl.semaphore_signal(barrier, 1, device_id=partner, device_id_type=MESH)
    pl.semaphore_signal(barrier, 1, device_id=other, device_id_type=MESH)

    def weight_copies():
        out = []
        for side, src in enumerate((wown, wpeer)):
            for i in range(3):
                out.append((src.at[pl.ds(i * kq, kq)], wqkv.at[pl.ds((2 * i + side) * kq, kq)]))
            for i, dst in enumerate((wo, w1, w2)):
                out.append((src.at[pl.ds((3 + i) * kq, kq)], dst.at[pl.ds(side * kq, kq)]))
            for i, dst in enumerate((wf1, wf2)):
                out.append((src.at[pl.ds(6 * kq + i * fq, fq)], dst.at[pl.ds(side * fq, fq)]))
        return [
            pltpu.make_async_copy(a, b, wsem.at[i]) for i, (a, b) in enumerate(out)
        ]

    copies = weight_copies()
    for cp in copies:
        cp.start()

    def bias_body(h, _):
        wide = jnp.broadcast_to(diag_ref[pl.ds(h, 1), :], (seq, 2 * seq))
        bias[h] = pltpu.roll(wide, 0, 1, stride=1, stride_axis=0)[:, :seq].astype(bf16)
        return 0

    lax.fori_loop(0, heads, bias_body, 0)
    dgain_ref[...] = jnp.zeros_like(dgain_ref)
    for cp in copies:
        cp.wait()
    pl.semaphore_wait(barrier, 2)

    lane = lax.broadcasted_iota(jnp.int32, (1, PAIR), 1)
    half_f = [jnp.where(lane // DK == hh, 1.0, 0.0) for hh in range(2)]
    half_b = [m.astype(bf16) for m in half_f]
    key_at = lax.broadcasted_iota(jnp.int32, (1, seq), 1)

    def key_mask(length):
        return jnp.where(key_at < length, 0.0, MASKED)

    def gather_copy(kind, buf, e):
        return pltpu.make_async_remote_copy(
            buf.at[e, :, core], buf.at[e, :, core], gs.at[kind, e], gr.at[kind, e],
            device_id=partner, device_id_type=MESH,
        )

    def gather_start(kind, buf, e, value):
        buf[e, :, core] = value.reshape(2, tb, width)
        gather_copy(kind, buf, e).start()

    def gather_use(kind, buf, e, fn):
        def body(i, _):
            ch = lax.rem(core + i, 2)

            @pl.when(i == 1)
            def _():
                gather_copy(kind, buf, e).wait()

            fn(buf[e, :, ch].reshape(rows, width), ch)
            return 0

        lax.fori_loop(0, 2, body, 0)

    def scatter(kind, e, slot, fn):
        copy = pltpu.make_async_remote_copy(
            rss.at[slot], rsr.at[slot], ss.at[kind, e], sr.at[kind, e],
            device_id=partner, device_id_type=MESH,
        )

        def body(i, _):
            ch = lax.rem(core + 1 + i, 2)
            rsa[...] = fn(ch)

            @pl.when(i == 0)
            def _():
                rss[slot] = rsa[...].astype(bf16)
                copy.start()

            return 0

        lax.fori_loop(0, 2, body, 0)
        copy.wait()
        return rsa[...] + rsr[slot].astype(f32)

    def norm(v, row):
        inv = lax.rsqrt(jnp.mean(v * v, axis=-1, keepdims=True) + EPS)
        return (v * inv * gain_ref[pl.ds(row, 1), :]).astype(bf16)

    def norm_back(v, row, grad):
        inv = lax.rsqrt(jnp.mean(v * v, axis=-1, keepdims=True) + EPS)
        unit = v * inv
        dgain_ref[pl.ds(row, 1), :] += jnp.sum(grad * unit, axis=0, keepdims=True)
        gg = grad * gain_ref[pl.ds(row, 1), :]
        return inv * (gg - unit * jnp.mean(gg * unit, axis=-1, keepdims=True))

    def attend(load_q, load_k, load_v, length, use_bias, store_ctx, store_lse):
        mask = key_mask(length)

        def body(yb, _):
            lse_t = jnp.zeros((rows, PAIR), f32)
            for p in range(pairs):
                lanes = pl.ds(p * PAIR, PAIR)
                k, v, q = load_k(lanes), load_v(lanes), load_q(yb, lanes)
                total, scale = None, None
                for hh in range(2):
                    h = 2 * p + hh
                    s = nt(q * half_b[hh], k) + mask
                    if use_bias:
                        s = s + bias[h, pl.ds(yb * rows, rows), :].astype(f32)
                    top = jnp.max(s, axis=-1, keepdims=True)
                    w = jnp.exp(s - top)
                    den = jnp.sum(w, axis=-1, keepdims=True)
                    part = nn(w.astype(bf16), v * half_b[hh])
                    total = part if total is None else total + part
                    inv = (1.0 / den) * half_f[hh]
                    scale = inv if scale is None else scale + inv
                    lse_t = jnp.where(lane == h, top + jnp.log(den), lse_t)
                store_ctx(yb, lanes, (total * scale).astype(bf16))
            store_lse(yb, lse_t)
            return 0

        lax.fori_loop(0, 2, body, 0)

    def attend_back(
        load_q, load_k, load_v, load_do, load_o, load_lse, length, dsacc, store_dq, store_dk, store_dv
    ):
        mask = key_mask(length)

        def body(p, _):
            lanes = pl.ds(pl.multiple_of(p * PAIR, PAIR), PAIR)
            k, v = load_k(lanes), load_v(lanes)
            dk = dv = None
            for yb in range(2):
                q, do = load_q(yb, lanes), load_do(yb, lanes)
                both = do.astype(f32) * load_o(yb, lanes).astype(f32)
                lse_t = load_lse(yb)
                dq = None
                for hh in range(2):
                    h = 2 * p + hh
                    qm, dom = q * half_b[hh], do * half_b[hh]
                    lse_c = jnp.sum(jnp.where(lane == h, lse_t, 0.0), axis=-1, keepdims=True)
                    delta = jnp.sum(both * half_f[hh], axis=-1, keepdims=True)
                    s = nt(qm, k) + mask
                    if dsacc is not None:
                        s = s + bias[h, pl.ds(yb * rows, rows), :].astype(f32)
                    w = jnp.exp(s - lse_c)
                    ds = w * (nt(dom, v) - delta)
                    wb, db = w.astype(bf16), ds.astype(bf16)
                    if dsacc is not None:
                        dsacc[h, pl.ds(yb * rows, rows), :] += ds
                    dvp, dkp, dqp = tn(wb, dom), tn(db, qm), nn(db, k * half_b[hh])
                    dv = dvp if dv is None else dv + dvp
                    dk = dkp if dk is None else dk + dkp
                    dq = dqp if dq is None else dq + dqp
                store_dq(yb, lanes, dq.astype(bf16))
            store_dk(lanes, dk.astype(bf16))
            store_dv(lanes, dv.astype(bf16))
            return 0

        lax.fori_loop(0, pairs, body, 0)

    def block_of(ref, *at):
        def lanes_at(first, lanes):
            return pl.ds(lanes.start + first, PAIR) if first else lanes

        def load_rows(first=0):
            return lambda yb, lanes: ref[(*at, yb, slice(None), slice(None), lanes_at(first, lanes))].reshape(rows, PAIR)

        def load_all(first=0):
            return lambda lanes: ref[(*at, slice(None), slice(None), slice(None), lanes_at(first, lanes))].reshape(seq, PAIR)

        def store_rows(first=0):
            def store(yb, lanes, value):
                ref[(*at, yb, slice(None), slice(None), lanes_at(first, lanes))] = value.reshape(2, tb, PAIR)

            return store

        def store_all(first=0):
            def store(lanes, value):
                ref[(*at, slice(None), slice(None), slice(None), lanes_at(first, lanes))] = value.reshape(2, 2, tb, PAIR)

            return store

        return load_rows, load_all, store_rows, store_all

    def in_rows(e):
        return x_ref[e].reshape(rows, width).astype(f32)

    def cot_rows(e):
        return cot_ref[e].reshape(rows, width)

    def half_rows(ref, e, ch, count):
        return ref[e, :, ch].reshape(rows, count)

    def self_forward(e, slot, length):
        gather_start(G_IN, fin, e, norm(in_rows(e), 0))

        def project(a, ch):
            qkv[e, :, ch] = nt(a, wqkv[...]).astype(bf16).reshape(2, tb, 3 * kc)

        gather_use(G_IN, fin, e, project)
        lr, la, _, _ = block_of(qkv, e)
        _, _, store_ctx, _ = block_of(ctx, e)

        def store_lse(yb, value):
            lse[e, yb] = value

        attend(lr(), la(kc), la(2 * kc), length, True, store_ctx(), store_lse)
        h1[e] = in_rows(e) + scatter(
            S_ATT, e, slot, lambda ch: nn(half_rows(ctx, e, ch, kc), wo[...])
        )

    def ffn_forward(e, slot, src, act, dg):
        gather_start(G_FFN, ffnf, e, norm(src[e], 2))
        third = fc // 3

        def expand(a, ch):
            for i in range(3):
                pre = nt(a, wf1[pl.ds(i * third, third), :])
                sq = pre * pre
                th = jnp.tanh(0.7978845608028654 * pre * (1.0 + 0.044715 * sq))
                gate = 0.5 + 0.5 * th
                slope = gate + (0.5 * 0.7978845608028654) * pre * (1.0 - th * th) * (
                    1.0 + (3 * 0.044715) * sq
                )
                lanes = pl.ds(i * third, third)
                act[e, :, ch, :, lanes] = (pre * gate).astype(bf16).reshape(2, tb, third)
                dg[e, :, ch, :, lanes] = slope.astype(bf16).reshape(2, tb, third)

        gather_use(G_FFN, ffnf, e, expand)
        return src[e] + scatter(S_FFN, e, slot, lambda ch: nn(half_rows(act, e, ch, fc), wf2[...]))

    def ffn_back(e, slot, grad_b, grad_f, src, act, dg):
        gather_start(G_DFFN, fffn, e, grad_b)
        third = fc // 3

        def contract(a, ch):
            for i in range(3):
                lanes = pl.ds(i * third, third)
                dact = nt(a, wf2[pl.ds(i * third, third), :])
                slope = dg[e, :, ch, :, lanes].reshape(rows, third).astype(f32)
                dg[e, :, ch, :, lanes] = (dact * slope).astype(bf16).reshape(2, tb, third)

        gather_use(G_DFFN, fffn, e, contract)
        dn = scatter(S_DFFN, e, slot, lambda ch: nn(half_rows(dg, e, ch, fc), wf1[...]))
        return grad_f() + norm_back(src[e], 2, dn)

    def context_grad(kind, buf, e, w):
        def project(a, ch):
            dctx[0, :, ch] = nt(a, w[...]).astype(bf16).reshape(2, tb, kc)

        gather_use(kind, buf, e, project)

    def self_back(e, slot, length, dsacc):
        gather_start(G_DATT, fatt, e, r2[e].astype(bf16))
        context_grad(G_DATT, fatt, e, wo)
        lr, la, sr_, sa_ = block_of(qkv, e)
        ldo = block_of(dctx, 0)[0]
        lo = block_of(ctx, e)[0]
        attend_back(
            lr(), la(kc), la(2 * kc), ldo(), lo(), lambda yb: lse[e, yb], length, dsacc,
            sr_(), sa_(kc), sa_(2 * kc),
        )
        dn = scatter(S_DIN, e, slot, lambda ch: nn(half_rows(qkv, e, ch, 3 * kc), wqkv[...]))
        ing_ref[e] = (r2[e] + norm_back(in_rows(e), 0, dn)).astype(ing_ref.dtype).reshape(2, tb, width)

    def pass_copy(e):
        return pltpu.make_async_remote_copy(
            kvs.at[e], kvr.at[e], ps.at[e], pr.at[e], device_id=other, device_id_type=MESH
        )

    def weight_grad(count, load_a, load_b, where_to):
        def body(i, _):
            stage[0] = tn(load_a(i), load_b()).astype(bf16)
            for side, (ref, at) in enumerate(where_to(i)):
                cp = pltpu.make_async_copy(
                    stage.at[0, pl.ds(side * kq, kq)], ref.at[pl.ds(at, kq)], osem.at[side]
                )
                cp.start()
            for side, (ref, at) in enumerate(where_to(i)):
                pltpu.make_async_copy(
                    stage.at[0, pl.ds(side * kq, kq)], ref.at[pl.ds(at, kq)], osem.at[side]
                ).wait()
            return 0

        lax.fori_loop(0, count, body, 0)

    def columns(ref, *at):
        def load(i):
            lanes = pl.ds(pl.multiple_of(i * kc, PAIR), kc)
            if at:
                return ref[:, at[0], :, :, :, lanes].reshape(ex * seq, kc)
            return ref[:, :, :, :, lanes].reshape(ex * seq, kc)

        return load

    def whole(ref):
        return lambda: ref[...].reshape(ex * seq, width)

    def to_pair(at):
        return lambda i: ((gown, at + i * kq), (gpeer, at + i * kq))

    def to_one(ref, at):
        return lambda i: ((ref, at + i * kc), (ref, at + i * kc + kq))

    def ffn_weight_grads(act, dg):
        per = fq // kc
        for a, b, at in ((dg, ffnf, 6 * kq), (act, fffn, 6 * kq + fq)):
            load = columns(a)
            weight_grad(per, load, whole(b), to_one(gown, at))
            weight_grad(per, lambda i, load=load: load(i + per), whole(b), to_one(gpeer, at))

    def mid_weight_grads(a1, a2, b2):
        weight_grad(1, a1, whole(mid), to_pair(4 * kq))
        weight_grad(1, a2, whole(b2), to_pair(5 * kq))

    def self_weight_grads():
        weight_grad(3, columns(qkv), whole(fin), to_pair(0))
        weight_grad(1, columns(ctx), whole(fatt), to_pair(3 * kq))

    def bias_grads(dsacc):
        at_r = lax.broadcasted_iota(jnp.int32, (seq, seq), 0)
        at_c = lax.broadcasted_iota(jnp.int32, (seq, seq), 1)
        flip = jnp.where(at_r + at_c == seq - 1, 1.0, 0.0).astype(bf16)

        def body(h, _):
            turned = nn(dsacc[h].astype(bf16), flip)
            wide = jnp.concatenate([turned, jnp.zeros((seq, seq), f32)], axis=1)
            wide = pltpu.roll(wide, 0, 1, stride=1, stride_axis=0)
            dbias_ref[pl.ds(h, 1), :] = jnp.sum(wide, axis=0, keepdims=True)
            return 0

        lax.fori_loop(0, heads, body, 0)

    def loop(fn):
        def body(e, _):
            fn(e)
            return 0

        lax.fori_loop(0, ex, body, 0)

    def self_back_all(own_length):
        def run(dsacc):
            dsacc[...] = jnp.zeros_like(dsacc)
            loop(lambda e: self_back(e, lax.rem(e, 2), own_length(e), dsacc))
            bias_grads(dsacc)

        pl.run_scoped(run, pltpu.VMEM((heads, seq, seq), f32))
        self_weight_grads()

    feed = pltpu.VMEM((ex, 2, 2, tb, fc), bf16)

    @pl.when(pipe == 0)
    def _():
        def own_length(e):
            return len_ref[e, 0]

        def run(act, dg):
            def ahead(e):
                self_forward(e, 0, own_length(e))
                r2[e] = ffn_forward(e, 1, h1, act, dg)
                memory = norm(r2[e], 1)
                sec_ref[e] = memory.reshape(2, tb, width)
                gather_start(G_MID, mid, e, memory)

                def project(a, ch):
                    for i, w in enumerate((w1, w2)):
                        kvs[e, i, :, ch] = nt(a, w[...]).astype(bf16).reshape(2, tb, kc)

                gather_use(G_MID, mid, e, project)
                pass_copy(e).start()

            def back(e):
                pass_copy(e).wait()

                def partial_sum(ch):
                    return nn(kvr[e, 0, :, ch].reshape(rows, kc), w1[...]) + nn(
                        kvr[e, 1, :, ch].reshape(rows, kc), w2[...]
                    )

                dmem = cot_rows(e).astype(f32) + scatter(S_DMEM, e, 0, partial_sum)
                r2[e] = norm_back(r2[e], 1, dmem)
                r2[e] = ffn_back(e, 1, r2[e].astype(bf16), lambda: r2[e], h1, act, dg)

            loop(ahead)
            loop(back)
            ffn_weight_grads(act, dg)

        pl.run_scoped(run, feed, feed)
        first, second = columns(kvr, 0), columns(kvr, 1)
        mid_weight_grads(first, second, mid)
        self_back_all(own_length)

    @pl.when(pipe == 1)
    def _():
        def own_length(e):
            return len_ref[e, 1]

        loop(lambda e: self_forward(e, lax.rem(e, 2), own_length(e)))

        def run(act, dg):
            def there_and_back(e):
                gather_start(G_MID, mid, e, norm(h1[e], 1))

                def project(a, ch):
                    cq[e, :, ch] = nt(a, w1[...]).astype(bf16).reshape(2, tb, kc)

                gather_use(G_MID, mid, e, project)
                pass_copy(e).wait_recv()
                lq, _, sq, _ = block_of(cq, e)
                _, lk, _, _ = block_of(kvr, e, 0)
                _, lv, _, _ = block_of(kvr, e, 1)
                lc, _, sc, _ = block_of(cctx, e)

                def store_lse(yb, value):
                    clse[yb] = value

                attend(lq(), lk(), lv(), len_ref[e, 0], False, sc(), store_lse)
                r2[e] = h1[e] + scatter(
                    S_MID, e, 0, lambda ch: nn(half_rows(cctx, e, ch, kc), w2[...])
                )
                sec_ref[e] = ffn_forward(e, 1, r2, act, dg).astype(bf16).reshape(2, tb, width)
                r2[e] = ffn_back(
                    e, 0, cot_rows(e), lambda: cot_rows(e).astype(f32), r2, act, dg
                )
                gather_start(G_DMID, fmid, e, r2[e].astype(bf16))
                context_grad(G_DMID, fmid, e, w2)
                ldo = block_of(dctx, 0)[0]
                sk, sv = block_of(kvs, e, 0)[3], block_of(kvs, e, 1)[3]
                attend_back(
                    lq(), lk(), lv(), ldo(), lc(), lambda yb: clse[yb], len_ref[e, 0], None,
                    sq(), sk(), sv(),
                )
                pass_copy(e).start()
                dn = scatter(S_DMID, e, 1, lambda ch: nn(half_rows(cq, e, ch, kc), w1[...]))
                r2[e] += norm_back(h1[e], 1, dn)

            loop(there_and_back)
            ffn_weight_grads(act, dg)

        pl.run_scoped(run, feed, feed)
        mid_weight_grads(columns(cq), columns(cctx), fmid)
        loop(lambda e: pass_copy(e).wait_send())
        self_back_all(own_length)


def swap(value, axis):
    return lax.ppermute(value, axis, [(0, 2), (1, 3), (2, 0), (3, 1)])


def run_sections(x, cot, wown, wpeer, gains, lens, diag):
    ex, _, tb, width = x.shape
    rows, seq = 2 * tb, 4 * tb
    kq = DK * diag.shape[0] // 2
    kc = 2 * kq
    fq = (wown.shape[0] - 6 * kq) // 2
    fc = 2 * fq
    vmem = pl.BlockSpec(memory_space=pltpu.VMEM)
    hbm = pl.BlockSpec(memory_space=pl.ANY)
    smem = pl.BlockSpec(memory_space=pltpu.SMEM)
    full = (ex, 2, 2, tb)
    V = pltpu.VMEM
    scratch = [
        V((3 * kc, width), bf16), V((kc, width), bf16), V((kc, width), bf16), V((kc, width), bf16),
        V((fc, width), bf16), V((fc, width), bf16), V((kc // DK, seq, seq), bf16),
        V((*full, width), bf16),
        V((*full, 3 * kc), bf16),
        V((*full, kc), bf16),
        V((ex, 2, rows, PAIR), f32),
        V((ex, rows, width), f32),
        V((*full, width), bf16),
        V((*full, width), bf16),
        V((ex, 2, 2, 2, tb, kc), bf16),
        V((ex, 2, 2, 2, tb, kc), bf16),
        V((*full, kc), bf16),
        V((*full, kc), bf16),
        V((2, rows, PAIR), f32),
        V((*full, width), bf16),
        V((ex, rows, width), f32),
        V((*full, width), bf16),
        V((*full, width), bf16),
        V((1, 2, 2, tb, kc), bf16),
        V((rows, width), f32),
        V((2, rows, width), bf16),
        V((2, rows, width), bf16),
        V((1, kc, width), bf16),
        pltpu.SemaphoreType.DMA((16,)),
        pltpu.SemaphoreType.DMA((6, ex)), pltpu.SemaphoreType.DMA((6, ex)),
        pltpu.SemaphoreType.DMA((7, ex)), pltpu.SemaphoreType.DMA((7, ex)),
        pltpu.SemaphoreType.DMA((ex,)), pltpu.SemaphoreType.DMA((ex,)),
        pltpu.SemaphoreType.DMA((2,)),
    ]
    return pl.pallas_call(
        section_kernel,
        out_shape=(
            jax.ShapeDtypeStruct((ex, 2, tb, width), bf16),
            jax.ShapeDtypeStruct((ex, 2, tb, width), bf16),
            jax.ShapeDtypeStruct(wown.shape, bf16),
            jax.ShapeDtypeStruct(wown.shape, bf16),
            jax.ShapeDtypeStruct((8, 2 * seq), f32),
            jax.ShapeDtypeStruct((8, width), f32),
        ),
        in_specs=[vmem, vmem, hbm, hbm, vmem, smem, vmem],
        out_specs=(vmem, vmem, hbm, hbm, vmem, vmem),
        scratch_shapes=scratch,
        compiler_params=pltpu.CompilerParams(
            collective_id=0, has_side_effects=True, vmem_limit_bytes=64 * 2**20 - 65536
        ),
        name="sections",
    )(x, cot, wown, wpeer, gains, lens, diag)


def local(
    section_input, lengths, norm_gain, attn_in, attn_out, cross_first, cross_second,
    ffn_in, ffn_out, rel_bias, out_grad,
):
    pipe = lax.axis_index("pipe")
    tensor = lax.axis_index("tensor")
    side = tensor // 2
    batch, tb, width = section_input.shape[1:]
    ex = batch // 2
    seq = tb * lax.axis_size("tensor")
    kq, fq = attn_out.shape[1], ffn_out.shape[1]
    enc = pipe == 0

    wown = jnp.concatenate(
        [
            attn_in[0, 0].T * jnp.asarray(0.125, bf16),
            attn_in[0, 1].T,
            attn_in[0, 2].T,
            attn_out[0],
            cross_first[0].T * jnp.where(enc, 1.0, 0.125).astype(bf16),
            cross_second[0].T,
            ffn_in[0].T,
            ffn_out[0],
        ],
        0,
    )
    wpeer = swap(wown, "tensor")

    def mine(rows):
        parts = rows.reshape(2, ex, tb, width)
        got = swap(lax.dynamic_index_in_dim(parts, 1 - side, 0, keepdims=False), "tensor")
        own = lax.dynamic_index_in_dim(parts, side, 0, keepdims=False)
        return jnp.stack([jnp.where(side == 0, own, got), jnp.where(side == 0, got, own)], 1)

    def back(rows):
        got = swap(lax.dynamic_index_in_dim(rows, 1 - side, 1, keepdims=False), "tensor")
        own = lax.dynamic_index_in_dim(rows, side, 1, keepdims=False)
        return jnp.concatenate(
            [jnp.where(side == 0, own, got), jnp.where(side == 0, got, own)], 0
        )

    x, cot = mine(section_input[0]), mine(out_grad[0])
    lens = lax.dynamic_slice_in_dim(lengths, side * ex, ex, 0)

    offsets = list(range(seq)) + [0] + list(range(-seq + 1, 0))
    spots = jnp.where(
        enc,
        jnp.array(bucket_list(offsets, True), jnp.int32),
        jnp.array(bucket_list(offsets, False), jnp.int32),
    )
    hot = (spots[:, None] == jnp.arange(NB, dtype=jnp.int32)).astype(bf16)
    tables = jnp.concatenate([rel_bias[0], swap(rel_bias[0], "tensor")], 1)
    diag = jnp.einsum("mb,bh->hm", hot, tables, preferred_element_type=f32)
    hidden = jnp.logical_and(~enc, jnp.array(offsets, jnp.int32) > 0)
    diag = jnp.where(hidden, MASKED, diag)

    sec, ing, gown, gpeer, dbias, dgain = run_sections(
        x, cot, wown, wpeer, norm_gain[0], lens, diag
    )

    section_output = back(sec)[None]
    input_grad = back(ing)[None].astype(f32)
    total = gown.astype(f32) + swap(gpeer, "tensor").astype(f32)
    data = lax.axis_size("dp")
    packed = total.reshape(-1, data, width // data).transpose(1, 0, 2).astype(bf16)
    shard = lax.psum_scatter(packed, "dp", scatter_dimension=0, tiled=False).astype(f32)
    piece = [shard[i * kq : (i + 1) * kq] for i in range(6)]
    w_in = jnp.stack([piece[0].T * 0.125, piece[1].T, piece[2].T])
    first = piece[4].T * jnp.where(enc, 1.0, 0.125)
    spots_m = jnp.where(
        enc,
        jnp.array(bucket_list([seq - 1 - m for m in range(2 * seq)], True), jnp.int32),
        jnp.array(bucket_list([seq - 1 - m for m in range(2 * seq)], False), jnp.int32),
    )
    hot_m = (spots_m[:, None] == jnp.arange(NB, dtype=jnp.int32)).astype(f32)
    heads = 2 * (kq // DK)
    bsum = jnp.einsum("mb,hm->bh", hot_m, dbias[:heads], precision=lax.Precision.HIGHEST)
    bsum = bsum[:, : heads // 2] + swap(bsum[:, heads // 2 :], "tensor")
    bias_grad = lax.psum_scatter(bsum, "dp", scatter_dimension=0, tiled=True)
    gain_grad = lax.psum_scatter(
        dgain[None, :3], ("dp", "tensor"), scatter_dimension=2, tiled=True
    )
    return (
        section_output,
        input_grad,
        w_in[None],
        piece[3][None],
        first[None],
        piece[5].T[None],
        shard[6 * kq : 6 * kq + fq].T[None],
        shard[6 * kq + fq :][None],
        bias_grad[None],
        gain_grad,
    )


def solution(mesh):
    placed = (
        P("pipe", "dp", "tensor", None),
        P("dp", None),
        P("pipe", None, None),
        P("pipe", None, None, "tensor"),
        P("pipe", "tensor", None),
        P("pipe", None, "tensor"),
        P("pipe", None, "tensor"),
        P("pipe", None, "tensor"),
        P("pipe", "tensor", None),
        P("pipe", None, "tensor"),
        P("pipe", "dp", "tensor", None),
    )
    return jax.shard_map(
        local,
        mesh=mesh,
        in_specs=placed,
        out_specs=(
            P("pipe", "dp", "tensor", None),
            P("pipe", "dp", "tensor", None),
            P("pipe", None, "dp", "tensor"),
            P("pipe", "tensor", "dp"),
            P("pipe", "dp", "tensor"),
            P("pipe", "dp", "tensor"),
            P("pipe", "dp", "tensor"),
            P("pipe", "tensor", "dp"),
            P("pipe", "dp", "tensor"),
            P("pipe", None, ("dp", "tensor")),
        ),
        check_vma=False,
    )
```

```python
import math
from functools import partial

import jax
import jax.numpy as jnp
import numpy as np
from jax import lax
from jax.experimental import pallas as pl
from jax.experimental.pallas import tpu as pltpu
from jax.sharding import PartitionSpec as P

NB = 32
MAX_DIST = 128
DK = 64
EPS = 1e-06
MASKED = -1000000000.0
MESH = pl.DeviceIdType.MESH
bf16, f32 = jnp.bfloat16, jnp.float32
PAIR = 128
G_IN, G_MID, G_FFN, G_DFFN, G_DMID, G_DATT = range(6)
S_ATT, S_MID, S_FFN, S_DMEM, S_DFFN, S_DMID, S_DIN = range(7)


def bucket_list(offsets, both_ways):
    half = NB // 2 if both_ways else NB
    exact = half // 2
    out = []
    for r in offsets:
        base = half if both_ways and r > 0 else 0
        n = abs(r) if both_ways else max(-r, 0)
        if n < exact:
            out.append(base + n)
        else:
            at = exact + math.floor(
                math.log(n / exact) / math.log(MAX_DIST / exact) * (half - exact)
            )
            out.append(base + min(half - 1, at))
    return out


def nt(a, b):
    return lax.dot_general(a, b, (((1,), (1,)), ((), ())), preferred_element_type=f32)


def nn(a, b):
    return lax.dot_general(a, b, (((1,), (0,)), ((), ())), preferred_element_type=f32)


def tn(a, b):
    return lax.dot_general(a, b, (((0,), (0,)), ((), ())), preferred_element_type=f32)


W_Q, W_K, W_V, W_O, W_C1, W_C2, W_F1, W_F2 = range(8)


def section_kernel(
    xin, cin, w_in, w_out, c_1, c_2, f_1, f_2, gain_ref, len_ref, table_ref, hot_ref,
    sec_out, ing_out, zs, zr, fin_out, small_out, gown, ysend, yrecv,
    wqkv, wo, w1, w2, wf1, wf2, bias,
    xr, cot, sec, ing,
    fin, qkv, ctx, lse, h1, fatt, mid, kvs, kvr, cq, cctx, clse, fmid,
    r2, ffnf, fffn, dctx, rsa, rss, rsr, diag, small, small_c, small_y, small_z,
    lsem, xs, xg, ts, tg, ys, yg, zps, zpg, gs, gr, ss, sr, ps, pr, os, og, us, ug, vs, vg, ms, mg,
    *, direct,
):
    ex, _, tb, width = xr.shape
    rows = 2 * tb
    kq = wo.shape[0] // 2
    kc = wo.shape[0]
    fq = wf1.shape[2]
    fc = 2 * fq
    seq = 2 * rows
    heads = kc // DK
    pairs = kc // PAIR
    own_heads = heads // 2

    tensor = lax.axis_index("tensor")
    pipe = lax.axis_index("pipe")
    data = lax.axis_index("dp")
    count = lax.axis_size("dp")
    core = lax.rem(tensor, 2)
    side = tensor // 2
    parity = lax.rem(data, 2)
    partner = {"tensor": tensor + 1 - 2 * core}
    peer = {"tensor": lax.rem(tensor + 2, 4)}
    near = {"dp": data + 1 - 2 * parity}
    other = {"pipe": 1 - pipe}

    def away(step):
        return lax.rem(data + step, count)

    barrier = pltpu.get_barrier_semaphore()
    met = [partner, peer, other]
    met += [{"dp": away(i)} for i in range(1, count)] if direct else [near]
    for device in met:
        pl.semaphore_signal(barrier, 1, device_id=device, device_id_type=MESH)

    def remote(src, dst, send, recv, device):
        return pltpu.make_async_remote_copy(
            src, dst, send, recv, device_id=device, device_id_type=MESH
        )

    def own_copies(raw):
        pairs_of = [(w_in.at[i], raw.at[i]) for i in range(3)]
        pairs_of += [(w_out, wo.at[pl.ds(0, kq)]), (c_1, raw.at[3]), (c_2, raw.at[4])]
        pairs_of += [(f_1, wf1.at[0]), (f_2, wf2.at[0])]
        for e in range(ex):
            pairs_of.append((xin.at[side * ex + e], xr.at[e, side]))
        for e in range(ex):
            pairs_of.append((cin.at[side * ex + e], cot.at[e, side]))
        return [pltpu.make_async_copy(p, q, lsem.at[i]) for i, (p, q) in enumerate(pairs_of)]

    def x_copy(e):
        return remote(xin.at[(1 - side) * ex + e], xr.at[e, side], xs.at[0, e], xg.at[0, e], peer)

    def cot_copy(e):
        return remote(cin.at[(1 - side) * ex + e], cot.at[e, side], xs.at[1, e], xg.at[1, e], peer)

    def diag_copy():
        return remote(diag.at[0], diag.at[1], ts.at[0], tg.at[0], peer)

    half_kq, half_fq = kq // 2, wf1.shape[1] // 2

    def small_home(i, part):
        first = kq + part * half_kq
        if i < 3:
            return wqkv.at[pl.ds(pl.multiple_of(i * kc + first, 16), half_kq)]
        return (wo, w1, w2)[i - 3].at[pl.ds(pl.multiple_of(first, 16), half_kq)]

    def big_home(i, part):
        ref = (wf1, wf2)[i - W_F1]
        return ref.at[1, pl.ds(pl.multiple_of(part * half_fq, 16), half_fq)]

    def home(i, part):
        return big_home(i, part) if i >= W_F1 else small_home(i, part)

    def w_copy(i):
        if i >= W_F1:
            ref = (wf1, wf2)[i - W_F1]
            src = ref.at[0, pl.ds(pl.multiple_of(parity * half_fq, 16), half_fq)]
        else:
            src = fatt.at[i // 2, i % 2, parity, pl.ds(0, half_kq)]
        return remote(src, home(i, parity), ys.at[i], yg.at[i], peer)

    def w_pass(i):
        return remote(home(i, parity), home(i, parity), zps.at[i], zpg.at[i], near)

    def w_on(i):
        w_copy(i).wait_recv()
        w_pass(i).start()

    def w_done(i):
        w_pass(i).wait()

    def turned(i, value):
        if i < 3:
            wqkv[i * kc : i * kc + kq] = value
        elif i > 3:
            (w1, w2)[i - 4][0:kq] = value
        last = kq - DK
        fatt[i // 2, i % 2, 0, 0:DK] = value[last:]
        fatt[i // 2, i % 2, 0, DK:half_kq] = value[: half_kq - DK]
        fatt[i // 2, i % 2, 1, 0:half_kq] = value[half_kq - DK : last]

    def make_diag():
        values = tn(table_ref[...], hot_ref[pipe])
        at = lax.broadcasted_iota(jnp.int32, (1, 2 * seq), 1)
        hidden = jnp.logical_and(jnp.logical_and(at > 0, at < seq), pipe == 1)
        values = jnp.where(hidden, MASKED, values)
        diag[0, 0:own_heads] = values
        diag[0, own_heads:] = jnp.zeros((8 - own_heads, 2 * seq), f32)

    def begin(raw):
        copies = own_copies(raw)
        for cp in copies:
            cp.start()
        make_diag()
        pl.semaphore_wait(barrier, len(met))
        diag_copy().start()
        x_copy(0).start()
        scale_q = jnp.asarray(0.125, bf16)
        for i in range(3):
            copies[i].wait()
            value = raw[i].T
            turned(i, value * scale_q if i == 0 else value)
            w_copy(i).start()
        for e in range(1, ex):
            x_copy(e).start()
        copies[3].wait()
        turned(W_O, wo[0:kq])
        w_copy(W_O).start()
        scale_c = jnp.where(pipe == 0, 1.0, 0.125).astype(bf16)
        for i in (W_C1, W_C2):
            copies[i].wait()
            value = raw[i - 1].T
            turned(i, value * scale_c if i == W_C1 else value)
        for i in (W_F1, W_F2):
            copies[i].wait()

        def start_all(order):
            for i in order:
                w_copy(i).start()

        @pl.when(pipe == 0)
        def _():
            start_all((W_F1, W_F2, W_C1, W_C2))

        @pl.when(pipe == 1)
        def _():
            start_all((W_C1, W_C2, W_F1, W_F2))

        for e in range(ex):
            cot_copy(e).start()
        for cp in copies[8:]:
            cp.wait()

    pl.run_scoped(begin, pltpu.VMEM((5, width, kq), bf16))
    small[...] = jnp.zeros_like(small)
    diag_copy().wait()
    local_order = [(0, h) for h in range(own_heads)] + [(1, (h + 2) % 3) for h in range(own_heads)]
    for h, (from_side, at) in enumerate(local_order):
        wide = jnp.broadcast_to(diag[from_side, at : at + 1, :], (seq, 2 * seq))
        bias[h] = pltpu.roll(wide, 0, 1, stride=1, stride_axis=0)[:, :seq].astype(bf16)
    for i in range(3):
        w_on(i)
    for i in range(3):
        w_done(i)

    lane = lax.broadcasted_iota(jnp.int32, (1, PAIR), 1)
    half_f = [jnp.where(lane // DK == hh, 1.0, 0.0) for hh in range(2)]
    half_b = [m.astype(bf16) for m in half_f]
    key_at = lax.broadcasted_iota(jnp.int32, (1, seq), 1)

    def key_mask(length):
        return jnp.where(key_at < length, 0.0, MASKED)

    def gather_copy(kind, buf, e):
        return remote(
            buf.at[e, :, core], buf.at[e, :, core], gs.at[kind, e], gr.at[kind, e], partner
        )

    def gather_start(kind, buf, e, value):
        buf[e, :, core] = value.reshape(2, tb, width)
        gather_copy(kind, buf, e).start()

    def gather_use(kind, buf, e, fn):
        def body(i, _):
            ch = lax.rem(core + i, 2)

            @pl.when(i == 1)
            def _():
                gather_copy(kind, buf, e).wait()

            fn(buf[e, :, ch].reshape(rows, width), ch)
            return 0

        lax.fori_loop(0, 2, body, 0)

    def scatter(kind, e, slot, fn):
        copy = remote(rss.at[slot], rsr.at[slot], ss.at[kind, e], sr.at[kind, e], partner)

        def body(i, _):
            ch = lax.rem(core + 1 + i, 2)
            rsa[...] = fn(ch)

            @pl.when(i == 0)
            def _():
                rss[slot] = rsa[...].astype(bf16)
                copy.start()

            return 0

        lax.fori_loop(0, 2, body, 0)
        copy.wait()
        return rsa[...] + rsr[slot].astype(f32)

    def norm(v, row):
        inv = lax.rsqrt(jnp.mean(v * v, axis=-1, keepdims=True) + EPS)
        return (v * inv * gain_ref[pl.ds(row, 1), :]).astype(bf16)

    def norm_back(v, row, grad):
        inv = lax.rsqrt(jnp.mean(v * v, axis=-1, keepdims=True) + EPS)
        unit = v * inv
        small[pl.ds(row, 1), 0:width] += jnp.sum(grad * unit, axis=0, keepdims=True)
        gg = grad * gain_ref[pl.ds(row, 1), :]
        return inv * (gg - unit * jnp.mean(gg * unit, axis=-1, keepdims=True))

    def attend(load_q, load_k, load_v, length, use_bias, store_ctx, store_lse):
        mask = key_mask(length)

        def body(yb, _):
            lse_t = jnp.zeros((rows, PAIR), f32)
            for p in range(pairs):
                lanes = pl.ds(p * PAIR, PAIR)
                k, v, q = load_k(lanes), load_v(lanes), load_q(yb, lanes)
                total, scale = None, None
                for hh in range(2):
                    h = 2 * p + hh
                    s = nt(q * half_b[hh], k) + mask
                    if use_bias:
                        s = s + bias[h, pl.ds(yb * rows, rows), :].astype(f32)
                    top = jnp.max(s, axis=-1, keepdims=True)
                    w = jnp.exp(s - top)
                    den = jnp.sum(w, axis=-1, keepdims=True)
                    part = nn(w.astype(bf16), v * half_b[hh])
                    total = part if total is None else total + part
                    inv = (1.0 / den) * half_f[hh]
                    scale = inv if scale is None else scale + inv
                    lse_t = jnp.where(lane == h, top + jnp.log(den), lse_t)
                store_ctx(yb, lanes, (total * scale).astype(bf16))
            store_lse(yb, lse_t)
            return 0

        lax.fori_loop(0, 2, body, 0)

    def attend_back(
        load_q, load_k, load_v, load_do, load_o, load_lse, length, dsacc, store_dq, store_dk, store_dv
    ):
        mask = key_mask(length)

        def body(p, _):
            lanes = pl.ds(pl.multiple_of(p * PAIR, PAIR), PAIR)
            k, v = load_k(lanes), load_v(lanes)
            dk = dv = None
            for yb in range(2):
                q, do = load_q(yb, lanes), load_do(yb, lanes)
                both = do.astype(f32) * load_o(yb, lanes).astype(f32)
                lse_t = load_lse(yb)
                dq = None
                for hh in range(2):
                    h = 2 * p + hh
                    qm, dom = q * half_b[hh], do * half_b[hh]
                    lse_c = jnp.sum(jnp.where(lane == h, lse_t, 0.0), axis=-1, keepdims=True)
                    delta = jnp.sum(both * half_f[hh], axis=-1, keepdims=True)
                    s = nt(qm, k) + mask
                    if dsacc is not None:
                        s = s + bias[h, pl.ds(yb * rows, rows), :].astype(f32)
                    w = jnp.exp(s - lse_c)
                    ds = w * (nt(dom, v) - delta)
                    wb, db = w.astype(bf16), ds.astype(bf16)
                    if dsacc is not None:
                        dsacc[h, pl.ds(yb * rows, rows), :] += ds
                    dvp, dkp, dqp = tn(wb, dom), tn(db, qm), nn(db, k * half_b[hh])
                    dv = dvp if dv is None else dv + dvp
                    dk = dkp if dk is None else dk + dkp
                    dq = dqp if dq is None else dq + dqp
                store_dq(yb, lanes, dq.astype(bf16))
            store_dk(lanes, dk.astype(bf16))
            store_dv(lanes, dv.astype(bf16))
            return 0

        lax.fori_loop(0, pairs, body, 0)

    def block_of(ref, *at):
        def lanes_at(first, lanes):
            return pl.ds(lanes.start + first, PAIR) if first else lanes

        def load_rows(first=0):
            return lambda yb, lanes: ref[(*at, yb, slice(None), slice(None), lanes_at(first, lanes))].reshape(rows, PAIR)

        def load_all(first=0):
            return lambda lanes: ref[(*at, slice(None), slice(None), slice(None), lanes_at(first, lanes))].reshape(seq, PAIR)

        def store_rows(first=0):
            def store(yb, lanes, value):
                ref[(*at, yb, slice(None), slice(None), lanes_at(first, lanes))] = value.reshape(2, tb, PAIR)

            return store

        def store_all(first=0):
            def store(lanes, value):
                ref[(*at, slice(None), slice(None), slice(None), lanes_at(first, lanes))] = value.reshape(2, 2, tb, PAIR)

            return store

        return load_rows, load_all, store_rows, store_all

    def in_rows(e):
        return xr[e].reshape(rows, width).astype(f32)

    def cot_rows(e):
        return cot[e].reshape(rows, width)

    def half_rows(ref, e, ch, count):
        return ref[e, :, ch].reshape(rows, count)

    def self_forward(e, slot, length):
        x_copy(e).wait()
        gather_start(G_IN, fin, e, norm(in_rows(e), 0))

        def project(a, ch):
            qkv[e, :, ch] = nt(a, wqkv[...]).astype(bf16).reshape(2, tb, 3 * kc)

        gather_use(G_IN, fin, e, project)
        lr, la, _, _ = block_of(qkv, e)
        _, _, store_ctx, _ = block_of(ctx, e)

        def store_lse(yb, value):
            lse[e, yb] = value

        attend(lr(), la(kc), la(2 * kc), length, True, store_ctx(), store_lse)

        @pl.when(e == 0)
        def _():
            w_on(W_O)
            w_done(W_O)

        h1[e] = in_rows(e) + scatter(
            S_ATT, e, slot, lambda ch: nn(half_rows(ctx, e, ch, kc), wo[...])
        )

    def ffn_forward(e, slot, src, act, dg):
        gather_start(G_FFN, ffnf, e, norm(src[e], 2))

        def expand(a, ch):
            for i in range(2):
                pre = nn(a, wf1[i])
                sq = pre * pre
                th = jnp.tanh(0.7978845608028654 * pre * (1.0 + 0.044715 * sq))
                gate = 0.5 + 0.5 * th
                slope = gate + (0.5 * 0.7978845608028654) * pre * (1.0 - th * th) * (
                    1.0 + (3 * 0.044715) * sq
                )
                lanes = pl.ds(i * fq, fq)
                act[e, :, ch, :, lanes] = (pre * gate).astype(bf16).reshape(2, tb, fq)
                dg[e, :, ch, :, lanes] = slope.astype(bf16).reshape(2, tb, fq)

        gather_use(G_FFN, ffnf, e, expand)
        return src[e] + scatter(
            S_FFN, e, slot, lambda ch: nn(half_rows(act, e, ch, fc), wf2[...].reshape(fc, width))
        )

    def ffn_back(e, slot, grad_b, grad_f, src, act, dg):
        gather_start(G_DFFN, fffn, e, grad_b)

        def contract(a, ch):
            for i in range(2):
                lanes = pl.ds(i * fq, fq)
                dact = nt(a, wf2[i])
                slope = dg[e, :, ch, :, lanes].reshape(rows, fq).astype(f32)
                dg[e, :, ch, :, lanes] = (dact * slope).astype(bf16).reshape(2, tb, fq)

        gather_use(G_DFFN, fffn, e, contract)


        def partial_sum(ch):
            both = half_rows(dg, e, ch, fc)
            return nt(both[:, :fq], wf1[0]) + nt(both[:, fq:], wf1[1])

        dn = scatter(S_DFFN, e, slot, partial_sum)
        return grad_f() + norm_back(src[e], 2, dn)

    def context_grad(kind, buf, e, w):
        def project(a, ch):
            dctx[0, :, ch] = nt(a, w[...]).astype(bf16).reshape(2, tb, kc)

        gather_use(kind, buf, e, project)

    def self_back(e, slot, length, dsacc):
        gather_start(G_DATT, fatt, e, r2[e].astype(bf16))
        context_grad(G_DATT, fatt, e, wo)
        lr, la, sr_, sa_ = block_of(qkv, e)
        ldo = block_of(dctx, 0)[0]
        lo = block_of(ctx, e)[0]
        attend_back(
            lr(), la(kc), la(2 * kc), ldo(), lo(), lambda yb: lse[e, yb], length, dsacc,
            sr_(), sa_(kc), sa_(2 * kc),
        )
        dn = scatter(S_DIN, e, slot, lambda ch: nn(half_rows(qkv, e, ch, 3 * kc), wqkv[...]))
        ing[e] = (r2[e] + norm_back(in_rows(e), 0, dn)).astype(bf16).reshape(2, tb, width)
        hand_out(1, ing, ing_out, e)

    def out_copies(kind, buf, out, e):
        at = side * ex + e
        return (
            pltpu.make_async_copy(buf.at[e, side], out.at[at], lsem.at[8 + kind * ex + e]),
            remote(buf.at[e, 1 - side], out.at[at], os.at[kind, e], og.at[kind, e], peer),
        )

    def hand_out(kind, buf, out, e):
        for cp in out_copies(kind, buf, out, e):
            cp.start()

    def pass_copy(e):
        return remote(kvs.at[e], kvr.at[e], ps.at[e], pr.at[e], other)

    def y_copy(u):
        return remote(ysend.at[u], yrecv.at[u], us.at[u], ug.at[u], peer)

    def all_rows(ref, lanes):
        n = lanes.size
        return ref[:, :, :, :, lanes].reshape(ex * seq, n)

    half = width // 2

    def lanes_of(r):
        return pl.ds(pl.multiple_of(r * half, PAIR), half)

    def ffn_grads(u, src, feed_ref, gst):
        def to(dst, first):
            def body(r, _):
                rhs = all_rows(feed_ref, pl.ds(first, fq))
                gst[...] = tn(all_rows(src, lanes_of(r)), rhs).astype(bf16)
                cps = [
                    pltpu.make_async_copy(
                        gst.at[:, pl.ds(i * kc, kc)], dst.at[u + i, lanes_of(r)], lsem.at[i]
                    )
                    for i in range(2)
                ]
                for cp in cps:
                    cp.start()
                for cp in cps:
                    cp.wait()
                return 0

            lax.fori_loop(0, 2, body, 0)

        to(ysend, fq)
        for i in range(2):
            y_copy(u + i).start()
        to(gown, 0)

    def pair_grads(u, lhs_a, load_a, lhs_b, load_b, scale, gst):
        def body(r, _):
            a = tn(all_rows(lhs_a, lanes_of(r)), load_a())
            if scale is not None:
                a = a * scale
            b = tn(all_rows(lhs_b, lanes_of(r)), load_b())
            low = lane < DK
            a1, b1 = a[:, PAIR : 2 * PAIR], b[:, PAIR : 2 * PAIR]
            mix_own = jnp.where(low, a1, pltpu.roll(b1, DK, 1))
            mix_peer = jnp.where(low, pltpu.roll(a1, DK, 1), b1)
            for j, part in enumerate(
                (a[:, :PAIR], mix_own, b[:, :PAIR], a[:, 2 * PAIR :], mix_peer, b[:, 2 * PAIR :])
            ):
                gst[:, j * PAIR : (j + 1) * PAIR] = part.astype(bf16)
            cps = [
                pltpu.make_async_copy(
                    gst.at[:, pl.ds(i * kc, kc)], dst.at[u, lanes_of(r)], lsem.at[i]
                )
                for i, dst in enumerate((gown, ysend))
            ]
            for cp in cps:
                cp.start()
            for cp in cps:
                cp.wait()
            return 0

        lax.fori_loop(0, 2, body, 0)
        y_copy(u).start()

    def mid_grads(load_a, lhs_b, load_b, scale):
        pl.run_scoped(
            partial(pair_grads, 4, mid, load_a, lhs_b, load_b, scale),
            pltpu.VMEM((half, 2 * kc), bf16),
        )

    def z_copy(u, step):
        block = width // count
        at = away(step)
        return remote(
            zs.at[u, pl.ds(pl.multiple_of(at * block, 16), block)], zr.at[u, step - 1],
            vs.at[u, step - 1], vg.at[u, step - 1], {"dp": at},
        )

    def pump(u, va, vb):
        y_copy(u).wait_recv()
        cps = [
            pltpu.make_async_copy(gown.at[u], va, lsem.at[0]),
            pltpu.make_async_copy(yrecv.at[u], vb, lsem.at[1]),
        ]
        for cp in cps:
            cp.start()
        for cp in cps:
            cp.wait()
        va[...] = (va[...].astype(f32) + vb[...].astype(f32)).astype(bf16)
        cp = pltpu.make_async_copy(va, zs.at[u], lsem.at[0])
        cp.start()
        cp.wait()
        if direct:
            for step in range(1, count):
                z_copy(u, step).start()

    def finish(u, va, vf):
        block = width // count
        for step in range(1, count):
            z_copy(u, step).wait()
        mine = pl.ds(pl.multiple_of(data * block, 16), block)
        cps = [pltpu.make_async_copy(zs.at[u, mine], va.at[pl.ds(0, block)], lsem.at[0])]
        for step in range(1, count):
            cps.append(
                pltpu.make_async_copy(
                    zr.at[u, step - 1], va.at[pl.ds(step * block, block)], lsem.at[step]
                )
            )
        for cp in cps:
            cp.start()
        for cp in cps:
            cp.wait()
        total = va[0:block].astype(f32)
        for step in range(1, count):
            total = total + va[step * block : (step + 1) * block].astype(f32)
        vf[...] = total
        cp = pltpu.make_async_copy(vf, fin_out.at[u], lsem.at[0])
        cp.start()
        cp.wait()

    def small_sums():
        first = remote(small.at[pl.ds(0, 8)], small_c, ms.at[0], mg.at[0], partner)
        first.start()
        first.wait()
        small[0:8] += small_c[...]
        second = remote(small, small_y, ms.at[1], mg.at[1], peer)
        second.start()
        second.wait()
        small[0:8] += small_y[0:8]
        for h in range(own_heads):
            at = 8 + own_heads + (h + 1) % 3
            small[8 + h : 9 + h] += small_y[at : at + 1]
        if direct:
            sends = [
                remote(small, small_z.at[i - 1], ms.at[1 + i], mg.at[1 + i], {"dp": away(i)})
                for i in range(1, count)
            ]
            for cp in sends:
                cp.start()
            for cp in sends:
                cp.wait()
            total = small[...]
            for i in range(1, count):
                total = total + small_z[i - 1]
            small_out[...] = total
        else:
            small_out[...] = small[...]

    def bias_grads(dsacc):
        at_r = lax.broadcasted_iota(jnp.int32, (seq, seq), 0)
        at_c = lax.broadcasted_iota(jnp.int32, (seq, seq), 1)
        flip = jnp.where(at_r + at_c == seq - 1, 1.0, 0.0).astype(bf16)

        def body(h, _):
            reverse = nn(dsacc[h].astype(bf16), flip)
            wide = jnp.concatenate([reverse, jnp.zeros((seq, seq), f32)], axis=1)
            wide = pltpu.roll(wide, 0, 1, stride=1, stride_axis=0)
            small[pl.ds(8 + h, 1), :] = jnp.sum(wide, axis=0, keepdims=True)
            return 0

        lax.fori_loop(0, heads, body, 0)

    def loop(fn):
        def body(e, _):
            fn(e)
            return 0

        lax.fori_loop(0, ex, body, 0)

    def self_back_all(own_length):
        def run(dsacc, gst, va, vb, vf):
            dsacc[...] = jnp.zeros_like(dsacc)

            def one(e):
                self_back(e, lax.rem(e, 2), own_length(e), dsacc)
                pump(e, va, vb)

            loop(one)
            bias_grads(dsacc)
            lanes = [pl.ds(i * kc, kc) for i in range(3)]
            pair_grads(
                5, fin, lambda: all_rows(qkv, lanes[0]), fin, lambda: all_rows(qkv, lanes[1]),
                0.125, gst,
            )
            pair_grads(
                6, fin, lambda: all_rows(qkv, lanes[2]), fatt, lambda: all_rows(ctx, lanes[0]),
                None, gst,
            )
            small_sums()

            def rest(u, _):
                pump(u, va, vb)
                if direct:
                    finish(u - 3, va, vf)
                return 0

            lax.fori_loop(3, 7, rest, 0)
            if direct:

                def last(u, _):
                    finish(u, va, vf)
                    return 0

                lax.fori_loop(4, 7, last, 0)

            def sent(u, _):
                y_copy(u).wait_send()
                return 0

            lax.fori_loop(0, 7, sent, 0)

        V = pltpu.VMEM
        block = width // count
        pl.run_scoped(
            run, V((heads, seq, seq), f32), V((half, 2 * kc), bf16), V((width, kc), bf16),
            V((width, kc), bf16), V((block, kc), f32),
        )
        for kind, (buf, out) in enumerate(((sec, sec_out), (ing, ing_out))):
            for e in range(ex):
                for cp in out_copies(kind, buf, out, e):
                    cp.wait()

    def begun():
        for i in range(8):
            w_copy(i).wait_send()
        for e in range(ex):
            cot_copy(e).wait_send()

    feed = pltpu.VMEM((ex, 2, 2, tb, fc), bf16)
    grad_stage = pltpu.VMEM((half, 2 * kc), bf16)

    @pl.when(pipe == 0)
    def _():
        def own_length(e):
            return len_ref[side * ex + e, 0]

        def run(act, dg):
            def first(e):
                self_forward(e, lax.rem(e, 2), own_length(e))

                @pl.when(e == 1)
                def _():
                    w_on(W_F1)

            def ahead(e):
                r2[e] = ffn_forward(e, 0, h1, act, dg)

                @pl.when(e == 0)
                def _():
                    for i in (W_C1, W_C2):
                        w_done(i)

                memory = norm(r2[e], 1)
                sec[e] = memory.reshape(2, tb, width)
                hand_out(0, sec, sec_out, e)
                gather_start(G_MID, mid, e, memory)

                def project(a, ch):
                    for i, w in enumerate((w1, w2)):
                        kvs[e, i, :, ch] = nt(a, w[...]).astype(bf16).reshape(2, tb, kc)

                gather_use(G_MID, mid, e, project)
                pass_copy(e).start()

            def back(e):
                pass_copy(e).wait()
                cot_copy(e).wait_recv()

                def partial_sum(ch):
                    return nn(kvr[e, 0, :, ch].reshape(rows, kc), w1[...]) + nn(
                        kvr[e, 1, :, ch].reshape(rows, kc), w2[...]
                    )

                dmem = cot_rows(e).astype(f32) + scatter(S_DMEM, e, 0, partial_sum)
                r2[e] = norm_back(r2[e], 1, dmem)
                r2[e] = ffn_back(e, 1, r2[e].astype(bf16), lambda: r2[e], h1, act, dg)

            loop(first)
            w_on(W_F2)
            w_done(W_F1)
            w_on(W_C1)
            w_on(W_C2)
            w_done(W_F2)
            loop(ahead)
            begun()
            loop(back)

            def grads(gst):
                ffn_grads(0, ffnf, dg, gst)
                ffn_grads(2, fffn, act, gst)

            pl.run_scoped(grads, grad_stage)

        pl.run_scoped(run, feed, feed)

        def keys(i):
            return lambda: kvr[:, i].reshape(ex * seq, kc)

        mid_grads(keys(0), mid, keys(1), None)
        self_back_all(own_length)

    @pl.when(pipe == 1)
    def _():
        def own_length(e):
            return len_ref[side * ex + e, 1]

        def first(e):
            self_forward(e, lax.rem(e, 2), own_length(e))

            @pl.when(e == 1)
            def _():
                w_on(W_C1)
                w_on(W_C2)

        loop(first)
        w_on(W_F1)
        w_done(W_C1)
        w_done(W_C2)
        w_on(W_F2)
        w_done(W_F1)
        w_done(W_F2)
        begun()

        def run(act, dg):
            def there_and_back(e):
                gather_start(G_MID, mid, e, norm(h1[e], 1))

                def project(a, ch):
                    cq[e, :, ch] = nt(a, w1[...]).astype(bf16).reshape(2, tb, kc)

                gather_use(G_MID, mid, e, project)
                pass_copy(e).wait_recv()
                lq, _, sq, _ = block_of(cq, e)
                _, lk, _, _ = block_of(kvr, e, 0)
                _, lv, _, _ = block_of(kvr, e, 1)
                lc, _, sc, _ = block_of(cctx, e)

                def store_lse(yb, value):
                    clse[yb] = value

                source_length = len_ref[side * ex + e, 0]
                attend(lq(), lk(), lv(), source_length, False, sc(), store_lse)
                r2[e] = h1[e] + scatter(
                    S_MID, e, 0, lambda ch: nn(half_rows(cctx, e, ch, kc), w2[...])
                )
                sec[e] = ffn_forward(e, 1, r2, act, dg).astype(bf16).reshape(2, tb, width)
                hand_out(0, sec, sec_out, e)
                cot_copy(e).wait_recv()
                r2[e] = ffn_back(
                    e, 0, cot_rows(e), lambda: cot_rows(e).astype(f32), r2, act, dg
                )
                gather_start(G_DMID, fmid, e, r2[e].astype(bf16))
                context_grad(G_DMID, fmid, e, w2)
                ldo = block_of(dctx, 0)[0]
                sk, sv = block_of(kvs, e, 0)[3], block_of(kvs, e, 1)[3]
                attend_back(
                    lq(), lk(), lv(), ldo(), lc(), lambda yb: clse[yb], source_length, None,
                    sq(), sk(), sv(),
                )
                pass_copy(e).start()
                dn = scatter(S_DMID, e, 1, lambda ch: nn(half_rows(cq, e, ch, kc), w1[...]))
                r2[e] += norm_back(h1[e], 1, dn)

            loop(there_and_back)

            def grads(gst):
                ffn_grads(0, ffnf, dg, gst)
                ffn_grads(2, fffn, act, gst)

            pl.run_scoped(grads, grad_stage)

        pl.run_scoped(run, feed, feed)
        lanes = pl.ds(0, kc)
        mid_grads(lambda: all_rows(cq, lanes), fmid, lambda: all_rows(cctx, lanes), 0.125)
        loop(lambda e: pass_copy(e).wait_send())
        self_back_all(own_length)


def run_sections(x, cot, w_in, w_out, c_1, c_2, f_1, f_2, gains, lens, table, hot, direct):
    batch, tb, width = x.shape
    ex = batch // 2
    rows, seq = 2 * tb, 4 * tb
    kq, fq = w_out.shape[0], f_1.shape[1]
    kc, fc = 2 * kq, 2 * fq
    heads = kc // DK
    count = lax.axis_size("dp")
    vmem = pl.BlockSpec(memory_space=pltpu.VMEM)
    hbm = pl.BlockSpec(memory_space=pl.ANY)
    smem = pl.BlockSpec(memory_space=pltpu.SMEM)
    full = (ex, 2, 2, tb)
    units = (7, width, kc)
    V = pltpu.VMEM
    D = pltpu.SemaphoreType.DMA
    S = jax.ShapeDtypeStruct
    scratch = [
        V((3 * kc, width), bf16), V((kc, width), bf16), V((kc, width), bf16), V((kc, width), bf16),
        V((2, width, fq), bf16), V((2, fq, width), bf16), V((heads, seq, seq), bf16),
        V((ex, 2, tb, width), bf16), V((ex, 2, tb, width), bf16),
        V((ex, 2, tb, width), bf16), V((ex, 2, tb, width), bf16),
        V((*full, width), bf16),
        V((*full, 3 * kc), bf16),
        V((*full, kc), bf16),
        V((ex, 2, rows, PAIR), f32),
        V((ex, rows, width), f32),
        V((*full, width), bf16),
        V((*full, width), bf16),
        V((ex, 2, 2, 2, tb, kc), bf16),
        V((ex, 2, 2, 2, tb, kc), bf16),
        V((*full, kc), bf16),
        V((*full, kc), bf16),
        V((2, rows, PAIR), f32),
        V((*full, width), bf16),
        V((ex, rows, width), f32),
        V((*full, width), bf16),
        V((*full, width), bf16),
        V((1, 2, 2, tb, kc), bf16),
        V((rows, width), f32),
        V((2, rows, width), bf16),
        V((2, rows, width), bf16),
        V((2, 8, 2 * seq), f32),
        V((16, 2 * seq), f32), V((8, 2 * seq), f32), V((16, 2 * seq), f32),
        V((max(1, count - 1) if direct else 1, 16, 2 * seq), f32),
        D((8 + 2 * ex,)),
        D((2, ex)), D((2, ex)), D((1,)), D((1,)), D((8,)), D((8,)), D((8,)), D((8,)),
        D((6, ex)), D((6, ex)), D((7, ex)), D((7, ex)), D((ex,)), D((ex,)),
        D((2, ex)), D((2, ex)), D((7,)), D((7,)), D((7, 3)), D((7, 3)), D((5,)), D((5,)),
    ]
    slots = count - 1 if direct else 1
    return pl.pallas_call(
        partial(section_kernel, direct=direct),
        out_shape=(
            S((batch, tb, width), bf16),
            S((batch, tb, width), bf16),
            S(units, bf16),
            S((7, slots, width // count if direct else 16, kc), bf16),
            S((7, width // count if direct else 8, kc), f32),
            S((16, 2 * seq), f32),
            S(units, bf16),
            S(units, bf16),
            S(units, bf16),
        ),
        in_specs=[hbm] * 8 + [vmem, smem, vmem, vmem],
        out_specs=(hbm, hbm, hbm, hbm, hbm, vmem, hbm, hbm, hbm),
        scratch_shapes=scratch,
        compiler_params=pltpu.CompilerParams(
            collective_id=0, has_side_effects=True, vmem_limit_bytes=64 * 2**20 - 65536
        ),
        name="sections",
    )(x, cot, w_in, w_out, c_1, c_2, f_1, f_2, gains, lens, table, hot)


def local(
    section_input, lengths, norm_gain, attn_in, attn_out, cross_first, cross_second,
    ffn_in, ffn_out, rel_bias, out_grad,
):
    pipe = lax.axis_index("pipe")
    enc = pipe == 0
    tb, width = section_input.shape[2:]
    seq = tb * lax.axis_size("tensor")
    kq, fq = attn_out.shape[1], ffn_out.shape[1]
    data = lax.axis_size("dp")
    at_data = lax.axis_index("dp")
    direct = data <= 4 and (width // data) % 16 == 0

    offsets = list(range(seq)) + [0] + list(range(-seq + 1, 0))
    both = [np.array(bucket_list(offsets, ways)) for ways in (True, False)]
    hot = np.stack([np.arange(NB)[:, None] == spots[None] for spots in both])

    sec, ing, zs, _, fin, small, _, _, _ = run_sections(
        section_input[0], out_grad[0], attn_in[0], attn_out[0], cross_first[0], cross_second[0],
        ffn_in[0], ffn_out[0], norm_gain[0], lengths, rel_bias[0], jnp.asarray(hot, bf16), direct,
    )

    turned = [seq - 1 - m for m in range(2 * seq)]
    hot_m = np.stack(
        [np.array(bucket_list(turned, ways))[:, None] == np.arange(NB) for ways in (True, False)]
    )
    hot_m = jnp.where(enc, jnp.asarray(hot_m[0], f32), jnp.asarray(hot_m[1], f32))
    bsum = jnp.einsum(
        "mb,hm->bh", hot_m, small[8 : 8 + kq // DK], precision=lax.Precision.HIGHEST
    )
    gains = small[:3, :width]
    if direct:
        shard = fin
        share = NB // data
        bias_grad = lax.dynamic_slice_in_dim(bsum, at_data * share, share, 0)
    else:
        packed = zs.reshape(7, data, width // data, 2 * kq)
        shard = lax.psum_scatter(packed, "dp", scatter_dimension=1, tiled=False).astype(f32)
        bias_grad = lax.psum_scatter(bsum, "dp", scatter_dimension=0, tiled=True)
        gains = lax.psum(gains, "dp")
    share = width // (data * lax.axis_size("tensor"))
    at = (at_data * lax.axis_size("tensor") + lax.axis_index("tensor")) * share
    gain_grad = lax.dynamic_slice_in_dim(gains, at, share, 1)

    def first_of(u):
        return jnp.concatenate([shard[u, :, :128], shard[u, :, 128:192]], 1)

    def second_of(u):
        return jnp.concatenate([shard[u, :, 256:], shard[u, :, 192:256]], 1)

    f_in = jnp.concatenate([shard[0], shard[1]], 1)
    f_out = jnp.concatenate([shard[2], shard[3]], 1).T
    w_in = jnp.stack([first_of(5), second_of(5), first_of(6)])
    return (
        sec[None],
        ing[None].astype(f32),
        w_in[None],
        second_of(6).T[None],
        first_of(4)[None],
        second_of(4)[None],
        f_in[None],
        f_out[None],
        bias_grad[None],
        gain_grad[None],
    )


def solution(mesh):
    placed = (
        P("pipe", "dp", "tensor", None),
        P("dp", None),
        P("pipe", None, None),
        P("pipe", None, None, "tensor"),
        P("pipe", "tensor", None),
        P("pipe", None, "tensor"),
        P("pipe", None, "tensor"),
        P("pipe", None, "tensor"),
        P("pipe", "tensor", None),
        P("pipe", None, "tensor"),
        P("pipe", "dp", "tensor", None),
    )
    return jax.shard_map(
        local,
        mesh=mesh,
        in_specs=placed,
        out_specs=(
            P("pipe", "dp", "tensor", None),
            P("pipe", "dp", "tensor", None),
            P("pipe", None, "dp", "tensor"),
            P("pipe", "tensor", "dp"),
            P("pipe", "dp", "tensor"),
            P("pipe", "dp", "tensor"),
            P("pipe", "dp", "tensor"),
            P("pipe", "tensor", "dp"),
            P("pipe", "dp", "tensor"),
            P("pipe", None, ("dp", "tensor")),
        ),
        check_vma=False,
    )
```

```python
import math
from functools import partial

import jax
import jax.numpy as jnp
import numpy as np
from jax import lax
from jax.experimental import pallas as pl
from jax.experimental.pallas import tpu as pltpu
from jax.sharding import PartitionSpec as P

NB = 32
MAX_DIST = 128
DK = 64
EPS = 1e-06
MASKED = -1000000000.0
MESH = pl.DeviceIdType.MESH
bf16, f32 = jnp.bfloat16, jnp.float32
PAIR = 128
G_IN, G_MID, G_FFN, G_DFFN, G_DMID, G_DATT = range(6)
S_ATT, S_MID, S_FFN, S_DMEM, S_DFFN, S_DMID, S_DIN = range(7)


def bucket_list(offsets, both_ways):
    half = NB // 2 if both_ways else NB
    exact = half // 2
    out = []
    for r in offsets:
        base = half if both_ways and r > 0 else 0
        n = abs(r) if both_ways else max(-r, 0)
        if n < exact:
            out.append(base + n)
        else:
            at = exact + math.floor(
                math.log(n / exact) / math.log(MAX_DIST / exact) * (half - exact)
            )
            out.append(base + min(half - 1, at))
    return out


def nt(a, b):
    return lax.dot_general(a, b, (((1,), (1,)), ((), ())), preferred_element_type=f32)


def nn(a, b):
    return lax.dot_general(a, b, (((1,), (0,)), ((), ())), preferred_element_type=f32)


def tn(a, b):
    return lax.dot_general(a, b, (((0,), (0,)), ((), ())), preferred_element_type=f32)


W_Q, W_K, W_V, W_O, W_C1, W_C2, W_F1, W_G1, W_F2, W_G2 = range(10)


def section_kernel(
    xin, cin, w_in, w_out, c_1, c_2, f_1, f_2, gain_ref, len_ref, table_ref, hot_ref,
    sec_out, ing_out, zs, zr, fin_out, small_out, gown, ysend, yrecv,
    wqkv, wo, w1, w2, wf1, wf2, bias,
    xr, cot, out_rows,
    fin, qkv, ctx, lse, h1, fatt, mid, kvs, kvr, fmid,
    r2, ffnf, fffn, dctx, rsa, rss, rsr, diag, small, small_c, small_y, small_z,
    lsem, xs, xg, ts, tg, ys, yg, zps, zpg, gs, gr, ss, sr, ps, pr, os, og, us, ug, vs, vg, ms, mg,
    *, direct,
):
    ex, _, tb, width = xr.shape
    rows = 2 * tb
    kq = wo.shape[0] // 2
    kc = wo.shape[0]
    fq = wf1.shape[2]
    fc = 2 * fq
    seq = 2 * rows
    heads = kc // DK
    pairs = kc // PAIR
    own_heads = heads // 2

    tensor = lax.axis_index("tensor")
    pipe = lax.axis_index("pipe")
    data = lax.axis_index("dp")
    count = lax.axis_size("dp")
    core = lax.rem(tensor, 2)
    side = tensor // 2
    parity = lax.rem(data, 2)
    partner = {"tensor": tensor + 1 - 2 * core}
    peer = {"tensor": lax.rem(tensor + 2, 4)}
    near = {"dp": data + 1 - 2 * parity}
    other = {"pipe": 1 - pipe}

    def away(step):
        return lax.rem(data + step, count)

    barrier = pltpu.get_barrier_semaphore()
    met = [partner, peer, other]
    met += [{"dp": away(i)} for i in range(1, count)] if direct else [near]
    for device in met:
        pl.semaphore_signal(barrier, 1, device_id=device, device_id_type=MESH)

    def remote(src, dst, send, recv, device):
        return pltpu.make_async_remote_copy(
            src, dst, send, recv, device_id=device, device_id_type=MESH
        )

    def own_copies(raw):
        pairs_of = [(w_in.at[i], raw.at[i]) for i in range(3)]
        pairs_of += [(w_out, wo.at[pl.ds(0, kq)]), (c_1, raw.at[3]), (c_2, raw.at[4])]
        pairs_of += [(f_1, wf1.at[0]), (f_2, wf2.at[0])]
        for e in range(ex):
            pairs_of.append((xin.at[side * ex + e], xr.at[e, side]))
        for e in range(ex):
            pairs_of.append((cin.at[side * ex + e], cot.at[e, side]))
        return [pltpu.make_async_copy(p, q, lsem.at[i]) for i, (p, q) in enumerate(pairs_of)]

    def x_copy(e):
        return remote(xin.at[(1 - side) * ex + e], xr.at[e, side], xs.at[0, e], xg.at[0, e], peer)

    def cot_copy(e):
        return remote(cin.at[(1 - side) * ex + e], cot.at[e, side], xs.at[1, e], xg.at[1, e], peer)

    def diag_copy():
        return remote(diag.at[0], diag.at[1], ts.at[0], tg.at[0], peer)

    half_kq, part_fq = kq // 2, wf1.shape[1] // 4

    def small_home(i, part):
        first = kq + part * half_kq
        if i < 3:
            return wqkv.at[pl.ds(pl.multiple_of(i * kc + first, 16), half_kq)]
        return (wo, w1, w2)[i - 3].at[pl.ds(pl.multiple_of(first, 16), half_kq)]

    def big_home(i, part, at=1):
        ref, piece = (wf1, wf2)[(i - W_F1) // 2], (i - W_F1) % 2
        return ref.at[at, pl.ds(pl.multiple_of((2 * piece + part) * part_fq, 16), part_fq)]

    def home(i, part):
        return big_home(i, part) if i >= W_F1 else small_home(i, part)

    def w_copy(i):
        if i >= W_F1:
            src = big_home(i, parity, 0)
        else:
            src = fatt.at[i // 2, i % 2, parity, pl.ds(0, half_kq)]
        return remote(src, home(i, parity), ys.at[i], yg.at[i], peer)

    def w_pass(i):
        return remote(home(i, parity), home(i, parity), zps.at[i], zpg.at[i], near)

    def w_on(i):
        w_copy(i).wait_recv()
        w_pass(i).start()

    def w_done(i):
        w_pass(i).wait()

    def turned(i, value):
        if i < 3:
            wqkv[i * kc : i * kc + kq] = value
        elif i > 3:
            (w1, w2)[i - 4][0:kq] = value
        last = kq - DK
        fatt[i // 2, i % 2, 0, 0:DK] = value[last:]
        fatt[i // 2, i % 2, 0, DK:half_kq] = value[: half_kq - DK]
        fatt[i // 2, i % 2, 1, 0:half_kq] = value[half_kq - DK : last]

    def make_diag():
        values = tn(table_ref[...], hot_ref[pipe])
        at = lax.broadcasted_iota(jnp.int32, (1, 2 * seq), 1)
        hidden = jnp.logical_and(jnp.logical_and(at > 0, at < seq), pipe == 1)
        values = jnp.where(hidden, MASKED, values)
        diag[0, 0:own_heads] = values
        diag[0, own_heads:] = jnp.zeros((8 - own_heads, 2 * seq), f32)

    def begin(raw):
        copies = own_copies(raw)
        for cp in copies:
            cp.start()
        make_diag()
        pl.semaphore_wait(barrier, len(met))
        diag_copy().start()
        x_copy(0).start()
        scale_q = jnp.asarray(0.125, bf16)
        for i in range(3):
            copies[i].wait()
            value = raw[i].T
            turned(i, value * scale_q if i == 0 else value)
            w_copy(i).start()
        copies[3].wait()
        turned(W_O, wo[0:kq])
        w_copy(W_O).start()

        def start_x():
            for e in range(1, ex):
                x_copy(e).start()

        def start_f(order):
            for i in (6, 7):
                copies[i].wait()
            for i in order:
                w_copy(i).start()

        def start_c():
            for i in (W_C1, W_C2):
                w_copy(i).start()

        @pl.when(pipe == 0)
        def _():
            start_f((W_F1, W_G1, W_F2, W_G2))

        @pl.when(pipe == 1)
        def _():
            start_x()

        scale_c = jnp.where(pipe == 0, 1.0, 0.125).astype(bf16)
        for i in (W_C1, W_C2):
            copies[i].wait()
            value = raw[i - 1].T
            turned(i, value * scale_c if i == W_C1 else value)
        start_c()

        @pl.when(pipe == 0)
        def _():
            start_x()

        @pl.when(pipe == 1)
        def _():
            start_f((W_F2, W_G2, W_F1, W_G1))

        for e in range(ex):
            cot_copy(e).start()
        for cp in copies[8:]:
            cp.wait()

    pl.run_scoped(begin, pltpu.VMEM((5, width, kq), bf16))
    small[...] = jnp.zeros_like(small)
    diag_copy().wait()
    local_order = [(0, h) for h in range(own_heads)] + [(1, (h + 2) % 3) for h in range(own_heads)]
    for h, (from_side, at) in enumerate(local_order):
        wide = jnp.broadcast_to(diag[from_side, at : at + 1, :], (seq, 2 * seq))
        bias[h] = pltpu.roll(wide, 0, 1, stride=1, stride_axis=0)[:, :seq].astype(bf16)
    for i in range(3):
        w_on(i)
    for i in range(3):
        w_done(i)

    lane = lax.broadcasted_iota(jnp.int32, (1, PAIR), 1)
    half_f = [jnp.where(lane // DK == hh, 1.0, 0.0) for hh in range(2)]
    half_b = [m.astype(bf16) for m in half_f]
    key_at = lax.broadcasted_iota(jnp.int32, (1, seq), 1)

    def key_mask(length):
        return jnp.where(key_at < length, 0.0, MASKED)

    def gather_copy(kind, buf, e):
        return remote(
            buf.at[e, :, core], buf.at[e, :, core], gs.at[kind, e], gr.at[kind, e], partner
        )

    def gather_start(kind, buf, e, value):
        buf[e, :, core] = value.reshape(2, tb, width)
        gather_copy(kind, buf, e).start()

    def gather_use(kind, buf, e, fn):
        def body(i, _):
            ch = lax.rem(core + i, 2)

            @pl.when(i == 1)
            def _():
                gather_copy(kind, buf, e).wait()

            fn(buf[e, :, ch].reshape(rows, width), ch)
            return 0

        lax.fori_loop(0, 2, body, 0)

    def scatter_copy(kind, e, slot):
        return remote(rss.at[slot], rsr.at[slot], ss.at[kind, e], sr.at[kind, e], partner)

    def scatter_send(kind, e, slot, value):
        rss[slot] = value.astype(bf16)
        scatter_copy(kind, e, slot).start()

    def scatter_start(kind, e, slot, fn):
        def body(i, _):
            ch = lax.rem(core + 1 + i, 2)
            rsa[...] = fn(ch)

            @pl.when(i == 0)
            def _():
                scatter_send(kind, e, slot, rsa[...])

            return 0

        lax.fori_loop(0, 2, body, 0)

    def scatter_end(kind, e, slot):
        scatter_copy(kind, e, slot).wait()
        return rsr[slot].astype(f32)

    def scatter(kind, e, slot, fn):
        scatter_start(kind, e, slot, fn)
        return scatter_end(kind, e, slot) + rsa[...]

    def norm(v, row):
        inv = lax.rsqrt(jnp.mean(v * v, axis=-1, keepdims=True) + EPS)
        return (v * inv * gain_ref[pl.ds(row, 1), :]).astype(bf16)

    def norm_back(v, row, grad):
        inv = lax.rsqrt(jnp.mean(v * v, axis=-1, keepdims=True) + EPS)
        unit = v * inv
        small[pl.ds(row, 1), 0:width] += jnp.sum(grad * unit, axis=0, keepdims=True)
        gg = grad * gain_ref[pl.ds(row, 1), :]
        return inv * (gg - unit * jnp.mean(gg * unit, axis=-1, keepdims=True))

    def attend(ready, load_q, load_k, load_v, length, use_bias, store_ctx, lse_ref):
        mask = key_mask(length)

        def body(p, _):
            ready(p)
            k, v = load_k(p), load_v(p)
            for yb in range(2):
                q = load_q(yb, p)
                total = scale = None
                lse_t = lse_ref[yb]
                for hh in range(2):
                    h = 2 * p + hh
                    s = nt(q * half_b[hh], k) + mask
                    if use_bias:
                        s = s + bias[h, pl.ds(yb * rows, rows), :].astype(f32)
                    top = jnp.max(s, axis=-1, keepdims=True)
                    w = jnp.exp(s - top)
                    den = jnp.sum(w, axis=-1, keepdims=True)
                    part = nn(w.astype(bf16), v * half_b[hh])
                    total = part if total is None else total + part
                    inv = (1.0 / den) * half_f[hh]
                    scale = inv if scale is None else scale + inv
                    lse_t = jnp.where(lane == h, top + jnp.log(den), lse_t)
                store_ctx(yb, p, (total * scale).astype(bf16))
                lse_ref[yb] = lse_t
            return 0

        lax.fori_loop(0, pairs, body, 0)

    def attend_back(
        load_q, load_k, load_v, load_do, load_o, lse_ref, length, dsacc, store_dq, store_dk, store_dv
    ):
        mask = key_mask(length)

        def body(p, _):
            k, v = load_k(p), load_v(p)
            dk = dv = None
            for yb in range(2):
                q, do = load_q(yb, p), load_do(yb, p)
                both = do.astype(f32) * load_o(yb, p).astype(f32)
                lse_t = lse_ref[yb]
                dq = None
                for hh in range(2):
                    h = 2 * p + hh
                    qm, dom = q * half_b[hh], do * half_b[hh]
                    lse_c = jnp.sum(jnp.where(lane == h, lse_t, 0.0), axis=-1, keepdims=True)
                    delta = jnp.sum(both * half_f[hh], axis=-1, keepdims=True)
                    s = nt(qm, k) + mask
                    if dsacc is not None:
                        s = s + bias[h, pl.ds(yb * rows, rows), :].astype(f32)
                    w = jnp.exp(s - lse_c)
                    ds = w * (nt(dom, v) - delta)
                    wb, db = w.astype(bf16), ds.astype(bf16)
                    if dsacc is not None:
                        at = pl.ds(yb * rows, rows)
                        dsacc[h, at, :] = (dsacc[h, at, :].astype(f32) + ds).astype(bf16)
                    dvp, dkp, dqp = tn(wb, dom), tn(db, qm), nn(db, k * half_b[hh])
                    dv = dvp if dv is None else dv + dvp
                    dk = dkp if dk is None else dk + dkp
                    dq = dqp if dq is None else dq + dqp
                store_dq(yb, p, dq.astype(bf16))
            store_dk(p, dk.astype(bf16))
            store_dv(p, dv.astype(bf16))
            return 0

        lax.fori_loop(0, pairs, body, 0)

    def block_of(ref, *at):
        def lanes_at(first, p):
            return pl.ds(pl.multiple_of(first + p * PAIR, PAIR), PAIR)

        def load_rows(first=0):
            return lambda yb, p: ref[(*at, yb, slice(None), slice(None), lanes_at(first, p))].reshape(rows, PAIR)

        def load_all(first=0):
            return lambda p: ref[(*at, slice(None), slice(None), slice(None), lanes_at(first, p))].reshape(seq, PAIR)

        def store_rows(first=0):
            def store(yb, p, value):
                ref[(*at, yb, slice(None), slice(None), lanes_at(first, p))] = value.reshape(2, tb, PAIR)

            return store

        def store_all(first=0):
            def store(p, value):
                ref[(*at, slice(None), slice(None), slice(None), lanes_at(first, p))] = value.reshape(2, 2, tb, PAIR)

            return store

        return load_rows, load_all, store_rows, store_all

    def pair_of(ref, e, i):
        def load(p):
            return ref[e, p, i].reshape(seq, PAIR)

        def store(p, value):
            ref[e, p, i] = value.reshape(2, 2, tb, PAIR)

        return load, store

    def in_rows(e):
        return xr[e].reshape(rows, width).astype(f32)

    def cot_rows(e):
        return cot[e].reshape(rows, width)

    def half_rows(ref, e, ch, count):
        return ref[e, :, ch].reshape(rows, count)

    def self_forward(e, slot, length):
        x_copy(e).wait()
        gather_start(G_IN, fin, e, norm(in_rows(e), 0))

        def project(a, ch):
            qkv[e, :, ch] = nt(a, wqkv[...]).astype(bf16).reshape(2, tb, 3 * kc)

        gather_use(G_IN, fin, e, project)
        lr, la, _, _ = block_of(qkv, e)
        _, _, store_ctx, _ = block_of(ctx, e)

        def ready(p):
            pass

        attend(ready, lr(), la(kc), la(2 * kc), length, True, store_ctx(), lse.at[e])

        @pl.when(e == 0)
        def _():
            w_on(W_O)
            w_done(W_O)

        h1[e] = in_rows(e) + scatter(
            S_ATT, e, slot, lambda ch: nn(half_rows(ctx, e, ch, kc), wo[...])
        )

    def ffn_expand(e, src, act, dg, has_grad):
        gather_start(G_FFN, ffnf, e, norm(src[e], 2))

        def expand(a, ch):
            for i in range(2):
                pre = nn(a, wf1[i])
                sq = pre * pre
                th = jnp.tanh(0.7978845608028654 * pre * (1.0 + 0.044715 * sq))
                gate = 0.5 + 0.5 * th
                slope = gate + (0.5 * 0.7978845608028654) * pre * (1.0 - th * th) * (
                    1.0 + (3 * 0.044715) * sq
                )
                lanes = pl.ds(i * fq, fq)
                act[e, :, ch, :, lanes] = (pre * gate).astype(bf16).reshape(2, tb, fq)
                if has_grad:
                    slope = slope * dg[e, :, ch, :, lanes].reshape(rows, fq).astype(f32)
                dg[e, :, ch, :, lanes] = slope.astype(bf16).reshape(2, tb, fq)

        gather_use(G_FFN, ffnf, e, expand)

    def ffn_out_part(e, act):
        return lambda ch: nn(half_rows(act, e, ch, fc), wf2[...].reshape(fc, width))

    def ffn_in_part(e, dg):
        def part(ch):
            both = half_rows(dg, e, ch, fc)
            return nt(both[:, :fq], wf1[0]) + nt(both[:, fq:], wf1[1])

        return part

    def ffn_contract(e, dg, has_slope):
        def contract(a, ch):
            for i in range(2):
                lanes = pl.ds(i * fq, fq)
                dact = nt(a, wf2[i])
                if has_slope:
                    dact = dact * dg[e, :, ch, :, lanes].reshape(rows, fq).astype(f32)
                dg[e, :, ch, :, lanes] = dact.astype(bf16).reshape(2, tb, fq)

        gather_use(G_DFFN, fffn, e, contract)

    def context_grad(kind, buf, e, w):
        def project(a, ch):
            dctx[0, :, ch] = nt(a, w[...]).astype(bf16).reshape(2, tb, kc)

        gather_use(kind, buf, e, project)

    def self_back(e, slot, length, dsacc):
        gather_start(G_DATT, fatt, e, r2[e].astype(bf16))
        context_grad(G_DATT, fatt, e, wo)
        lr, la, sr_, sa_ = block_of(qkv, e)
        ldo = block_of(dctx, 0)[0]
        lo = block_of(ctx, e)[0]
        attend_back(
            lr(), la(kc), la(2 * kc), ldo(), lo(), lse.at[e], length, dsacc,
            sr_(), sa_(kc), sa_(2 * kc),
        )
        dn = scatter(S_DIN, e, slot, lambda ch: nn(half_rows(qkv, e, ch, 3 * kc), wqkv[...]))
        hand_out(1, e, (r2[e] + norm_back(in_rows(e), 0, dn)).astype(bf16))

    def out_copies(kind, e):
        at, out = side * ex + e, (sec_out, ing_out)[kind]
        return (
            pltpu.make_async_copy(out_rows.at[e, side], out.at[at], lsem.at[8 + kind * ex + e]),
            remote(out_rows.at[e, 1 - side], out.at[at], os.at[kind, e], og.at[kind, e], peer),
        )

    def hand_out(kind, e, value):
        if kind == 1:
            for cp in out_copies(0, e):
                cp.wait()
        out_rows[e] = value.reshape(2, tb, width)
        for cp in out_copies(kind, e):
            cp.start()

    def pass_copy(e, p):
        return remote(kvs.at[e, p], kvr.at[e, p], ps.at[e, p], pr.at[e, p], other)

    def y_copy(u):
        return remote(ysend.at[u], yrecv.at[u], us.at[u], ug.at[u], peer)

    def all_rows(ref, lanes):
        n = lanes.size
        return ref[:, :, :, :, lanes].reshape(ex * seq, n)

    half = width // 2

    def lanes_of(r):
        return pl.ds(pl.multiple_of(r * half, PAIR), half)

    def stage_copy(gst, r, i, dst, u):
        return pltpu.make_async_copy(
            gst.at[r, :, pl.ds(i * kc, kc)], dst.at[u, lanes_of(r)], lsem.at[2 * r + i]
        )

    def drain(gst, r):
        for i in range(2):
            stage_copy(gst, r, i, gown, 0).wait()

    def ffn_grads(u, src, feed_ref, gst, pending):
        def to(dst, first, wait, sent):
            def body(r, _):
                if wait:
                    drain(gst, r)
                if sent:

                    @pl.when(r == 1)
                    def _():
                        for i in range(2):
                            y_copy(u + i).start()

                rhs = all_rows(feed_ref, pl.ds(first, fq))
                gst[r] = tn(all_rows(src, lanes_of(r)), rhs).astype(bf16)
                for i in range(2):
                    stage_copy(gst, r, i, dst, u + i).start()
                return 0

            lax.fori_loop(0, 2, body, 0)

        to(ysend, fq, pending, False)
        to(gown, 0, True, True)

    def pair_grads(u, lhs_a, load_a, lhs_b, load_b, scale, gst, pending):
        def body(r, _):
            if pending:
                drain(gst, r)
            a = tn(all_rows(lhs_a, lanes_of(r)), load_a())
            if scale is not None:
                a = a * scale
            b = tn(all_rows(lhs_b, lanes_of(r)), load_b())
            low = lane < DK
            a1, b1 = a[:, PAIR : 2 * PAIR], b[:, PAIR : 2 * PAIR]
            mix_own = jnp.where(low, a1, pltpu.roll(b1, DK, 1))
            mix_peer = jnp.where(low, pltpu.roll(a1, DK, 1), b1)
            for j, part in enumerate(
                (a[:, :PAIR], mix_own, b[:, :PAIR], a[:, 2 * PAIR :], mix_peer, b[:, 2 * PAIR :])
            ):
                gst[r, :, j * PAIR : (j + 1) * PAIR] = part.astype(bf16)
            for i, dst in enumerate((gown, ysend)):
                stage_copy(gst, r, i, dst, u).start()
            return 0

        lax.fori_loop(0, 2, body, 0)
        for r in range(2):
            drain(gst, r)
        y_copy(u).start()

    def z_copy(u, step):
        block = width // count
        at = away(step)
        return remote(
            zs.at[u, pl.ds(pl.multiple_of(at * block, 16), block)], zr.at[u, step - 1],
            vs.at[u, step - 1], vg.at[u, step - 1], {"dp": at},
        )

    def pump(u, gst):
        y_copy(u).wait_recv()
        loads, stores = [], []
        for r in range(2):
            own, came = gst.at[r, :, pl.ds(0, kc)], gst.at[r, :, pl.ds(kc, kc)]
            loads.append(pltpu.make_async_copy(gown.at[u, lanes_of(r)], own, lsem.at[4 + r]))
            loads.append(pltpu.make_async_copy(yrecv.at[u, lanes_of(r)], came, lsem.at[6 + r]))
            stores.append(pltpu.make_async_copy(own, zs.at[u, lanes_of(r)], lsem.at[4 + r]))
        for cp in loads:
            cp.start()
        for r in range(2):
            for cp in loads[2 * r : 2 * r + 2]:
                cp.wait()
            gst[r, :, 0:kc] = (
                gst[r, :, 0:kc].astype(f32) + gst[r, :, kc : 2 * kc].astype(f32)
            ).astype(bf16)
            stores[r].start()
        for cp in stores:
            cp.wait()
        if direct:
            for step in range(1, count):
                z_copy(u, step).start()

    def finish(u, va, vf):
        block = width // count
        for step in range(1, count):
            z_copy(u, step).wait()
        mine = pl.ds(pl.multiple_of(data * block, 16), block)
        cps = [pltpu.make_async_copy(zs.at[u, mine], va.at[pl.ds(0, block)], lsem.at[0])]
        for step in range(1, count):
            cps.append(
                pltpu.make_async_copy(
                    zr.at[u, step - 1], va.at[pl.ds(step * block, block)], lsem.at[step]
                )
            )
        for cp in cps:
            cp.start()
        for cp in cps:
            cp.wait()
        total = va[0:block].astype(f32)
        for step in range(1, count):
            total = total + va[step * block : (step + 1) * block].astype(f32)
        vf[...] = total
        cp = pltpu.make_async_copy(vf, fin_out.at[u], lsem.at[0])
        cp.start()
        cp.wait()

    def small_near():
        first = remote(small.at[pl.ds(0, 8)], small_c, ms.at[0], mg.at[0], partner)
        first.start()
        first.wait()
        small[0:8] += small_c[...]
        small_peer().start()

    def small_peer():
        return remote(small, small_y, ms.at[1], mg.at[1], peer)

    def small_far():
        return [
            remote(small, small_z.at[i - 1], ms.at[1 + i], mg.at[1 + i], {"dp": away(i)})
            for i in range(1, count)
        ]

    def small_middle():
        small_peer().wait()
        small[0:8] += small_y[0:8]
        for h in range(own_heads):
            at = 8 + own_heads + (h + 1) % 3
            small[8 + h : 9 + h] += small_y[at : at + 1]
        if direct:
            for cp in small_far():
                cp.start()

    def small_end():
        total = small[...]
        if direct:
            for cp in small_far():
                cp.wait()
            for i in range(1, count):
                total = total + small_z[i - 1]
        small_out[...] = total

    def bias_grads(dsacc):
        at_r = lax.broadcasted_iota(jnp.int32, (seq, seq), 0)
        at_c = lax.broadcasted_iota(jnp.int32, (seq, seq), 1)
        flip = jnp.where(at_r + at_c == seq - 1, 1.0, 0.0).astype(bf16)

        def body(h, _):
            reverse = nn(dsacc[h], flip)
            wide = jnp.concatenate([reverse, jnp.zeros((seq, seq), f32)], axis=1)
            wide = pltpu.roll(wide, 0, 1, stride=1, stride_axis=0)
            small[pl.ds(8 + h, 1), :] = jnp.sum(wide, axis=0, keepdims=True)
            return 0

        lax.fori_loop(0, heads, body, 0)

    def loop(fn):
        def body(e, _):
            fn(e)
            return 0

        lax.fori_loop(0, ex, body, 0)

    def last_grads(dsacc, gst, between):
        lanes = [pl.ds(i * kc, kc) for i in range(3)]
        pair_grads(
            5, fin, lambda: all_rows(qkv, lanes[0]), fin, lambda: all_rows(qkv, lanes[1]),
            0.125, gst, False,
        )
        between()
        bias_grads(dsacc)
        small_near()
        pair_grads(
            6, fin, lambda: all_rows(qkv, lanes[2]), fatt, lambda: all_rows(ctx, lanes[0]),
            None, gst, False,
        )

    def collect(order, done, gst):
        def run(va, vf):
            n = len(order)
            ended = 0
            for k in range(done, n):
                if k == n - 1:
                    small_middle()
                pump(order[k], gst)
                if direct:
                    while ended <= k - 3:
                        finish(order[ended], va, vf)
                        ended += 1
            if direct:
                while ended < n:
                    finish(order[ended], va, vf)
                    ended += 1
            small_end()
            for u in order:
                y_copy(u).wait_send()
            for e in range(ex):
                for cp in out_copies(1, e):
                    cp.wait()

        V = pltpu.VMEM
        pl.run_scoped(run, V((width, kc), bf16), V((width // count, kc), f32))

    def begun():
        for i in range(10):
            w_copy(i).wait_send()
        for e in range(ex):
            cot_copy(e).wait_send()

    V = pltpu.VMEM
    feed = V((ex, 2, 2, tb, fc), bf16)
    grad_stage = V((2, half, 2 * kc), bf16)
    score_sums = V((heads, seq, seq), bf16)
    last = ex - 1

    def pass_all(e, fn):
        for p in range(pairs):
            fn(pass_copy(e, p))

    def wide(ref, e, i, ch):
        return jnp.concatenate([ref[e, p, i, :, ch].reshape(rows, PAIR) for p in range(pairs)], 1)

    @pl.when(pipe == 0)
    def _():
        def own_length(e):
            return len_ref[side * ex + e, 0]

        def keys(i):
            return lambda: jnp.concatenate(
                [kvr[:, p, i].reshape(ex * seq, PAIR) for p in range(pairs)], 1
            )

        def run(act, dg, dsacc, gst):
            def ahead(e):
                self_forward(e, 0, own_length(e))

                @pl.when(e == 0)
                def _():
                    for i in (W_F1, W_G1, W_F2, W_G2, W_C1, W_C2):
                        w_on(i)
                    for i in (W_F1, W_G1, W_F2, W_G2):
                        w_done(i)

                ffn_expand(e, h1, act, dg, False)
                r2[e] = h1[e] + scatter(S_FFN, e, 1, ffn_out_part(e, act))
                memory = norm(r2[e], 1)
                gather_start(G_MID, mid, e, memory)
                hand_out(0, e, memory)

                @pl.when(e == 0)
                def _():
                    for i in (W_C1, W_C2):
                        w_done(i)

                def project(a, ch):
                    for i, w in enumerate((w1, w2)):
                        out = nt(a, w[...]).astype(bf16)
                        for p in range(pairs):
                            kvs[e, p, i, :, ch] = out[:, p * PAIR : (p + 1) * PAIR].reshape(
                                2, tb, PAIR
                            )

                gather_use(G_MID, mid, e, project)
                pass_all(e, lambda cp: cp.start())

            def back(e):
                pass_all(e, lambda cp: cp.wait())
                cot_copy(e).wait_recv()

                def partial_sum(ch):
                    return nn(wide(kvr, e, 0, ch), w1[...]) + nn(wide(kvr, e, 1, ch), w2[...])

                scatter_start(S_DMEM, e, 1, partial_sum)

                @pl.when(e == last)
                def _():
                    pair_grads(4, mid, keys(0), mid, keys(1), None, gst, False)

                dmem = cot_rows(e).astype(f32) + (scatter_end(S_DMEM, e, 1) + rsa[...])
                r2[e] = norm_back(r2[e], 1, dmem)
                gather_start(G_DFFN, fffn, e, r2[e].astype(bf16))
                ffn_contract(e, dg, True)
                scatter_start(S_DFFN, e, 0, ffn_in_part(e, dg))

                @pl.when(e == last)
                def _():
                    ffn_grads(2, fffn, act, gst, False)

                dn = scatter_end(S_DFFN, e, 0) + rsa[...]
                r2[e] += norm_back(h1[e], 2, dn)

                @pl.when(e == last)
                def _():
                    ffn_grads(0, ffnf, dg, gst, True)
                    for r in range(2):
                        drain(gst, r)
                    pump(4, gst)

                self_back(e, 0, own_length(e), dsacc)

            loop(ahead)
            dsacc[...] = jnp.zeros_like(dsacc)
            begun()
            loop(back)

        def outer(dsacc, gst):
            pl.run_scoped(lambda act, dg: run(act, dg, dsacc, gst), feed, feed)
            pump(2, gst)
            last_grads(dsacc, gst, lambda: pump(3, gst))
            collect((4, 2, 3, 0, 1, 5, 6), 3, gst)

        pl.run_scoped(outer, score_sums, grad_stage)

    @pl.when(pipe == 1)
    def _():
        def own_length(e):
            return len_ref[side * ex + e, 1]

        def run(act, dg, cq, cctx, clse, gst):
            def first(e):
                self_forward(e, lax.rem(e, 2), own_length(e))
                gather_start(G_MID, mid, e, norm(h1[e], 1))

            def second(e):
                def project(a, ch):
                    cq[e, :, ch] = nt(a, w1[...]).astype(bf16).reshape(2, tb, kc)

                gather_use(G_MID, mid, e, project)

            def third(e):
                cot_copy(e).wait_recv()
                gather_start(G_DFFN, fffn, e, cot_rows(e))

            def there_and_back(e):
                lq, _, sq, _ = block_of(cq, e)
                (lk, _), (lv, _) = pair_of(kvr, e, 0), pair_of(kvr, e, 1)
                lc, _, sc, _ = block_of(cctx, e)
                source_length = len_ref[side * ex + e, 0]
                attend(
                    lambda p: pass_copy(e, p).wait_recv(), lq(), lk, lv, source_length, False,
                    sc(), clse,
                )
                r2[e] = h1[e] + scatter(
                    S_MID, e, 1, lambda ch: nn(half_rows(cctx, e, ch, kc), w2[...])
                )
                ffn_expand(e, r2, act, dg, True)
                scatter_start(S_DFFN, e, 0, ffn_in_part(e, dg))
                scatter_send(S_FFN, e, 1, ffn_out_part(e, act)(1 - core))
                dn = scatter_end(S_DFFN, e, 0) + rsa[...]
                h2 = r2[e]
                grad = cot_rows(e).astype(f32) + norm_back(h2, 2, dn)
                rsa[...] = h2
                r2[e] = grad
                gather_start(G_DMID, fmid, e, grad.astype(bf16))
                out = rsa[...] + ffn_out_part(e, act)(core)
                hand_out(0, e, (out + scatter_end(S_FFN, e, 1)).astype(bf16))
                context_grad(G_DMID, fmid, e, w2)
                ldo = block_of(dctx, 0)[0]
                sk, sv = pair_of(kvs, e, 0)[1], pair_of(kvs, e, 1)[1]

                def store_values(p, value):
                    sv(p, value)
                    pass_copy(e, p).start()

                attend_back(
                    lq(), lk, lv, ldo(), lc(), clse, source_length, None, sq(), sk, store_values
                )
                dn = scatter(S_DMID, e, 0, lambda ch: nn(half_rows(cq, e, ch, kc), w1[...]))
                r2[e] += norm_back(h1[e], 1, dn)

            loop(first)
            for i in (W_C1, W_C2, W_F2):
                w_on(i)
            for i in (W_C1, W_C2):
                w_done(i)
            loop(second)
            for i in (W_G2, W_F1, W_G1):
                w_on(i)
            loop(third)
            for i in (W_F2, W_G2):
                w_done(i)
            loop(lambda e: ffn_contract(e, dg, False))
            for i in (W_F1, W_G1):
                w_done(i)
            begun()
            loop(there_and_back)
            ffn_grads(2, fffn, act, gst, False)
            ffn_grads(0, ffnf, dg, gst, True)
            lanes = pl.ds(0, kc)
            pair_grads(
                4, mid, lambda: all_rows(cq, lanes), fmid, lambda: all_rows(cctx, lanes),
                0.125, gst, True,
            )

        pl.run_scoped(
            run, feed, feed, V((ex, 2, 2, tb, kc), bf16), V((ex, 2, 2, tb, kc), bf16),
            V((2, rows, PAIR), f32), grad_stage,
        )

        def outer(dsacc, gst):
            dsacc[...] = jnp.zeros_like(dsacc)

            def body(e):
                self_back(e, lax.rem(e, 2), own_length(e), dsacc)
                pump(lax.rem(e + 2, 4), gst)

            loop(body)
            loop(lambda e: pass_all(e, lambda cp: cp.wait_send()))
            last_grads(dsacc, gst, lambda: None)
            collect((2, 3, 0, 1, 4, 5, 6), ex, gst)

        pl.run_scoped(outer, score_sums, grad_stage)


def run_sections(x, cot, w_in, w_out, c_1, c_2, f_1, f_2, gains, lens, table, hot, direct):
    batch, tb, width = x.shape
    ex = batch // 2
    rows, seq = 2 * tb, 4 * tb
    kq, fq = w_out.shape[0], f_1.shape[1]
    kc, fc = 2 * kq, 2 * fq
    heads = kc // DK
    count = lax.axis_size("dp")
    vmem = pl.BlockSpec(memory_space=pltpu.VMEM)
    hbm = pl.BlockSpec(memory_space=pl.ANY)
    smem = pl.BlockSpec(memory_space=pltpu.SMEM)
    full = (ex, 2, 2, tb)
    units = (7, width, kc)
    V = pltpu.VMEM
    D = pltpu.SemaphoreType.DMA
    S = jax.ShapeDtypeStruct
    scratch = [
        V((3 * kc, width), bf16), V((kc, width), bf16), V((kc, width), bf16), V((kc, width), bf16),
        V((2, width, fq), bf16), V((2, fq, width), bf16), V((heads, seq, seq), bf16),
        V((ex, 2, tb, width), bf16), V((ex, 2, tb, width), bf16),
        V((ex, 2, tb, width), bf16),
        V((*full, width), bf16),
        V((*full, 3 * kc), bf16),
        V((*full, kc), bf16),
        V((ex, 2, rows, PAIR), f32),
        V((ex, rows, width), f32),
        V((*full, width), bf16),
        V((*full, width), bf16),
        V((ex, kc // PAIR, 2, 2, 2, tb, PAIR), bf16),
        V((ex, kc // PAIR, 2, 2, 2, tb, PAIR), bf16),
        V((*full, width), bf16),
        V((ex, rows, width), f32),
        V((*full, width), bf16),
        V((*full, width), bf16),
        V((1, 2, 2, tb, kc), bf16),
        V((rows, width), f32),
        V((2, rows, width), bf16),
        V((2, rows, width), bf16),
        V((2, 8, 2 * seq), f32),
        V((16, 2 * seq), f32), V((8, 2 * seq), f32), V((16, 2 * seq), f32),
        V((max(1, count - 1) if direct else 1, 16, 2 * seq), f32),
        D((8 + 2 * ex,)),
        D((2, ex)), D((2, ex)), D((1,)), D((1,)), D((10,)), D((10,)), D((10,)), D((10,)),
        D((6, ex)), D((6, ex)), D((7, ex)), D((7, ex)), D((ex, kc // PAIR)), D((ex, kc // PAIR)),
        D((2, ex)), D((2, ex)), D((7,)), D((7,)), D((7, 3)), D((7, 3)), D((5,)), D((5,)),
    ]
    slots = count - 1 if direct else 1
    return pl.pallas_call(
        partial(section_kernel, direct=direct),
        out_shape=(
            S((batch, tb, width), bf16),
            S((batch, tb, width), bf16),
            S(units, bf16),
            S((7, slots, width // count if direct else 16, kc), bf16),
            S((7, width // count if direct else 8, kc), f32),
            S((16, 2 * seq), f32),
            S(units, bf16),
            S(units, bf16),
            S(units, bf16),
        ),
        in_specs=[hbm] * 8 + [vmem, smem, vmem, vmem],
        out_specs=(hbm, hbm, hbm, hbm, hbm, vmem, hbm, hbm, hbm),
        scratch_shapes=scratch,
        compiler_params=pltpu.CompilerParams(
            collective_id=0, has_side_effects=True, vmem_limit_bytes=64 * 2**20 - 65536
        ),
        name="sections",
    )(x, cot, w_in, w_out, c_1, c_2, f_1, f_2, gains, lens, table, hot)


def local(
    section_input, lengths, norm_gain, attn_in, attn_out, cross_first, cross_second,
    ffn_in, ffn_out, rel_bias, out_grad,
):
    pipe = lax.axis_index("pipe")
    enc = pipe == 0
    tb, width = section_input.shape[2:]
    seq = tb * lax.axis_size("tensor")
    kq, fq = attn_out.shape[1], ffn_out.shape[1]
    data = lax.axis_size("dp")
    at_data = lax.axis_index("dp")
    direct = data <= 4 and (width // data) % 16 == 0

    offsets = list(range(seq)) + [0] + list(range(-seq + 1, 0))
    both = [np.array(bucket_list(offsets, ways)) for ways in (True, False)]
    hot = np.stack([np.arange(NB)[:, None] == spots[None] for spots in both])

    sec, ing, zs, _, fin, small, _, _, _ = run_sections(
        section_input[0], out_grad[0], attn_in[0], attn_out[0], cross_first[0], cross_second[0],
        ffn_in[0], ffn_out[0], norm_gain[0], lengths, rel_bias[0], jnp.asarray(hot, bf16), direct,
    )

    turned = [seq - 1 - m for m in range(2 * seq)]
    hot_m = np.stack(
        [np.array(bucket_list(turned, ways))[:, None] == np.arange(NB) for ways in (True, False)]
    )
    hot_m = jnp.where(enc, jnp.asarray(hot_m[0], f32), jnp.asarray(hot_m[1], f32))
    bsum = jnp.einsum(
        "mb,hm->bh", hot_m, small[8 : 8 + kq // DK], precision=lax.Precision.HIGHEST
    )
    gains = small[:3, :width]
    if direct:
        shard = fin
        share = NB // data
        bias_grad = lax.dynamic_slice_in_dim(bsum, at_data * share, share, 0)
    else:
        packed = zs.reshape(7, data, width // data, 2 * kq)
        shard = lax.psum_scatter(packed, "dp", scatter_dimension=1, tiled=False).astype(f32)
        bias_grad = lax.psum_scatter(bsum, "dp", scatter_dimension=0, tiled=True)
        gains = lax.psum(gains, "dp")
    share = width // (data * lax.axis_size("tensor"))
    at = (at_data * lax.axis_size("tensor") + lax.axis_index("tensor")) * share
    gain_grad = lax.dynamic_slice_in_dim(gains, at, share, 1)

    def first_of(u):
        return jnp.concatenate([shard[u, :, :128], shard[u, :, 128:192]], 1)

    def second_of(u):
        return jnp.concatenate([shard[u, :, 256:], shard[u, :, 192:256]], 1)

    f_in = jnp.concatenate([shard[0], shard[1]], 1)
    f_out = jnp.concatenate([shard[2], shard[3]], 1).T
    w_in = jnp.stack([first_of(5), second_of(5), first_of(6)])
    return (
        sec[None],
        ing[None].astype(f32),
        w_in[None],
        second_of(6).T[None],
        first_of(4)[None],
        second_of(4)[None],
        f_in[None],
        f_out[None],
        bias_grad[None],
        gain_grad[None],
    )


def solution(mesh):
    placed = (
        P("pipe", "dp", "tensor", None),
        P("dp", None),
        P("pipe", None, None),
        P("pipe", None, None, "tensor"),
        P("pipe", "tensor", None),
        P("pipe", None, "tensor"),
        P("pipe", None, "tensor"),
        P("pipe", None, "tensor"),
        P("pipe", "tensor", None),
        P("pipe", None, "tensor"),
        P("pipe", "dp", "tensor", None),
    )
    return jax.shard_map(
        local,
        mesh=mesh,
        in_specs=placed,
        out_specs=(
            P("pipe", "dp", "tensor", None),
            P("pipe", "dp", "tensor", None),
            P("pipe", None, "dp", "tensor"),
            P("pipe", "tensor", "dp"),
            P("pipe", "dp", "tensor"),
            P("pipe", "dp", "tensor"),
            P("pipe", "dp", "tensor"),
            P("pipe", "tensor", "dp"),
            P("pipe", "dp", "tensor"),
            P("pipe", None, ("dp", "tensor")),
        ),
        check_vma=False,
    )
```

```python
import math
from functools import partial

import jax
import jax.numpy as jnp
import numpy as np
from jax import lax
from jax.experimental import pallas as pl
from jax.experimental.pallas import tpu as pltpu
from jax.sharding import PartitionSpec as P

NB = 32
MAX_DIST = 128
DK = 64
EPS = 1e-06
MASKED = -1000000000.0
MESH = pl.DeviceIdType.MESH
bf16, f32 = jnp.bfloat16, jnp.float32
PAIR = 128
G_IN, G_MID, G_FFN, G_DFFN, G_DMID, G_DATT = range(6)
S_ATT, S_MID, S_FFN, S_DMEM, S_DFFN, S_DMID, S_DIN = range(7)


def bucket_list(offsets, both_ways):
    half = NB // 2 if both_ways else NB
    exact = half // 2
    out = []
    for r in offsets:
        base = half if both_ways and r > 0 else 0
        n = abs(r) if both_ways else max(-r, 0)
        if n < exact:
            out.append(base + n)
        else:
            at = exact + math.floor(
                math.log(n / exact) / math.log(MAX_DIST / exact) * (half - exact)
            )
            out.append(base + min(half - 1, at))
    return out


def nt(a, b):
    return lax.dot_general(a, b, (((1,), (1,)), ((), ())), preferred_element_type=f32)


def nn(a, b):
    return lax.dot_general(a, b, (((1,), (0,)), ((), ())), preferred_element_type=f32)


def tn(a, b):
    return lax.dot_general(a, b, (((0,), (0,)), ((), ())), preferred_element_type=f32)


W_Q, W_K, W_V, W_O, W_C1, W_C2, W_F1, W_G1, W_F2, W_G2 = range(10)


def section_kernel(
    xin, cin, w_in, w_out, c_1, c_2, f_1, f_2, gain_ref, len_ref, table_ref, hot_ref,
    sec_out, ing_out, zs, zr, fin_out, small_out, gown, ysend, yrecv,
    wqkv, wo, w1, w2, wf1, wf2, bias,
    xr, cot, out_rows,
    fin, qkv, ctx, lse, h1, fatt, mid, kvs, kvr,
    r2, ffnf, fffn, dctx, rsa, rss, rsr, diag, small, small_c, small_y, small_z,
    lsem, xs, xg, ts, tg, ys, yg, zps, zpg, gs, gr, ss, sr, ps, pr, os, og, us, ug, vs, vg, ms, mg,
    *, direct,
):
    ex, _, tb, width = xr.shape
    fmid = fatt
    rows = 2 * tb
    kq = wo.shape[0] // 2
    kc = wo.shape[0]
    fq = wf1.shape[2]
    fc = 2 * fq
    seq = 2 * rows
    heads = kc // DK
    pairs = kc // PAIR
    own_heads = heads // 2

    tensor = lax.axis_index("tensor")
    pipe = lax.axis_index("pipe")
    data = lax.axis_index("dp")
    count = lax.axis_size("dp")
    core = lax.rem(tensor, 2)
    side = tensor // 2
    parity = lax.rem(data, 2)
    partner = {"tensor": tensor + 1 - 2 * core}
    peer = {"tensor": lax.rem(tensor + 2, 4)}
    near = {"dp": data + 1 - 2 * parity}
    other = {"pipe": 1 - pipe}

    def away(step):
        return lax.rem(data + step, count)

    barrier = pltpu.get_barrier_semaphore()
    met = [partner, peer, other]
    met += [{"dp": away(i)} for i in range(1, count)] if direct else [near]
    for device in met:
        pl.semaphore_signal(barrier, 1, device_id=device, device_id_type=MESH)

    def remote(src, dst, send, recv, device):
        return pltpu.make_async_remote_copy(
            src, dst, send, recv, device_id=device, device_id_type=MESH
        )

    def own_copies():
        pairs_of = [(w_in.at[i], wqkv.at[pl.ds(i * kc, kq)]) for i in range(3)]
        pairs_of += [(w, home_of.at[pl.ds(0, kq)]) for w, home_of in ((w_out, wo), (c_1, w1), (c_2, w2))]
        pairs_of += [(f_1, wf1.at[0]), (f_2, wf2.at[0])]
        for e in range(ex):
            pairs_of.append((xin.at[side * ex + e], xr.at[e, side]))
        for e in range(ex):
            pairs_of.append((cin.at[side * ex + e], cot.at[e, side]))
        return [pltpu.make_async_copy(p, q, lsem.at[i]) for i, (p, q) in enumerate(pairs_of)]

    def x_copy(e):
        return remote(xin.at[(1 - side) * ex + e], xr.at[e, side], xs.at[0, e], xg.at[0, e], peer)

    def cot_copy(e):
        return remote(cin.at[(1 - side) * ex + e], cot.at[e, side], xs.at[1, e], xg.at[1, e], peer)

    def diag_copy():
        return remote(diag.at[0], diag.at[1], ts.at[0], tg.at[0], peer)

    half_kq, part_fq = kq // 2, wf1.shape[1] // 4

    def rows_at(first, n):
        return pl.ds(pl.multiple_of(first, 16), n)

    def small_ref(i):
        return (wqkv, i * kc + kq) if i < 3 else ((wo, w1, w2)[i - 3], kq)

    def big_rows(i, part):
        return rows_at((2 * ((i - W_F1) % 2) + part) * part_fq, part_fq)

    def home(i, part):
        if i >= W_F1:
            return (wf1, wf2)[(i - W_F1) // 2].at[1, big_rows(i, part)]
        ref, first = small_ref(i)
        return ref.at[rows_at(first + part * half_kq, half_kq)]

    def w_copies(i):
        if i >= W_F1:
            src = (f_1, f_2)[(i - W_F1) // 2].at[big_rows(i, parity)]
            return [remote(src, home(i, parity), ys.at[i, 0], yg.at[i, 0], peer)]
        src = w_in.at[i] if i < 3 else (w_out, c_1, c_2)[i - 3]
        ref, first = small_ref(i)
        long, short = DK, half_kq - DK
        froms = (jnp.where(parity == 0, kq - DK, short), jnp.where(parity == 0, 0, DK + short))
        out = []
        for j, (at, n, skip) in enumerate(((froms[0], long, 0), (froms[1], short, long))):
            dst = ref.at[rows_at(first + parity * half_kq + skip, n)]
            out.append(remote(src.at[rows_at(at, n)], dst, ys.at[i, j], yg.at[i, j], peer))
        return out

    def w_start(order):
        for i in order:
            for cp in w_copies(i):
                cp.start()

    def w_pass(i):
        return remote(home(i, parity), home(i, parity), zps.at[i], zpg.at[i], near)

    def w_on(i):
        for cp in w_copies(i):
            cp.wait_recv()
        w_pass(i).start()

    def w_done(i):
        w_pass(i).wait()

    copies = own_copies()
    for cp in copies:
        cp.start()
    pl.semaphore_wait(barrier, len(met))
    x_copy(0).start()
    w_start((W_Q, W_K, W_V))
    values = nn(table_ref[...], hot_ref[pipe])
    at_m = lax.broadcasted_iota(jnp.int32, (1, 2 * seq), 1)
    hidden = jnp.logical_and(jnp.logical_and(at_m > 0, at_m < seq), pipe == 1)
    diag[0, 0:own_heads] = jnp.where(hidden, MASKED, values)
    diag[0, own_heads:] = jnp.zeros((8 - own_heads, 2 * seq), f32)
    diag_copy().start()
    w_start((W_O,))

    @pl.when(pipe == 0)
    def _():
        w_start((W_F1, W_G1, W_F2, W_G2, W_C1, W_C2))

    for e in range(1, ex):
        x_copy(e).start()

    @pl.when(pipe == 1)
    def _():
        w_start((W_C1, W_C2, W_F2, W_G2, W_F1, W_G1))

    for e in range(ex):
        cot_copy(e).start()
    small[...] = jnp.zeros_like(small)
    for cp in copies:
        cp.wait()
    diag_copy().wait()
    local_order = [(0, h) for h in range(own_heads)] + [(1, (h + 2) % 3) for h in range(own_heads)]
    for h, (from_side, at) in enumerate(local_order):
        wide = jnp.broadcast_to(diag[from_side, at : at + 1, :], (seq, 2 * seq))
        bias[h] = pltpu.roll(wide, 0, 1, stride=1, stride_axis=0)[:, :seq].astype(bf16)
    for i in (W_Q, W_K, W_V, W_O):
        w_on(i)
    for i in (W_Q, W_K, W_V):
        w_done(i)
    wqkv[0:kc] = wqkv[0:kc] * jnp.asarray(0.125, bf16)

    lane = lax.broadcasted_iota(jnp.int32, (1, PAIR), 1)
    half_f = [jnp.where(lane // DK == hh, 1.0, 0.0) for hh in range(2)]
    half_b = [m.astype(bf16) for m in half_f]
    key_at = lax.broadcasted_iota(jnp.int32, (1, seq), 1)

    def key_mask(length):
        return jnp.where(key_at < length, 0.0, MASKED)

    def gather_copy(kind, buf, e):
        return remote(
            buf.at[e, :, core], buf.at[e, :, core], gs.at[kind, e], gr.at[kind, e], partner
        )

    def gather_start(kind, buf, e, value):
        buf[e, :, core] = value.reshape(2, tb, width)
        gather_copy(kind, buf, e).start()

    def gather_use(kind, buf, e, fn):
        def body(i, _):
            ch = lax.rem(core + i, 2)

            @pl.when(i == 1)
            def _():
                gather_copy(kind, buf, e).wait()

            fn(buf[e, :, ch].reshape(rows, width), ch)
            return 0

        lax.fori_loop(0, 2, body, 0)

    def scatter_copy(kind, e, slot):
        return remote(rss.at[slot], rsr.at[slot], ss.at[kind, e], sr.at[kind, e], partner)

    def scatter_send(kind, e, slot, value):
        rss[slot] = value.astype(bf16)
        scatter_copy(kind, e, slot).start()

    def scatter_start(kind, e, slot, fn):
        def body(i, _):
            ch = lax.rem(core + 1 + i, 2)
            rsa[...] = fn(ch)

            @pl.when(i == 0)
            def _():
                scatter_send(kind, e, slot, rsa[...])

            return 0

        lax.fori_loop(0, 2, body, 0)

    def scatter_end(kind, e, slot):
        scatter_copy(kind, e, slot).wait()
        return rsr[slot].astype(f32)

    def scatter(kind, e, slot, fn):
        scatter_start(kind, e, slot, fn)
        return scatter_end(kind, e, slot) + rsa[...]

    def norm(v, row):
        inv = lax.rsqrt(jnp.mean(v * v, axis=-1, keepdims=True) + EPS)
        return (v * inv * gain_ref[row]).astype(bf16)

    def norm_back(v, row, grad):
        inv = lax.rsqrt(jnp.mean(v * v, axis=-1, keepdims=True) + EPS)
        unit = v * inv
        small[pl.ds(row, 1), 0:width] += jnp.sum(grad * unit, axis=0, keepdims=True)
        gg = grad * gain_ref[row]
        return inv * (gg - unit * jnp.mean(gg * unit, axis=-1, keepdims=True))

    def attend(ready, load_q, load_k, load_v, length, use_bias, store_ctx, lse_ref):
        mask = key_mask(length)

        def body(p, _):
            ready(p)
            k, v = load_k(p), load_v(p)
            for yb in range(2):
                q = load_q(yb, p)
                total = scale = None
                lse_t = lse_ref[yb]
                for hh in range(2):
                    h = 2 * p + hh
                    s = nt(q * half_b[hh], k) + mask
                    if use_bias:
                        s = s + bias[h, pl.ds(yb * rows, rows), :].astype(f32)
                    top = jnp.max(s, axis=-1, keepdims=True)
                    w = jnp.exp(s - top)
                    den = jnp.sum(w, axis=-1, keepdims=True)
                    part = nn(w.astype(bf16), v * half_b[hh])
                    total = part if total is None else total + part
                    inv = (1.0 / den) * half_f[hh]
                    scale = inv if scale is None else scale + inv
                    lse_t = jnp.where(lane == h, top + jnp.log(den), lse_t)
                store_ctx(yb, p, (total * scale).astype(bf16))
                lse_ref[yb] = lse_t
            return 0

        lax.fori_loop(0, pairs, body, 0)

    def attend_back(
        load_q, load_k, load_v, load_do, load_o, lse_ref, length, dsacc, store_dq, store_dk, store_dv
    ):
        mask = key_mask(length)

        def body(p, _):
            k, v = load_k(p), load_v(p)
            dk = dv = None
            for yb in range(2):
                q, do = load_q(yb, p), load_do(yb, p)
                both = do.astype(f32) * load_o(yb, p).astype(f32)
                lse_t = lse_ref[yb]
                dq = None
                for hh in range(2):
                    h = 2 * p + hh
                    qm, dom = q * half_b[hh], do * half_b[hh]
                    lse_c = jnp.sum(jnp.where(lane == h, lse_t, 0.0), axis=-1, keepdims=True)
                    delta = jnp.sum(both * half_f[hh], axis=-1, keepdims=True)
                    s = nt(qm, k) + mask
                    if dsacc is not None:
                        s = s + bias[h, pl.ds(yb * rows, rows), :].astype(f32)
                    w = jnp.exp(s - lse_c)
                    ds = w * (nt(dom, v) - delta)
                    wb, db = w.astype(bf16), ds.astype(bf16)
                    if dsacc is not None:
                        at = pl.ds(yb * rows, rows)
                        dsacc[h, at, :] = (dsacc[h, at, :].astype(f32) + ds).astype(bf16)
                    dvp, dkp, dqp = tn(wb, dom), tn(db, qm), nn(db, k * half_b[hh])
                    dv = dvp if dv is None else dv + dvp
                    dk = dkp if dk is None else dk + dkp
                    dq = dqp if dq is None else dq + dqp
                store_dq(yb, p, dq.astype(bf16))
            store_dk(p, dk.astype(bf16))
            store_dv(p, dv.astype(bf16))
            return 0

        lax.fori_loop(0, pairs, body, 0)

    def block_of(ref, *at):
        def lanes_at(first, p):
            return pl.ds(pl.multiple_of(first + p * PAIR, PAIR), PAIR)

        def load_rows(first=0):
            return lambda yb, p: ref[(*at, yb, slice(None), slice(None), lanes_at(first, p))].reshape(rows, PAIR)

        def load_all(first=0):
            return lambda p: ref[(*at, slice(None), slice(None), slice(None), lanes_at(first, p))].reshape(seq, PAIR)

        def store_rows(first=0):
            def store(yb, p, value):
                ref[(*at, yb, slice(None), slice(None), lanes_at(first, p))] = value.reshape(2, tb, PAIR)

            return store

        def store_all(first=0):
            def store(p, value):
                ref[(*at, slice(None), slice(None), slice(None), lanes_at(first, p))] = value.reshape(2, 2, tb, PAIR)

            return store

        return load_rows, load_all, store_rows, store_all

    def pair_of(ref, e, i):
        def load(p):
            return ref[e, p, i].reshape(seq, PAIR)

        def store(p, value):
            ref[e, p, i] = value.reshape(2, 2, tb, PAIR)

        return load, store

    def in_rows(e):
        return xr[e].reshape(rows, width).astype(f32)

    def cot_rows(e):
        return cot[e].reshape(rows, width)

    def half_rows(ref, e, ch, count):
        return ref[e, :, ch].reshape(rows, count)

    def self_forward(e, slot, length, middle=None):
        x_copy(e).wait()
        gather_start(G_IN, fin, e, norm(in_rows(e), 0))

        def project(a, ch):
            qkv[e, :, ch] = nt(a, wqkv[...]).astype(bf16).reshape(2, tb, 3 * kc)

        gather_use(G_IN, fin, e, project)
        lr, la, _, _ = block_of(qkv, e)
        _, _, store_ctx, _ = block_of(ctx, e)

        def ready(p):
            pass

        attend(ready, lr(), la(kc), la(2 * kc), length, True, store_ctx(), lse.at[e])

        @pl.when(e == 0)
        def _():
            w_done(W_O)

        if middle is not None:
            middle()

        h1[e] = in_rows(e) + scatter(
            S_ATT, e, slot, lambda ch: nn(half_rows(ctx, e, ch, kc), wo[...])
        )

    def ffn_expand(e, src, act, dg, has_grad):
        gather_start(G_FFN, ffnf, e, norm(src[e], 2))

        def expand(a, ch):
            for i in range(2):
                pre = nn(a, wf1[i])
                sq = pre * pre
                th = jnp.tanh(0.7978845608028654 * pre * (1.0 + 0.044715 * sq))
                gate = 0.5 + 0.5 * th
                slope = gate + (0.5 * 0.7978845608028654) * pre * (1.0 - th * th) * (
                    1.0 + (3 * 0.044715) * sq
                )
                lanes = pl.ds(i * fq, fq)
                act[e, :, ch, :, lanes] = (pre * gate).astype(bf16).reshape(2, tb, fq)
                if has_grad:
                    slope = slope * dg[e, :, ch, :, lanes].reshape(rows, fq).astype(f32)
                dg[e, :, ch, :, lanes] = slope.astype(bf16).reshape(2, tb, fq)

        gather_use(G_FFN, ffnf, e, expand)

    def ffn_out_part(e, act):
        return lambda ch: nn(half_rows(act, e, ch, fc), wf2[...].reshape(fc, width))

    def ffn_in_part(e, dg):
        def part(ch):
            both = half_rows(dg, e, ch, fc)
            return nt(both[:, :fq], wf1[0]) + nt(both[:, fq:], wf1[1])

        return part

    def ffn_contract(e, dg, has_slope):
        def contract(a, ch):
            for i in range(2):
                lanes = pl.ds(i * fq, fq)
                dact = nt(a, wf2[i])
                if has_slope:
                    dact = dact * dg[e, :, ch, :, lanes].reshape(rows, fq).astype(f32)
                dg[e, :, ch, :, lanes] = dact.astype(bf16).reshape(2, tb, fq)

        gather_use(G_DFFN, fffn, e, contract)

    def context_grad(kind, buf, e, w):
        def project(a, ch):
            dctx[0, :, ch] = nt(a, w[...]).astype(bf16).reshape(2, tb, kc)

        gather_use(kind, buf, e, project)

    def self_back(e, slot, length, dsacc, between=None):
        gather_start(G_DATT, fatt, e, r2[e].astype(bf16))
        context_grad(G_DATT, fatt, e, wo)
        if between is not None:
            between()
        lr, la, sr_, sa_ = block_of(qkv, e)
        ldo = block_of(dctx, 0)[0]
        lo = block_of(ctx, e)[0]
        attend_back(
            lr(), la(kc), la(2 * kc), ldo(), lo(), lse.at[e], length, dsacc,
            sr_(), sa_(kc), sa_(2 * kc),
        )
        dn = scatter(S_DIN, e, slot, lambda ch: nn(half_rows(qkv, e, ch, 3 * kc), wqkv[...]))
        hand_out(1, e, (r2[e] + norm_back(in_rows(e), 0, dn)).astype(bf16), e == ex - 1)

    def out_copies(kind, e):
        at, out = side * ex + e, (sec_out, ing_out)[kind]
        return (
            pltpu.make_async_copy(out_rows.at[e, side], out.at[at], lsem.at[8 + kind * ex + e]),
            remote(out_rows.at[e, 1 - side], out.at[at], os.at[kind, e], og.at[kind, e], peer),
        )

    def hand_out(kind, e, value, later=False):
        if kind == 1:
            for cp in out_copies(0, e):
                cp.wait()
        out_rows[e] = value.reshape(2, tb, width)

        def start():
            for cp in out_copies(kind, e):
                cp.start()

        pl.when(jnp.logical_not(later))(start)

    def pass_copy(e, p):
        return remote(kvs.at[e, p], kvr.at[e, p], ps.at[e, p], pr.at[e, p], other)

    def y_copy(u):
        return remote(ysend.at[u], yrecv.at[u], us.at[u], ug.at[u], peer)

    def all_rows(ref, lanes):
        n = lanes.size
        return ref[:, :, :, :, lanes].reshape(ex * seq, n)

    half = width // 2

    def lanes_of(r):
        return pl.ds(pl.multiple_of(r * half, PAIR), half)

    def stage_copy(gst, r, i, dst, u):
        return pltpu.make_async_copy(
            gst.at[r, :, pl.ds(i * kc, kc)], dst.at[u, lanes_of(r)], lsem.at[2 * r + i]
        )

    def drain(gst, r):
        for i in range(2):
            stage_copy(gst, r, i, gown, 0).wait()

    def ffn_grads(u, src, feed_ref, gst, pending):
        def to(dst, first, wait, sent):
            def body(r, _):
                if wait:
                    drain(gst, r)
                if sent:

                    @pl.when(r == 1)
                    def _():
                        for i in range(2):
                            y_copy(u + i).start()

                rhs = all_rows(feed_ref, pl.ds(first, fq))
                gst[r] = tn(all_rows(src, lanes_of(r)), rhs).astype(bf16)
                for i in range(2):
                    stage_copy(gst, r, i, dst, u + i).start()
                return 0

            lax.fori_loop(0, 2, body, 0)

        to(ysend, fq, pending, False)
        to(gown, 0, True, True)

    def pair_grads(u, lhs_a, load_a, lhs_b, load_b, scale, gst, pending):
        def body(r, _):
            if pending:
                drain(gst, r)
            a = tn(all_rows(lhs_a, lanes_of(r)), load_a())
            if scale is not None:
                a = a * scale
            b = tn(all_rows(lhs_b, lanes_of(r)), load_b())
            low = lane < DK
            a1, b1 = a[:, PAIR : 2 * PAIR], b[:, PAIR : 2 * PAIR]
            mix_own = jnp.where(low, a1, pltpu.roll(b1, DK, 1))
            mix_peer = jnp.where(low, pltpu.roll(a1, DK, 1), b1)
            for j, part in enumerate(
                (a[:, :PAIR], mix_own, b[:, :PAIR], a[:, 2 * PAIR :], mix_peer, b[:, 2 * PAIR :])
            ):
                gst[r, :, j * PAIR : (j + 1) * PAIR] = part.astype(bf16)
            for i, dst in enumerate((gown, ysend)):
                stage_copy(gst, r, i, dst, u).start()
            return 0

        lax.fori_loop(0, 2, body, 0)
        for r in range(2):
            drain(gst, r)
        y_copy(u).start()

    def z_copy(u, step):
        block = width // count
        at = away(step)
        return remote(
            zs.at[u, pl.ds(pl.multiple_of(at * block, 16), block)], zr.at[u, step - 1],
            vs.at[u, step - 1], vg.at[u, step - 1], {"dp": at},
        )

    def pump(u, gst):
        y_copy(u).wait_recv()
        loads, stores = [], []
        for r in range(2):
            own, came = gst.at[r, :, pl.ds(0, kc)], gst.at[r, :, pl.ds(kc, kc)]
            loads.append(pltpu.make_async_copy(gown.at[u, lanes_of(r)], own, lsem.at[4 + r]))
            loads.append(pltpu.make_async_copy(yrecv.at[u, lanes_of(r)], came, lsem.at[6 + r]))
            stores.append(pltpu.make_async_copy(own, zs.at[u, lanes_of(r)], lsem.at[4 + r]))
        for cp in loads:
            cp.start()
        for r in range(2):
            for cp in loads[2 * r : 2 * r + 2]:
                cp.wait()
            gst[r, :, 0:kc] = (
                gst[r, :, 0:kc].astype(f32) + gst[r, :, kc : 2 * kc].astype(f32)
            ).astype(bf16)
            stores[r].start()
        for cp in stores:
            cp.wait()
        if direct:
            for step in range(1, count):
                z_copy(u, step).start()

    def finish(u, va, vf):
        block = width // count
        for step in range(1, count):
            z_copy(u, step).wait()
        mine = pl.ds(pl.multiple_of(data * block, 16), block)
        cps = [pltpu.make_async_copy(zs.at[u, mine], va.at[pl.ds(0, block)], lsem.at[0])]
        for step in range(1, count):
            cps.append(
                pltpu.make_async_copy(
                    zr.at[u, step - 1], va.at[pl.ds(step * block, block)], lsem.at[step]
                )
            )
        for cp in cps:
            cp.start()
        for cp in cps:
            cp.wait()
        total = va[0:block].astype(f32)
        for step in range(1, count):
            total = total + va[step * block : (step + 1) * block].astype(f32)
        vf[...] = total
        cp = pltpu.make_async_copy(vf, fin_out.at[u], lsem.at[0])
        cp.start()
        cp.wait()

    def small_near():
        first = remote(small.at[pl.ds(0, 8)], small_c, ms.at[0], mg.at[0], partner)
        first.start()
        first.wait()
        small[0:8] += small_c[...]
        small_peer().start()

    def small_peer():
        return remote(small, small_y, ms.at[1], mg.at[1], peer)

    def small_far():
        return [
            remote(small, small_z.at[i - 1], ms.at[1 + i], mg.at[1 + i], {"dp": away(i)})
            for i in range(1, count)
        ]

    def small_middle():
        small_peer().wait()
        small[0:8] += small_y[0:8]
        for h in range(own_heads):
            at = 8 + own_heads + (h + 1) % 3
            small[8 + h : 9 + h] += small_y[at : at + 1]
        if direct:
            for cp in small_far():
                cp.start()

    def small_end():
        total = small[...]
        if direct:
            for cp in small_far():
                cp.wait()
            for i in range(1, count):
                total = total + small_z[i - 1]
        small_out[...] = total

    def bias_grads(dsacc):
        at_r = lax.broadcasted_iota(jnp.int32, (seq, seq), 0)
        at_c = lax.broadcasted_iota(jnp.int32, (seq, seq), 1)
        flip = jnp.where(at_r + at_c == seq - 1, 1.0, 0.0).astype(bf16)

        def body(h, _):
            reverse = nn(dsacc[h], flip)
            wide = jnp.concatenate([reverse, jnp.zeros((seq, seq), f32)], axis=1)
            wide = pltpu.roll(wide, 0, 1, stride=1, stride_axis=0)
            small[pl.ds(8 + h, 1), :] = jnp.sum(wide, axis=0, keepdims=True)
            return 0

        lax.fori_loop(0, heads, body, 0)

    def loop(fn):
        def body(e, _):
            fn(e)
            return 0

        lax.fori_loop(0, ex, body, 0)

    def last_grads(dsacc, gst, between, small_first):
        def small_now():
            bias_grads(dsacc)
            small_near()

        lanes = [pl.ds(i * kc, kc) for i in range(3)]
        if small_first:
            small_now()
            between()
        pair_grads(
            5, fin, lambda: all_rows(qkv, lanes[0]), fin, lambda: all_rows(qkv, lanes[1]),
            0.125, gst, False,
        )
        pair_grads(
            6, fin, lambda: all_rows(qkv, lanes[2]), fatt, lambda: all_rows(ctx, lanes[0]),
            None, gst, False,
        )
        if not small_first:
            between()
            small_now()
        for cp in out_copies(1, ex - 1):
            cp.start()

    def collect(order, done, gst, small_first):
        def run(va, vf):
            n = len(order)
            ended = 0
            for k in range(done, n):
                if direct:
                    while ended <= k - 3:
                        finish(order[ended], va, vf)
                        ended += 1
                if k == n - 1 and small_first:
                    small_middle()
                pump(order[k], gst)
            if not small_first:
                small_middle()
            if direct:
                while ended < n:
                    finish(order[ended], va, vf)
                    ended += 1
            small_end()
            for u in order:
                y_copy(u).wait_send()
            for e in range(ex):
                for cp in out_copies(1, e):
                    cp.wait()

        V = pltpu.VMEM
        pl.run_scoped(run, V((width, kc), bf16), V((width // count, kc), f32))

    def begun():
        for i in range(10):
            for cp in w_copies(i):
                cp.wait_send()
        for e in range(ex):
            cot_copy(e).wait_send()

    V = pltpu.VMEM
    feed = V((ex, 2, 2, tb, fc), bf16)
    grad_stage = V((2, half, 2 * kc), bf16)
    score_sums = V((heads, seq, seq), bf16)
    last = ex - 1

    def pass_all(e, fn):
        for p in range(pairs):
            fn(pass_copy(e, p))

    def wide(ref, e, i, ch):
        return jnp.concatenate([ref[e, p, i, :, ch].reshape(rows, PAIR) for p in range(pairs)], 1)

    @pl.when(pipe == 0)
    def _():
        def own_length(e):
            return len_ref[0, side * ex + e]

        def keys(i):
            return lambda: jnp.concatenate(
                [kvr[:, p, i].reshape(ex * seq, PAIR) for p in range(pairs)], 1
            )

        def run(act, dg, dsacc, gst):
            def ahead(e):
                def middle():
                    pl.when(e == 0)(lambda: w_on(W_F1))

                self_forward(e, 0, own_length(e), middle)

                @pl.when(e == 0)
                def _():
                    for i in (W_G1, W_F2, W_G2):
                        w_on(i)
                    for i in (W_F1, W_G1, W_F2, W_G2):
                        w_done(i)

                ffn_expand(e, h1, act, dg, False)

                @pl.when(e == 0)
                def _():
                    for i in (W_C1, W_C2):
                        w_on(i)

                r2[e] = h1[e] + scatter(S_FFN, e, 1, ffn_out_part(e, act))
                memory = norm(r2[e], 1)
                gather_start(G_MID, mid, e, memory)
                hand_out(0, e, memory)

                @pl.when(e == 0)
                def _():
                    for i in (W_C1, W_C2):
                        w_done(i)

                def project(a, ch):
                    for i, w in enumerate((w1, w2)):
                        out = nt(a, w[...]).astype(bf16)
                        for p in range(pairs):
                            kvs[e, p, i, :, ch] = out[:, p * PAIR : (p + 1) * PAIR].reshape(
                                2, tb, PAIR
                            )

                gather_use(G_MID, mid, e, project)
                pass_all(e, lambda cp: cp.start())

            def back(e):
                pass_all(e, lambda cp: cp.wait())
                cot_copy(e).wait_recv()

                def partial_sum(ch):
                    return nn(wide(kvr, e, 0, ch), w1[...]) + nn(wide(kvr, e, 1, ch), w2[...])

                scatter_start(S_DMEM, e, 1, partial_sum)

                @pl.when(e == last)
                def _():
                    pair_grads(4, mid, keys(0), mid, keys(1), None, gst, False)

                dmem = cot_rows(e).astype(f32) + (scatter_end(S_DMEM, e, 1) + rsa[...])
                r2[e] = norm_back(r2[e], 1, dmem)
                gather_start(G_DFFN, fffn, e, r2[e].astype(bf16))
                ffn_contract(e, dg, True)
                scatter_start(S_DFFN, e, 0, ffn_in_part(e, dg))

                @pl.when(e == last)
                def _():
                    ffn_grads(2, fffn, act, gst, False)

                dn = scatter_end(S_DFFN, e, 0) + rsa[...]
                r2[e] += norm_back(h1[e], 2, dn)

                @pl.when(e == last)
                def _():
                    for r in range(2):
                        drain(gst, r)
                    pump(4, gst)
                    ffn_grads(0, ffnf, dg, gst, False)
                    for r in range(2):
                        drain(gst, r)

                self_back(
                    e, 0, own_length(e), dsacc, lambda: pl.when(e == last)(lambda: pump(2, gst))
                )

            loop(ahead)
            dsacc[...] = jnp.zeros_like(dsacc)
            begun()
            loop(back)

        def outer(dsacc, gst):
            pl.run_scoped(lambda act, dg: run(act, dg, dsacc, gst), feed, feed)
            pump(3, gst)
            last_grads(dsacc, gst, lambda: pump(0, gst), True)
            collect((4, 2, 3, 0, 1, 5, 6), 4, gst, True)

        pl.run_scoped(outer, score_sums, grad_stage)

    @pl.when(pipe == 1)
    def _():
        def own_length(e):
            return len_ref[1, side * ex + e]

        def run(act, dg, cq, cctx, clse, gst):
            def first(e):
                self_forward(e, lax.rem(e, 2), own_length(e))
                gather_start(G_MID, mid, e, norm(h1[e], 1))

            def second(e):
                def project(a, ch):
                    cq[e, :, ch] = nt(a, w1[...]).astype(bf16).reshape(2, tb, kc)

                gather_use(G_MID, mid, e, project)

            def third(e):
                cot_copy(e).wait_recv()
                gather_start(G_DFFN, fffn, e, cot_rows(e))

            def there_and_back(e):
                lq, _, sq, _ = block_of(cq, e)
                (lk, _), (lv, _) = pair_of(kvr, e, 0), pair_of(kvr, e, 1)
                lc, _, sc, _ = block_of(cctx, e)
                source_length = len_ref[0, side * ex + e]
                attend(
                    lambda p: pass_copy(e, p).wait_recv(), lq(), lk, lv, source_length, False,
                    sc(), clse,
                )
                r2[e] = h1[e] + scatter(
                    S_MID, e, 1, lambda ch: nn(half_rows(cctx, e, ch, kc), w2[...])
                )
                ffn_expand(e, r2, act, dg, True)
                scatter_start(S_DFFN, e, 0, ffn_in_part(e, dg))
                scatter_send(S_FFN, e, 1, ffn_out_part(e, act)(1 - core))
                dn = scatter_end(S_DFFN, e, 0) + rsa[...]
                h2 = r2[e]
                grad = cot_rows(e).astype(f32) + norm_back(h2, 2, dn)
                rsa[...] = h2
                r2[e] = grad
                gather_start(G_DMID, fmid, e, grad.astype(bf16))
                out = rsa[...] + ffn_out_part(e, act)(core)
                hand_out(0, e, (out + scatter_end(S_FFN, e, 1)).astype(bf16))
                context_grad(G_DMID, fmid, e, w2)
                ldo = block_of(dctx, 0)[0]
                sk, sv = pair_of(kvs, e, 0)[1], pair_of(kvs, e, 1)[1]

                def store_values(p, value):
                    sv(p, value)
                    pass_copy(e, p).start()

                attend_back(
                    lq(), lk, lv, ldo(), lc(), clse, source_length, None, sq(), sk, store_values
                )

                pl.when(e < last)(lambda: finish_cross(e))

            def finish_cross(e):
                dn = scatter(S_DMID, e, 0, lambda ch: nn(half_rows(cq, e, ch, kc), w1[...]))
                r2[e] += norm_back(h1[e], 1, dn)

            loop(first)
            for i in (W_C1, W_C2, W_F2):
                w_on(i)
            for i in (W_C1, W_C2):
                w_done(i)
            w1[...] = w1[...] * jnp.asarray(0.125, bf16)
            loop(second)
            for i in (W_G2, W_F1, W_G1):
                w_on(i)
            loop(third)
            for i in (W_F2, W_G2):
                w_done(i)
            loop(lambda e: ffn_contract(e, dg, False))
            for i in (W_F1, W_G1):
                w_done(i)
            begun()
            loop(there_and_back)
            ffn_grads(2, fffn, act, gst, False)
            ffn_grads(0, ffnf, dg, gst, True)
            lanes = pl.ds(0, kc)
            pair_grads(
                4, mid, lambda: all_rows(cq, lanes), fmid, lambda: all_rows(cctx, lanes),
                0.125, gst, True,
            )
            pump(2, gst)
            finish_cross(last)

        pl.run_scoped(
            run, feed, feed, V((ex, 2, 2, tb, kc), bf16), V((ex, 2, 2, tb, kc), bf16),
            V((2, rows, PAIR), f32), grad_stage,
        )

        def outer(dsacc, gst):
            dsacc[...] = jnp.zeros_like(dsacc)

            def body(e):
                def between():
                    pl.when(e == 0)(lambda: pump(3, gst))
                    pl.when(e == last)(lambda: pump(4, gst))

                self_back(e, 1 - lax.rem(e, 2), own_length(e), dsacc, between)
                pl.when(e < last)(lambda: pump(e, gst))

            loop(body)
            loop(lambda e: pass_all(e, lambda cp: cp.wait_send()))
            last_grads(dsacc, gst, lambda: None, False)
            collect((2, 3, 0, 1, 4, 5, 6), 5, gst, False)

        pl.run_scoped(outer, score_sums, grad_stage)


def run_sections(x, cot, w_in, w_out, c_1, c_2, f_1, f_2, gains, lens, table, hot, direct):
    batch, tb, width = x.shape
    ex = batch // 2
    rows, seq = 2 * tb, 4 * tb
    kq, fq = w_out.shape[0], f_1.shape[1]
    kc, fc = 2 * kq, 2 * fq
    heads = kc // DK
    count = lax.axis_size("dp")
    vmem = pl.BlockSpec(memory_space=pltpu.VMEM)
    hbm = pl.BlockSpec(memory_space=pl.ANY)
    smem = pl.BlockSpec(memory_space=pltpu.SMEM)
    full = (ex, 2, 2, tb)
    units = (7, width, kc)
    V = pltpu.VMEM
    D = pltpu.SemaphoreType.DMA
    S = jax.ShapeDtypeStruct
    scratch = [
        V((3 * kc, width), bf16), V((kc, width), bf16), V((kc, width), bf16), V((kc, width), bf16),
        V((2, width, fq), bf16), V((2, fq, width), bf16), V((heads, seq, seq), bf16),
        V((ex, 2, tb, width), bf16), V((ex, 2, tb, width), bf16),
        V((ex, 2, tb, width), bf16),
        V((*full, width), bf16),
        V((*full, 3 * kc), bf16),
        V((*full, kc), bf16),
        V((ex, 2, rows, PAIR), f32),
        V((ex, rows, width), f32),
        V((*full, width), bf16),
        V((*full, width), bf16),
        V((ex, kc // PAIR, 2, 2, 2, tb, PAIR), bf16),
        V((ex, kc // PAIR, 2, 2, 2, tb, PAIR), bf16),
        V((ex, rows, width), f32),
        V((*full, width), bf16),
        V((*full, width), bf16),
        V((1, 2, 2, tb, kc), bf16),
        V((rows, width), f32),
        V((2, rows, width), bf16),
        V((2, rows, width), bf16),
        V((2, 8, 2 * seq), f32),
        V((16, 2 * seq), f32), V((8, 2 * seq), f32), V((16, 2 * seq), f32),
        V((max(1, count - 1) if direct else 1, 16, 2 * seq), f32),
        D((8 + 2 * ex,)),
        D((2, ex)), D((2, ex)), D((1,)), D((1,)), D((10, 2)), D((10, 2)), D((10,)), D((10,)),
        D((6, ex)), D((6, ex)), D((7, ex)), D((7, ex)), D((ex, kc // PAIR)), D((ex, kc // PAIR)),
        D((2, ex)), D((2, ex)), D((7,)), D((7,)), D((7, 3)), D((7, 3)), D((5,)), D((5,)),
    ]
    slots = count - 1 if direct else 1
    return pl.pallas_call(
        partial(section_kernel, direct=direct),
        out_shape=(
            S((batch, tb, width), bf16),
            S((batch, tb, width), bf16),
            S(units, bf16),
            S((7, slots, width // count if direct else 16, kc), bf16),
            S((7, width // count if direct else 8, kc), f32),
            S((16, 2 * seq), f32),
            S(units, bf16),
            S(units, bf16),
            S(units, bf16),
        ),
        in_specs=[hbm] * 8 + [vmem, smem, vmem, vmem],
        out_specs=(hbm, hbm, hbm, hbm, hbm, vmem, hbm, hbm, hbm),
        scratch_shapes=scratch,
        compiler_params=pltpu.CompilerParams(
            collective_id=0, has_side_effects=True, vmem_limit_bytes=64 * 2**20 - 65536
        ),
        name="sections",
    )(x, cot, w_in, w_out, c_1, c_2, f_1, f_2, gains, lens, table, hot)


def ends_kernel(
    sec, ing, fin_hbm, small, hot_ref,
    o_sec, o_ing, o_in, o_out, o_c1, o_c2, o_f1, o_f2, o_bias, o_gain,
    low_rows, high_rows, out_rows, fin, lsem, ssem,
):
    batch = ing.shape[0]
    whole_in = pltpu.make_async_copy(sec, out_rows, lsem.at[batch])
    whole = pltpu.make_async_copy(out_rows, o_sec.at[0], lsem.at[batch])
    sums_in = pltpu.make_async_copy(fin_hbm, fin, lsem.at[batch + 1])
    loads = [pltpu.make_async_copy(ing.at[e], low_rows.at[e], lsem.at[e]) for e in range(batch)]
    stores = [
        pltpu.make_async_copy(high_rows.at[e], o_ing.at[0, e], ssem.at[e]) for e in range(batch)
    ]
    for cp in loads:
        cp.start()
    sums_in.start()
    whole_in.start()
    for e in range(batch):
        loads[e].wait()
        high_rows[e] = low_rows[e].astype(f32)
        stores[e].start()
    whole_in.wait()
    whole.start()
    sums_in.wait()

    def first(u):
        return jnp.concatenate([fin[u, :, :PAIR], fin[u, :, PAIR : PAIR + DK]], 1)

    def second(u):
        return jnp.concatenate([fin[u, :, 2 * PAIR :], fin[u, :, PAIR + DK : 2 * PAIR]], 1)

    o_in[0, 0], o_in[0, 1], o_in[0, 2] = first(5), second(5), first(6)
    o_out[0] = second(6).T
    o_c1[0], o_c2[0] = first(4), second(4)
    kc = fin.shape[2]
    for i in range(2):
        o_f1[0, :, i * kc : (i + 1) * kc] = fin[i]
        o_f2[0, :, i * kc : (i + 1) * kc] = fin[2 + i]
    sums = small[8:16, :]
    high = sums.astype(bf16)
    rest = sums - high.astype(f32)
    middle = rest.astype(bf16)
    low = (rest - middle.astype(f32)).astype(bf16)
    hot = hot_ref[lax.axis_index("pipe"), lax.axis_index("dp")]
    bias = nt(high, hot) + nt(middle, hot) + nt(low, hot)
    for h in range(o_bias.shape[0]):
        o_bias[h] = bias[h : h + 1]
    share = o_gain.shape[2]
    at = (lax.axis_index("dp") * lax.axis_size("tensor") + lax.axis_index("tensor")) * share
    moved = pltpu.roll(small[0:8, :], lax.rem(small.shape[1] - at, small.shape[1]), 1)
    for i in range(3):
        o_gain[i] = moved[i : i + 1, :share]
    whole.wait()
    for cp in stores:
        cp.wait()


def ends(sec, ing, fin, small, hot, share, heads):
    batch, tb, width = ing.shape
    _, block, kc = fin.shape
    kq = kc // 2
    S = jax.ShapeDtypeStruct
    D = pltpu.SemaphoreType.DMA
    vmem = pl.BlockSpec(memory_space=pltpu.VMEM)
    hbm = pl.BlockSpec(memory_space=pl.ANY)
    return pl.pallas_call(
        ends_kernel,
        out_shape=(
            S((1, batch, tb, width), bf16), S((1, batch, tb, width), f32),
            S((1, 3, block, kq), f32), S((1, kq, block), f32),
            S((1, block, kq), f32), S((1, block, kq), f32), S((1, block, 2 * kc), f32),
            S((1, block, 2 * kc), f32), S((heads, 1, hot.shape[2]), f32), S((3, 1, share), f32),
        ),
        in_specs=[hbm, hbm, hbm, vmem, vmem],
        out_specs=(hbm, hbm) + (vmem,) * 8,
        scratch_shapes=[
            pltpu.VMEM((batch, tb, width), bf16), pltpu.VMEM((batch, tb, width), f32),
            pltpu.VMEM((batch, tb, width), bf16), pltpu.VMEM(fin.shape, f32), D((batch + 2,)), D((batch,)),
        ],
        compiler_params=pltpu.CompilerParams(vmem_limit_bytes=64 * 2**20 - 65536),
        name="ends",
    )(sec, ing, fin, small, hot)


def local(
    section_input, lengths, norm_gain, attn_in, attn_out, cross_first, cross_second,
    ffn_in, ffn_out, rel_bias, out_grad,
):
    enc = lax.axis_index("pipe") == 0
    tb, width = section_input.shape[2:]
    seq = tb * lax.axis_size("tensor")
    kq = attn_out.shape[1]
    data = lax.axis_size("dp")
    at_data = lax.axis_index("dp")
    direct = data <= 4 and (width // data) % 16 == 0
    heads = kq // DK

    offsets = list(range(seq)) + [0] + list(range(-seq + 1, 0))
    both = [np.array(bucket_list(offsets, ways)) for ways in (True, False)]
    hot = np.stack([np.arange(NB)[:, None] == spots[None] for spots in both])
    turned = [seq - 1 - m for m in range(2 * seq)]
    hot_m = np.stack(
        [np.arange(NB)[:, None] == np.array(bucket_list(turned, ways)) for ways in (True, False)]
    )

    def across(w):
        return jnp.swapaxes(w, -1, -2)

    sec, ing, zs, _, fin, small, _, _, _ = run_sections(
        section_input[0], out_grad[0], across(attn_in[0]), attn_out[0], across(cross_first[0]),
        across(cross_second[0]), ffn_in[0], ffn_out[0], jnp.swapaxes(norm_gain, 0, 1),
        lengths.T, rel_bias[0].T, jnp.asarray(hot, bf16), direct,
    )
    share = width // (data * lax.axis_size("tensor"))
    if direct:
        by_data = jnp.asarray(hot_m.reshape(2, data, NB // data, 2 * seq), bf16)
        sec, ing, w_in, w_out, c_1, c_2, f_1, f_2, bias, gains = ends(
            sec, ing, fin, small, by_data, share, heads
        )
        return (
            sec, ing, w_in, w_out, c_1, c_2, f_1, across(f_2),
            jnp.transpose(bias, (1, 2, 0)), jnp.swapaxes(gains, 0, 1),
        )

    packed = zs.reshape(7, data, width // data, 2 * kq)
    shard = lax.psum_scatter(packed, "dp", scatter_dimension=1, tiled=False).astype(f32)
    hot_m = jnp.where(enc, jnp.asarray(hot_m[0], f32), jnp.asarray(hot_m[1], f32))
    bsum = jnp.einsum("bm,hm->bh", hot_m, small[8 : 8 + heads], precision=lax.Precision.HIGHEST)
    bias_grad = lax.psum_scatter(bsum, "dp", scatter_dimension=0, tiled=True)
    gains = lax.psum(small[:3, :width], "dp")
    at = (at_data * lax.axis_size("tensor") + lax.axis_index("tensor")) * share
    gain_grad = lax.dynamic_slice_in_dim(gains, at, share, 1)

    def first_of(u):
        return jnp.concatenate([shard[u, :, :PAIR], shard[u, :, PAIR : PAIR + DK]], 1)

    def second_of(u):
        return jnp.concatenate([shard[u, :, 2 * PAIR :], shard[u, :, PAIR + DK : 2 * PAIR]], 1)

    return (
        sec[None],
        ing[None].astype(f32),
        jnp.stack([first_of(5), second_of(5), first_of(6)])[None],
        second_of(6).T[None],
        first_of(4)[None],
        second_of(4)[None],
        jnp.concatenate([shard[0], shard[1]], 1)[None],
        jnp.concatenate([shard[2], shard[3]], 1).T[None],
        bias_grad[None],
        gain_grad[None],
    )


def solution(mesh):
    placed = (
        P("pipe", "dp", "tensor", None),
        P("dp", None),
        P("pipe", None, None),
        P("pipe", None, None, "tensor"),
        P("pipe", "tensor", None),
        P("pipe", None, "tensor"),
        P("pipe", None, "tensor"),
        P("pipe", None, "tensor"),
        P("pipe", "tensor", None),
        P("pipe", None, "tensor"),
        P("pipe", "dp", "tensor", None),
    )
    return jax.shard_map(
        local,
        mesh=mesh,
        in_specs=placed,
        out_specs=(
            P("pipe", "dp", "tensor", None),
            P("pipe", "dp", "tensor", None),
            P("pipe", None, "dp", "tensor"),
            P("pipe", "tensor", "dp"),
            P("pipe", "dp", "tensor"),
            P("pipe", "dp", "tensor"),
            P("pipe", "dp", "tensor"),
            P("pipe", "tensor", "dp"),
            P("pipe", "dp", "tensor"),
            P("pipe", None, ("dp", "tensor")),
        ),
        check_vma=False,
    )
```

```python
import math
from functools import partial

import jax
import jax.numpy as jnp
import numpy as np
from jax import lax
from jax.experimental import pallas as pl
from jax.experimental.pallas import tpu as pltpu
from jax.sharding import PartitionSpec as P

NB = 32
MAX_DIST = 128
DK = 64
EPS = 1e-06
MASKED = -1000000000.0
MESH = pl.DeviceIdType.MESH
bf16, f32 = jnp.bfloat16, jnp.float32
PAIR = 128
G_IN, G_MID, G_FFN, G_DFFN, G_DMID, G_DATT = range(6)
S_ATT, S_MID, S_FFN, S_DMEM, S_DFFN, S_DMID, S_DIN = range(7)


def bucket_list(offsets, both_ways):
    half = NB // 2 if both_ways else NB
    exact = half // 2
    out = []
    for r in offsets:
        base = half if both_ways and r > 0 else 0
        n = abs(r) if both_ways else max(-r, 0)
        if n < exact:
            out.append(base + n)
        else:
            at = exact + math.floor(
                math.log(n / exact) / math.log(MAX_DIST / exact) * (half - exact)
            )
            out.append(base + min(half - 1, at))
    return out


def nt(a, b):
    return lax.dot_general(a, b, (((1,), (1,)), ((), ())), preferred_element_type=f32)


def nn(a, b):
    return lax.dot_general(a, b, (((1,), (0,)), ((), ())), preferred_element_type=f32)


def tn(a, b):
    return lax.dot_general(a, b, (((0,), (0,)), ((), ())), preferred_element_type=f32)


W_Q, W_K, W_V, W_O, W_C1, W_C2 = range(6)
W_F1, W_F2, WEIGHTS = range(6, 10), range(10, 14), 14


def section_kernel(
    xin, cin, w_in, w_out, c_1, c_2, f_1, f_2, gain_ref, len_ref, table_ref, hot_ref,
    sec_out, ing_out, zs, zr, fin_out, small_out, gown, ysend, yrecv,
    wqkv, wo, w1, w2, wf1, wf2, bias,
    xr, cot, out_rows,
    fin, qkv, ctx, lse, h1, fatt, mid, kvs, kvr,
    r2, ffnf, fffn, dctx, rsa, rss, rsr, diag, small, small_c, small_y, small_z,
    lsem, xs, xg, ts, tg, ys, yg, zps, zpg, gs, gr, ss, sr, ps, pr, os, og, us, ug, vs, vg, ms, mg,
    *, direct,
):
    ex, _, tb, width = xr.shape
    fmid = fatt
    rows = 2 * tb
    kq = wo.shape[0] // 2
    kc = wo.shape[0]
    fq = wf1.shape[2]
    fc = 2 * fq
    seq = 2 * rows
    heads = kc // DK
    pairs = kc // PAIR
    own_heads = heads // 2

    tensor = lax.axis_index("tensor")
    pipe = lax.axis_index("pipe")
    data = lax.axis_index("dp")
    count = lax.axis_size("dp")
    core = lax.rem(tensor, 2)
    side = tensor // 2
    parity = lax.rem(data, 2)
    partner = {"tensor": tensor + 1 - 2 * core}
    peer = {"tensor": lax.rem(tensor + 2, 4)}
    near = {"dp": data + 1 - 2 * parity}
    other = {"pipe": 1 - pipe}

    def away(step):
        return lax.rem(data + step, count)

    barrier = pltpu.get_barrier_semaphore()
    met = [partner, peer, other]
    met += [{"dp": away(i)} for i in range(1, count)] if direct else [near]
    for device in met:
        pl.semaphore_signal(barrier, 1, device_id=device, device_id_type=MESH)

    def remote(src, dst, send, recv, device):
        return pltpu.make_async_remote_copy(
            src, dst, send, recv, device_id=device, device_id_type=MESH
        )

    def own_copies():
        pairs_of = [(w_in.at[i], wqkv.at[pl.ds(i * kc, kq)]) for i in range(3)]
        pairs_of += [(w, home_of.at[pl.ds(0, kq)]) for w, home_of in ((w_out, wo), (c_1, w1), (c_2, w2))]
        pairs_of += [(f_1, wf1.at[0]), (f_2, wf2.at[0])]
        for e in range(ex):
            pairs_of.append((xin.at[side * ex + e], xr.at[e, side]))
        for e in range(ex):
            pairs_of.append((cin.at[side * ex + e], cot.at[e, side]))
        return [pltpu.make_async_copy(p, q, lsem.at[i]) for i, (p, q) in enumerate(pairs_of)]

    def x_copy(e):
        return remote(xin.at[(1 - side) * ex + e], xr.at[e, side], xs.at[0, e], xg.at[0, e], peer)

    def cot_copy(e):
        return remote(cin.at[(1 - side) * ex + e], cot.at[e, side], xs.at[1, e], xg.at[1, e], peer)

    def diag_copy():
        return remote(diag.at[0], diag.at[1], ts.at[0], tg.at[0], peer)

    half_kq, part_fq = kq // 2, wf1.shape[1] // 8

    def rows_at(first, n):
        return pl.ds(pl.multiple_of(first, 16), n)

    def small_ref(i):
        return (wqkv, i * kc + kq) if i < 3 else ((wo, w1, w2)[i - 3], kq)

    def big_rows(i, part):
        return rows_at((2 * ((i - W_F1[0]) % 4) + part) * part_fq, part_fq)

    def home(i, part):
        if i >= W_F1[0]:
            return (wf1, wf2)[(i - W_F1[0]) // 4].at[1, big_rows(i, part)]
        ref, first = small_ref(i)
        return ref.at[rows_at(first + part * half_kq, half_kq)]

    def w_copies(i):
        if i >= W_F1[0]:
            src = (f_1, f_2)[(i - W_F1[0]) // 4].at[big_rows(i, parity)]
            return [remote(src, home(i, parity), ys.at[i, 0], yg.at[i, 0], peer)]
        src = w_in.at[i] if i < 3 else (w_out, c_1, c_2)[i - 3]
        ref, first = small_ref(i)
        long, short = DK, half_kq - DK
        froms = (jnp.where(parity == 0, kq - DK, short), jnp.where(parity == 0, 0, DK + short))
        out = []
        for j, (at, n, skip) in enumerate(((froms[0], long, 0), (froms[1], short, long))):
            dst = ref.at[rows_at(first + parity * half_kq + skip, n)]
            out.append(remote(src.at[rows_at(at, n)], dst, ys.at[i, j], yg.at[i, j], peer))
        return out

    def w_start(order):
        for i in order:
            for cp in w_copies(i):
                cp.start()

    def w_pass(i):
        return remote(home(i, parity), home(i, parity), zps.at[i], zpg.at[i], near)

    def w_on(i):
        for cp in w_copies(i):
            cp.wait_recv()
        w_pass(i).start()

    def w_done(i):
        w_pass(i).wait()

    copies = own_copies()
    for cp in copies:
        cp.start()
    pl.semaphore_wait(barrier, len(met))
    x_copy(0).start()
    w_start((W_Q, W_K, W_V))
    values = nn(table_ref[...], hot_ref[pipe])
    at_m = lax.broadcasted_iota(jnp.int32, (1, 2 * seq), 1)
    hidden = jnp.logical_and(jnp.logical_and(at_m > 0, at_m < seq), pipe == 1)
    diag[0, 0:own_heads] = jnp.where(hidden, MASKED, values)
    diag[0, own_heads:] = jnp.zeros((8 - own_heads, 2 * seq), f32)
    diag_copy().start()
    w_start((W_O,))

    @pl.when(pipe == 0)
    def _():
        w_start((*W_F1, *W_F2, W_C1, W_C2))

    for e in range(1, ex):
        x_copy(e).start()

    @pl.when(pipe == 1)
    def _():
        w_start((W_C1, W_C2, *W_F2, *W_F1))

    for e in range(ex):
        cot_copy(e).start()
    small[...] = jnp.zeros_like(small)
    for cp in copies:
        cp.wait()
    diag_copy().wait()
    local_order = [(0, h) for h in range(own_heads)] + [(1, (h + 2) % 3) for h in range(own_heads)]
    for h, (from_side, at) in enumerate(local_order):
        wide = jnp.broadcast_to(diag[from_side, at : at + 1, :], (seq, 2 * seq))
        bias[h] = pltpu.roll(wide, 0, 1, stride=1, stride_axis=0)[:, :seq].astype(bf16)
    for i in (W_Q, W_K, W_V, W_O):
        w_on(i)
    for i in (W_Q, W_K, W_V):
        w_done(i)
    wqkv[0:kc] = wqkv[0:kc] * jnp.asarray(0.125, bf16)

    lane = lax.broadcasted_iota(jnp.int32, (1, PAIR), 1)
    half_f = [jnp.where(lane // DK == hh, 1.0, 0.0) for hh in range(2)]
    half_b = [m.astype(bf16) for m in half_f]
    key_at = lax.broadcasted_iota(jnp.int32, (1, seq), 1)

    def key_mask(length):
        return jnp.where(key_at < length, 0.0, MASKED)

    def gather_copy(kind, buf, e):
        return remote(
            buf.at[e, :, core], buf.at[e, :, core], gs.at[kind, e], gr.at[kind, e], partner
        )

    def gather_start(kind, buf, e, value):
        buf[e, :, core] = value.reshape(2, tb, width)
        gather_copy(kind, buf, e).start()

    def gather_use(kind, buf, e, fn):
        def body(i, _):
            ch = lax.rem(core + i, 2)

            @pl.when(i == 1)
            def _():
                gather_copy(kind, buf, e).wait()

            fn(buf[e, :, ch].reshape(rows, width), ch)
            return 0

        lax.fori_loop(0, 2, body, 0)

    def scatter_copy(kind, e, slot):
        return remote(rss.at[slot], rsr.at[slot], ss.at[kind, e], sr.at[kind, e], partner)

    def scatter_send(kind, e, slot, value):
        rss[slot] = value.astype(bf16)
        scatter_copy(kind, e, slot).start()

    def scatter_start(kind, e, slot, fn):
        def body(i, _):
            ch = lax.rem(core + 1 + i, 2)
            rsa[...] = fn(ch)

            @pl.when(i == 0)
            def _():
                scatter_send(kind, e, slot, rsa[...])

            return 0

        lax.fori_loop(0, 2, body, 0)

    def scatter_end(kind, e, slot):
        scatter_copy(kind, e, slot).wait()
        return rsr[slot].astype(f32)

    def scatter(kind, e, slot, fn):
        scatter_start(kind, e, slot, fn)
        return scatter_end(kind, e, slot) + rsa[...]

    def norm(v, row):
        inv = lax.rsqrt(jnp.mean(v * v, axis=-1, keepdims=True) + EPS)
        return (v * inv * gain_ref[row]).astype(bf16)

    def norm_back(v, row, grad):
        inv = lax.rsqrt(jnp.mean(v * v, axis=-1, keepdims=True) + EPS)
        unit = v * inv
        small[pl.ds(row, 1), 0:width] += jnp.sum(grad * unit, axis=0, keepdims=True)
        gg = grad * gain_ref[row]
        return inv * (gg - unit * jnp.mean(gg * unit, axis=-1, keepdims=True))

    def attend(ready, load_q, load_k, load_v, length, use_bias, store_ctx, lse_ref):
        mask = key_mask(length)

        def body(p, _):
            ready(p)
            k, v = load_k(p), load_v(p)
            for yb in range(2):
                q = load_q(yb, p)
                total = scale = None
                lse_t = lse_ref[yb]
                for hh in range(2):
                    h = 2 * p + hh
                    s = nt(q * half_b[hh], k) + mask
                    if use_bias:
                        s = s + bias[h, pl.ds(yb * rows, rows), :].astype(f32)
                    top = jnp.max(s, axis=-1, keepdims=True)
                    w = jnp.exp(s - top)
                    den = jnp.sum(w, axis=-1, keepdims=True)
                    part = nn(w.astype(bf16), v * half_b[hh])
                    total = part if total is None else total + part
                    inv = (1.0 / den) * half_f[hh]
                    scale = inv if scale is None else scale + inv
                    lse_t = jnp.where(lane == h, top + jnp.log(den), lse_t)
                store_ctx(yb, p, (total * scale).astype(bf16))
                lse_ref[yb] = lse_t
            return 0

        lax.fori_loop(0, pairs, body, 0)

    def attend_back(
        load_q, load_k, load_v, load_do, load_o, lse_ref, length, dsacc, store_dq, store_dk, store_dv
    ):
        mask = key_mask(length)

        def body(p, _):
            k, v = load_k(p), load_v(p)
            dk = dv = None
            for yb in range(2):
                q, do = load_q(yb, p), load_do(yb, p)
                both = do.astype(f32) * load_o(yb, p).astype(f32)
                lse_t = lse_ref[yb]
                dq = None
                for hh in range(2):
                    h = 2 * p + hh
                    qm, dom = q * half_b[hh], do * half_b[hh]
                    lse_c = jnp.sum(jnp.where(lane == h, lse_t, 0.0), axis=-1, keepdims=True)
                    delta = jnp.sum(both * half_f[hh], axis=-1, keepdims=True)
                    s = nt(qm, k) + mask
                    if dsacc is not None:
                        s = s + bias[h, pl.ds(yb * rows, rows), :].astype(f32)
                    w = jnp.exp(s - lse_c)
                    ds = w * (nt(dom, v) - delta)
                    wb, db = w.astype(bf16), ds.astype(bf16)
                    if dsacc is not None:
                        at = pl.ds(yb * rows, rows)
                        dsacc[h, at, :] = (dsacc[h, at, :].astype(f32) + ds).astype(bf16)
                    dvp, dkp, dqp = tn(wb, dom), tn(db, qm), nn(db, k * half_b[hh])
                    dv = dvp if dv is None else dv + dvp
                    dk = dkp if dk is None else dk + dkp
                    dq = dqp if dq is None else dq + dqp
                store_dq(yb, p, dq.astype(bf16))
            store_dk(p, dk.astype(bf16))
            store_dv(p, dv.astype(bf16))
            return 0

        lax.fori_loop(0, pairs, body, 0)

    def block_of(ref, *at):
        def lanes_at(first, p):
            return pl.ds(pl.multiple_of(first + p * PAIR, PAIR), PAIR)

        def load_rows(first=0):
            return lambda yb, p: ref[(*at, yb, slice(None), slice(None), lanes_at(first, p))].reshape(rows, PAIR)

        def load_all(first=0):
            return lambda p: ref[(*at, slice(None), slice(None), slice(None), lanes_at(first, p))].reshape(seq, PAIR)

        def store_rows(first=0):
            def store(yb, p, value):
                ref[(*at, yb, slice(None), slice(None), lanes_at(first, p))] = value.reshape(2, tb, PAIR)

            return store

        def store_all(first=0):
            def store(p, value):
                ref[(*at, slice(None), slice(None), slice(None), lanes_at(first, p))] = value.reshape(2, 2, tb, PAIR)

            return store

        return load_rows, load_all, store_rows, store_all

    def pair_of(ref, e, i):
        def load(p):
            return ref[e, p, i].reshape(seq, PAIR)

        def store(p, value):
            ref[e, p, i] = value.reshape(2, 2, tb, PAIR)

        return load, store

    def in_rows(e):
        return xr[e].reshape(rows, width).astype(f32)

    def cot_rows(e):
        return cot[e].reshape(rows, width)

    def half_rows(ref, e, ch, count):
        return ref[e, :, ch].reshape(rows, count)

    def self_forward(e, slot, length, middle=None):
        x_copy(e).wait()
        gather_start(G_IN, fin, e, norm(in_rows(e), 0))

        def project(a, ch):
            qkv[e, :, ch] = nt(a, wqkv[...]).astype(bf16).reshape(2, tb, 3 * kc)

        gather_use(G_IN, fin, e, project)
        lr, la, _, _ = block_of(qkv, e)
        _, _, store_ctx, _ = block_of(ctx, e)

        def ready(p):
            pass

        attend(ready, lr(), la(kc), la(2 * kc), length, True, store_ctx(), lse.at[e])

        @pl.when(e == 0)
        def _():
            w_done(W_O)

        if middle is not None:
            middle()

        h1[e] = in_rows(e) + scatter(
            S_ATT, e, slot, lambda ch: nn(half_rows(ctx, e, ch, kc), wo[...])
        )

    def ffn_expand(e, src, act, dg, has_grad):
        gather_start(G_FFN, ffnf, e, norm(src[e], 2))

        def expand(a, ch):
            for i in range(2):
                pre = nn(a, wf1[i])
                sq = pre * pre
                th = jnp.tanh(0.7978845608028654 * pre * (1.0 + 0.044715 * sq))
                gate = 0.5 + 0.5 * th
                slope = gate + (0.5 * 0.7978845608028654) * pre * (1.0 - th * th) * (
                    1.0 + (3 * 0.044715) * sq
                )
                lanes = pl.ds(i * fq, fq)
                act[e, :, ch, :, lanes] = (pre * gate).astype(bf16).reshape(2, tb, fq)
                if has_grad:
                    slope = slope * dg[e, :, ch, :, lanes].reshape(rows, fq).astype(f32)
                dg[e, :, ch, :, lanes] = slope.astype(bf16).reshape(2, tb, fq)

        gather_use(G_FFN, ffnf, e, expand)

    def ffn_out_part(e, act):
        return lambda ch: nn(half_rows(act, e, ch, fc), wf2[...].reshape(fc, width))

    def ffn_in_part(e, dg):
        def part(ch):
            both = half_rows(dg, e, ch, fc)
            return nt(both[:, :fq], wf1[0]) + nt(both[:, fq:], wf1[1])

        return part

    def ffn_contract(e, dg, has_slope):
        def contract(a, ch):
            for i in range(2):
                lanes = pl.ds(i * fq, fq)
                dact = nt(a, wf2[i])
                if has_slope:
                    dact = dact * dg[e, :, ch, :, lanes].reshape(rows, fq).astype(f32)
                dg[e, :, ch, :, lanes] = dact.astype(bf16).reshape(2, tb, fq)

        gather_use(G_DFFN, fffn, e, contract)

    def context_grad(kind, buf, e, w):
        def project(a, ch):
            dctx[0, :, ch] = nt(a, w[...]).astype(bf16).reshape(2, tb, kc)

        gather_use(kind, buf, e, project)

    def self_back(e, slot, length, dsacc, between=None):
        gather_start(G_DATT, fatt, e, r2[e].astype(bf16))
        context_grad(G_DATT, fatt, e, wo)
        if between is not None:
            between()
        lr, la, sr_, sa_ = block_of(qkv, e)
        ldo = block_of(dctx, 0)[0]
        lo = block_of(ctx, e)[0]
        attend_back(
            lr(), la(kc), la(2 * kc), ldo(), lo(), lse.at[e], length, dsacc,
            sr_(), sa_(kc), sa_(2 * kc),
        )
        dn = scatter(S_DIN, e, slot, lambda ch: nn(half_rows(qkv, e, ch, 3 * kc), wqkv[...]))
        hand_out(1, e, (r2[e] + norm_back(in_rows(e), 0, dn)).astype(bf16), e == ex - 1)

    def out_copies(kind, e):
        at, out = side * ex + e, (sec_out, ing_out)[kind]
        return (
            pltpu.make_async_copy(out_rows.at[e, side], out.at[at], lsem.at[8 + kind * ex + e]),
            remote(out_rows.at[e, 1 - side], out.at[at], os.at[kind, e], og.at[kind, e], peer),
        )

    def hand_out(kind, e, value, later=False):
        if kind == 1:
            for cp in out_copies(0, e):
                cp.wait()
        out_rows[e] = value.reshape(2, tb, width)

        def start():
            for cp in out_copies(kind, e):
                cp.start()

        pl.when(jnp.logical_not(later))(start)

    def pass_copy(e, p):
        return remote(kvs.at[e, p], kvr.at[e, p], ps.at[e, p], pr.at[e, p], other)

    def y_copy(u):
        return remote(ysend.at[u], yrecv.at[u], us.at[u], ug.at[u], peer)

    def all_rows(ref, lanes):
        n = lanes.size
        return ref[:, :, :, :, lanes].reshape(ex * seq, n)

    half = width // 2

    def lanes_of(r):
        return pl.ds(pl.multiple_of(r * half, PAIR), half)

    def stage_copy(gst, r, i, dst, u):
        return pltpu.make_async_copy(
            gst.at[r, :, pl.ds(i * kc, kc)], dst.at[u, lanes_of(r)], lsem.at[2 * r + i]
        )

    def drain(gst, r):
        for i in range(2):
            stage_copy(gst, r, i, gown, 0).wait()

    def ffn_grads(u, src, feed_ref, gst, pending):
        def to(dst, first, wait, sent):
            def body(r, _):
                if wait:
                    drain(gst, r)
                if sent:

                    @pl.when(r == 1)
                    def _():
                        for i in range(2):
                            y_copy(u + i).start()

                rhs = all_rows(feed_ref, pl.ds(first, fq))
                gst[r] = tn(all_rows(src, lanes_of(r)), rhs).astype(bf16)
                for i in range(2):
                    stage_copy(gst, r, i, dst, u + i).start()
                return 0

            lax.fori_loop(0, 2, body, 0)

        to(ysend, fq, pending, False)
        to(gown, 0, True, True)

    def pair_grads(u, lhs_a, load_a, lhs_b, load_b, scale, gst, pending):
        def body(r, _):
            if pending:
                drain(gst, r)
            a = tn(all_rows(lhs_a, lanes_of(r)), load_a())
            if scale is not None:
                a = a * scale
            b = tn(all_rows(lhs_b, lanes_of(r)), load_b())
            low = lane < DK
            a1, b1 = a[:, PAIR : 2 * PAIR], b[:, PAIR : 2 * PAIR]
            mix_own = jnp.where(low, a1, pltpu.roll(b1, DK, 1))
            mix_peer = jnp.where(low, pltpu.roll(a1, DK, 1), b1)
            for j, part in enumerate(
                (a[:, :PAIR], mix_own, b[:, :PAIR], a[:, 2 * PAIR :], mix_peer, b[:, 2 * PAIR :])
            ):
                gst[r, :, j * PAIR : (j + 1) * PAIR] = part.astype(bf16)
            for i, dst in enumerate((gown, ysend)):
                stage_copy(gst, r, i, dst, u).start()
            return 0

        lax.fori_loop(0, 2, body, 0)
        for r in range(2):
            drain(gst, r)
        y_copy(u).start()

    def z_copy(u, step):
        block = width // count
        at = away(step)
        return remote(
            zs.at[u, pl.ds(pl.multiple_of(at * block, 16), block)], zr.at[u, step - 1],
            vs.at[u, step - 1], vg.at[u, step - 1], {"dp": at},
        )

    def pump(u, gst):
        y_copy(u).wait_recv()
        loads, stores = [], []
        for r in range(2):
            own, came = gst.at[r, :, pl.ds(0, kc)], gst.at[r, :, pl.ds(kc, kc)]
            loads.append(pltpu.make_async_copy(gown.at[u, lanes_of(r)], own, lsem.at[4 + r]))
            loads.append(pltpu.make_async_copy(yrecv.at[u, lanes_of(r)], came, lsem.at[6 + r]))
            stores.append(pltpu.make_async_copy(own, zs.at[u, lanes_of(r)], lsem.at[4 + r]))
        for cp in loads:
            cp.start()
        for r in range(2):
            for cp in loads[2 * r : 2 * r + 2]:
                cp.wait()
            gst[r, :, 0:kc] = (
                gst[r, :, 0:kc].astype(f32) + gst[r, :, kc : 2 * kc].astype(f32)
            ).astype(bf16)
            stores[r].start()
        for cp in stores:
            cp.wait()
        if direct:
            for step in range(1, count):
                z_copy(u, step).start()

    def finish(u, va, vf):
        block = width // count
        for step in range(1, count):
            z_copy(u, step).wait()
        mine = pl.ds(pl.multiple_of(data * block, 16), block)
        cps = [pltpu.make_async_copy(zs.at[u, mine], va.at[pl.ds(0, block)], lsem.at[0])]
        for step in range(1, count):
            cps.append(
                pltpu.make_async_copy(
                    zr.at[u, step - 1], va.at[pl.ds(step * block, block)], lsem.at[step]
                )
            )
        for cp in cps:
            cp.start()
        for cp in cps:
            cp.wait()
        total = va[0:block].astype(f32)
        for step in range(1, count):
            total = total + va[step * block : (step + 1) * block].astype(f32)
        vf[...] = total
        cp = pltpu.make_async_copy(vf, fin_out.at[u], lsem.at[0])
        cp.start()
        cp.wait()

    def small_near():
        first = remote(small.at[pl.ds(0, 8)], small_c, ms.at[0], mg.at[0], partner)
        first.start()
        first.wait()
        small[0:8] += small_c[...]
        small_peer().start()

    def small_peer():
        return remote(small, small_y, ms.at[1], mg.at[1], peer)

    def small_far():
        return [
            remote(small, small_z.at[i - 1], ms.at[1 + i], mg.at[1 + i], {"dp": away(i)})
            for i in range(1, count)
        ]

    def small_middle():
        small_peer().wait()
        small[0:8] += small_y[0:8]
        for h in range(own_heads):
            at = 8 + own_heads + (h + 1) % 3
            small[8 + h : 9 + h] += small_y[at : at + 1]
        if direct:
            for cp in small_far():
                cp.start()

    def small_end():
        total = small[...]
        if direct:
            for cp in small_far():
                cp.wait()
            for i in range(1, count):
                total = total + small_z[i - 1]
        small_out[...] = total

    def bias_grads(dsacc):
        at_r = lax.broadcasted_iota(jnp.int32, (seq, seq), 0)
        at_c = lax.broadcasted_iota(jnp.int32, (seq, seq), 1)
        flip = jnp.where(at_r + at_c == seq - 1, 1.0, 0.0).astype(bf16)

        def body(h, _):
            reverse = nn(dsacc[h], flip)
            wide = jnp.concatenate([reverse, jnp.zeros((seq, seq), f32)], axis=1)
            wide = pltpu.roll(wide, 0, 1, stride=1, stride_axis=0)
            small[pl.ds(8 + h, 1), :] = jnp.sum(wide, axis=0, keepdims=True)
            return 0

        lax.fori_loop(0, heads, body, 0)

    def loop(fn):
        def body(e, _):
            fn(e)
            return 0

        lax.fori_loop(0, ex, body, 0)

    def last_grads(dsacc, gst, between, small_first):
        def small_now():
            bias_grads(dsacc)
            small_near()

        lanes = [pl.ds(i * kc, kc) for i in range(3)]
        if small_first:
            small_now()
            between()
        pair_grads(
            5, fin, lambda: all_rows(qkv, lanes[0]), fin, lambda: all_rows(qkv, lanes[1]),
            0.125, gst, False,
        )
        pair_grads(
            6, fin, lambda: all_rows(qkv, lanes[2]), fatt, lambda: all_rows(ctx, lanes[0]),
            None, gst, False,
        )
        if not small_first:
            between()
            small_now()
        for cp in out_copies(1, ex - 1):
            cp.start()

    def collect(order, done, gst, small_first):
        def run(va, vf):
            n = len(order)
            ended = 0
            for k in range(done, n):
                if direct:
                    while ended <= k - 3:
                        finish(order[ended], va, vf)
                        ended += 1
                if k == n - 1 and small_first:
                    small_middle()
                pump(order[k], gst)
            if not small_first:
                small_middle()
            if direct:
                while ended < n:
                    finish(order[ended], va, vf)
                    ended += 1
            small_end()
            for u in order:
                y_copy(u).wait_send()
            for e in range(ex):
                for cp in out_copies(1, e):
                    cp.wait()

        V = pltpu.VMEM
        pl.run_scoped(run, V((width, kc), bf16), V((width // count, kc), f32))

    def begun():
        for i in range(WEIGHTS):
            for cp in w_copies(i):
                cp.wait_send()
        for e in range(ex):
            cot_copy(e).wait_send()

    V = pltpu.VMEM
    feed = V((ex, 2, 2, tb, fc), bf16)
    grad_stage = V((2, half, 2 * kc), bf16)
    score_sums = V((heads, seq, seq), bf16)
    last = ex - 1

    def pass_all(e, fn):
        for p in range(pairs):
            fn(pass_copy(e, p))

    def wide(ref, e, i, ch):
        return jnp.concatenate([ref[e, p, i, :, ch].reshape(rows, PAIR) for p in range(pairs)], 1)

    @pl.when(pipe == 0)
    def _():
        def own_length(e):
            return len_ref[0, side * ex + e]

        def keys(i):
            return lambda: jnp.concatenate(
                [kvr[:, p, i].reshape(ex * seq, PAIR) for p in range(pairs)], 1
            )

        def run(act, dg, dsacc, gst):
            def ahead(e):
                def middle():
                    pl.when(e == 0)(lambda: w_on(W_F1[0]))

                self_forward(e, 0, own_length(e), middle)

                @pl.when(e == 0)
                def _():
                    for i in (*W_F1[1:], *W_F2[:2]):
                        w_on(i)
                    for i in W_F1:
                        w_done(i)

                ffn_expand(e, h1, act, dg, False)

                @pl.when(e == 0)
                def _():
                    for i in W_F2[2:]:
                        w_on(i)
                    for i in W_F2:
                        w_done(i)
                    for i in (W_C1, W_C2):
                        w_on(i)

                r2[e] = h1[e] + scatter(S_FFN, e, 1, ffn_out_part(e, act))
                memory = norm(r2[e], 1)
                gather_start(G_MID, mid, e, memory)
                hand_out(0, e, memory)

                @pl.when(e == 0)
                def _():
                    for i in (W_C1, W_C2):
                        w_done(i)

                def project(a, ch):
                    for i, w in enumerate((w1, w2)):
                        out = nt(a, w[...]).astype(bf16)
                        for p in range(pairs):
                            kvs[e, p, i, :, ch] = out[:, p * PAIR : (p + 1) * PAIR].reshape(
                                2, tb, PAIR
                            )

                gather_use(G_MID, mid, e, project)
                pass_all(e, lambda cp: cp.start())

            def back(e):
                pass_all(e, lambda cp: cp.wait())
                cot_copy(e).wait_recv()

                def partial_sum(ch):
                    return nn(wide(kvr, e, 0, ch), w1[...]) + nn(wide(kvr, e, 1, ch), w2[...])

                scatter_start(S_DMEM, e, 1, partial_sum)

                @pl.when(e == last)
                def _():
                    pair_grads(4, mid, keys(0), mid, keys(1), None, gst, False)

                dmem = cot_rows(e).astype(f32) + (scatter_end(S_DMEM, e, 1) + rsa[...])
                r2[e] = norm_back(r2[e], 1, dmem)
                gather_start(G_DFFN, fffn, e, r2[e].astype(bf16))
                ffn_contract(e, dg, True)
                scatter_start(S_DFFN, e, 0, ffn_in_part(e, dg))

                @pl.when(e == last)
                def _():
                    ffn_grads(2, fffn, act, gst, False)

                dn = scatter_end(S_DFFN, e, 0) + rsa[...]
                r2[e] += norm_back(h1[e], 2, dn)

                @pl.when(e == last)
                def _():
                    for r in range(2):
                        drain(gst, r)
                    pump(4, gst)
                    ffn_grads(0, ffnf, dg, gst, False)
                    for r in range(2):
                        drain(gst, r)

                self_back(
                    e, 0, own_length(e), dsacc, lambda: pl.when(e == last)(lambda: pump(2, gst))
                )

            loop(ahead)
            dsacc[...] = jnp.zeros_like(dsacc)
            begun()
            loop(back)

        def outer(dsacc, gst):
            pl.run_scoped(lambda act, dg: run(act, dg, dsacc, gst), feed, feed)
            pump(3, gst)
            last_grads(dsacc, gst, lambda: pump(0, gst), True)
            collect((4, 2, 3, 0, 1, 5, 6), 4, gst, True)

        pl.run_scoped(outer, score_sums, grad_stage)

    @pl.when(pipe == 1)
    def _():
        def own_length(e):
            return len_ref[1, side * ex + e]

        def run(act, dg, cq, cctx, clse, gst):
            def first(e):
                self_forward(e, lax.rem(e, 2), own_length(e))
                gather_start(G_MID, mid, e, norm(h1[e], 1))

            def second(e):
                def project(a, ch):
                    cq[e, :, ch] = nt(a, w1[...]).astype(bf16).reshape(2, tb, kc)

                gather_use(G_MID, mid, e, project)

            def third(e):
                cot_copy(e).wait_recv()
                gather_start(G_DFFN, fffn, e, cot_rows(e))

            def there_and_back(e):
                lq, _, sq, _ = block_of(cq, e)
                (lk, _), (lv, _) = pair_of(kvr, e, 0), pair_of(kvr, e, 1)
                lc, _, sc, _ = block_of(cctx, e)
                source_length = len_ref[0, side * ex + e]
                attend(
                    lambda p: pass_copy(e, p).wait_recv(), lq(), lk, lv, source_length, False,
                    sc(), clse,
                )
                r2[e] = h1[e] + scatter(
                    S_MID, e, 1, lambda ch: nn(half_rows(cctx, e, ch, kc), w2[...])
                )
                ffn_expand(e, r2, act, dg, True)
                scatter_start(S_DFFN, e, 0, ffn_in_part(e, dg))
                scatter_send(S_FFN, e, 2, ffn_out_part(e, act)(1 - core))
                dn = scatter_end(S_DFFN, e, 0) + rsa[...]
                h2 = r2[e]
                grad = cot_rows(e).astype(f32) + norm_back(h2, 2, dn)
                rsa[...] = h2
                r2[e] = grad
                gather_start(G_DMID, fmid, e, grad.astype(bf16))
                out = rsa[...] + ffn_out_part(e, act)(core)
                hand_out(0, e, (out + scatter_end(S_FFN, e, 2)).astype(bf16))
                context_grad(G_DMID, fmid, e, w2)
                ldo = block_of(dctx, 0)[0]
                sk, sv = pair_of(kvs, e, 0)[1], pair_of(kvs, e, 1)[1]

                def store_values(p, value):
                    sv(p, value)
                    pass_copy(e, p).start()

                attend_back(
                    lq(), lk, lv, ldo(), lc(), clse, source_length, None, sq(), sk, store_values
                )


            def finish_cross(e):
                dn = scatter(S_DMID, e, lax.rem(e, 2), lambda ch: nn(half_rows(cq, e, ch, kc), w1[...]))
                r2[e] += norm_back(h1[e], 1, dn)

            loop(first)
            for i in (W_C1, W_C2, *W_F2[:2]):
                w_on(i)
            for i in (W_C1, W_C2):
                w_done(i)
            w1[...] = w1[...] * jnp.asarray(0.125, bf16)
            loop(second)
            for i in (*W_F2[2:], *W_F1):
                w_on(i)
            loop(third)
            for i in W_F2:
                w_done(i)
            loop(lambda e: ffn_contract(e, dg, False))
            for i in W_F1:
                w_done(i)
            begun()
            loop(there_and_back)
            ffn_grads(2, fffn, act, gst, False)
            ffn_grads(0, ffnf, dg, gst, True)
            lanes = pl.ds(0, kc)
            pair_grads(
                4, mid, lambda: all_rows(cq, lanes), fmid, lambda: all_rows(cctx, lanes),
                0.125, gst, True,
            )
            pump(2, gst)
            loop(finish_cross)

        pl.run_scoped(
            run, feed, feed, V((ex, 2, 2, tb, kc), bf16), V((ex, 2, 2, tb, kc), bf16),
            V((2, rows, PAIR), f32), grad_stage,
        )

        def outer(dsacc, gst):
            dsacc[...] = jnp.zeros_like(dsacc)

            def body(e):
                def between():
                    pl.when(e == 0)(lambda: pump(3, gst))
                    pl.when(e == last)(lambda: pump(4, gst))

                self_back(e, 1 - lax.rem(e, 2), own_length(e), dsacc, between)
                pl.when(e < last)(lambda: pump(e, gst))

            loop(body)
            loop(lambda e: pass_all(e, lambda cp: cp.wait_send()))
            last_grads(dsacc, gst, lambda: None, False)
            collect((2, 3, 0, 1, 4, 5, 6), 5, gst, False)

        pl.run_scoped(outer, score_sums, grad_stage)


def run_sections(x, cot, w_in, w_out, c_1, c_2, f_1, f_2, gains, lens, table, hot, direct):
    batch, tb, width = x.shape
    ex = batch // 2
    rows, seq = 2 * tb, 4 * tb
    kq, fq = w_out.shape[0], f_1.shape[1]
    kc, fc = 2 * kq, 2 * fq
    heads = kc // DK
    count = lax.axis_size("dp")
    vmem = pl.BlockSpec(memory_space=pltpu.VMEM)
    hbm = pl.BlockSpec(memory_space=pl.ANY)
    smem = pl.BlockSpec(memory_space=pltpu.SMEM)
    full = (ex, 2, 2, tb)
    units = (7, width, kc)
    V = pltpu.VMEM
    D = pltpu.SemaphoreType.DMA
    S = jax.ShapeDtypeStruct
    scratch = [
        V((3 * kc, width), bf16), V((kc, width), bf16), V((kc, width), bf16), V((kc, width), bf16),
        V((2, width, fq), bf16), V((2, fq, width), bf16), V((heads, seq, seq), bf16),
        V((ex, 2, tb, width), bf16), V((ex, 2, tb, width), bf16),
        V((ex, 2, tb, width), bf16),
        V((*full, width), bf16),
        V((*full, 3 * kc), bf16),
        V((*full, kc), bf16),
        V((ex, 2, rows, PAIR), f32),
        V((ex, rows, width), f32),
        V((*full, width), bf16),
        V((*full, width), bf16),
        V((ex, kc // PAIR, 2, 2, 2, tb, PAIR), bf16),
        V((ex, kc // PAIR, 2, 2, 2, tb, PAIR), bf16),
        V((ex, rows, width), f32),
        V((*full, width), bf16),
        V((*full, width), bf16),
        V((1, 2, 2, tb, kc), bf16),
        V((rows, width), f32),
        V((3, rows, width), bf16),
        V((3, rows, width), bf16),
        V((2, 8, 2 * seq), f32),
        V((16, 2 * seq), f32), V((8, 2 * seq), f32), V((16, 2 * seq), f32),
        V((max(1, count - 1) if direct else 1, 16, 2 * seq), f32),
        D((8 + 2 * ex,)),
        D((2, ex)), D((2, ex)), D((1,)), D((1,)), D((WEIGHTS, 2)), D((WEIGHTS, 2)), D((WEIGHTS,)), D((WEIGHTS,)),
        D((6, ex)), D((6, ex)), D((7, ex)), D((7, ex)), D((ex, kc // PAIR)), D((ex, kc // PAIR)),
        D((2, ex)), D((2, ex)), D((7,)), D((7,)), D((7, 3)), D((7, 3)), D((5,)), D((5,)),
    ]
    slots = count - 1 if direct else 1
    return pl.pallas_call(
        partial(section_kernel, direct=direct),
        out_shape=(
            S((batch, tb, width), bf16),
            S((batch, tb, width), bf16),
            S(units, bf16),
            S((7, slots, width // count if direct else 16, kc), bf16),
            S((7, width // count if direct else 8, kc), f32),
            S((16, 2 * seq), f32),
            S(units, bf16),
            S(units, bf16),
            S(units, bf16),
        ),
        in_specs=[hbm] * 8 + [vmem, smem, vmem, vmem],
        out_specs=(hbm, hbm, hbm, hbm, hbm, vmem, hbm, hbm, hbm),
        scratch_shapes=scratch,
        compiler_params=pltpu.CompilerParams(
            collective_id=0, has_side_effects=True, vmem_limit_bytes=64 * 2**20 - 65536
        ),
        name="sections",
    )(x, cot, w_in, w_out, c_1, c_2, f_1, f_2, gains, lens, table, hot)


def ends_kernel(
    sec, ing, fin_hbm, small, hot_ref,
    o_sec, o_ing, o_in, o_out, o_c1, o_c2, o_f1, o_f2, o_bias, o_gain,
    low_rows, high_rows, out_rows, fin, lsem, ssem,
):
    batch = ing.shape[0]
    whole_in = pltpu.make_async_copy(sec, out_rows, lsem.at[batch])
    whole = pltpu.make_async_copy(out_rows, o_sec.at[0], lsem.at[batch])
    sums_in = pltpu.make_async_copy(fin_hbm, fin, lsem.at[batch + 1])
    loads = [pltpu.make_async_copy(ing.at[e], low_rows.at[e], lsem.at[e]) for e in range(batch)]
    stores = [
        pltpu.make_async_copy(high_rows.at[e], o_ing.at[0, e], ssem.at[e]) for e in range(batch)
    ]
    for cp in loads:
        cp.start()
    sums_in.start()
    whole_in.start()
    for e in range(batch):
        loads[e].wait()
        high_rows[e] = low_rows[e].astype(f32)
        stores[e].start()
    whole_in.wait()
    whole.start()
    sums_in.wait()

    def first(u):
        return jnp.concatenate([fin[u, :, :PAIR], fin[u, :, PAIR : PAIR + DK]], 1)

    def second(u):
        return jnp.concatenate([fin[u, :, 2 * PAIR :], fin[u, :, PAIR + DK : 2 * PAIR]], 1)

    o_in[0, 0], o_in[0, 1], o_in[0, 2] = first(5), second(5), first(6)
    o_out[0] = second(6).T
    o_c1[0], o_c2[0] = first(4), second(4)
    kc = fin.shape[2]
    for i in range(2):
        o_f1[0, :, i * kc : (i + 1) * kc] = fin[i]
        o_f2[0, :, i * kc : (i + 1) * kc] = fin[2 + i]
    sums = small[8:16, :]
    high = sums.astype(bf16)
    rest = sums - high.astype(f32)
    middle = rest.astype(bf16)
    low = (rest - middle.astype(f32)).astype(bf16)
    hot = hot_ref[lax.axis_index("pipe"), lax.axis_index("dp")]
    bias = nt(high, hot) + nt(middle, hot) + nt(low, hot)
    for h in range(o_bias.shape[0]):
        o_bias[h] = bias[h : h + 1]
    share = o_gain.shape[2]
    at = (lax.axis_index("dp") * lax.axis_size("tensor") + lax.axis_index("tensor")) * share
    moved = pltpu.roll(small[0:8, :], lax.rem(small.shape[1] - at, small.shape[1]), 1)
    for i in range(3):
        o_gain[i] = moved[i : i + 1, :share]
    whole.wait()
    for cp in stores:
        cp.wait()


def ends(sec, ing, fin, small, hot, share, heads):
    batch, tb, width = ing.shape
    _, block, kc = fin.shape
    kq = kc // 2
    S = jax.ShapeDtypeStruct
    D = pltpu.SemaphoreType.DMA
    vmem = pl.BlockSpec(memory_space=pltpu.VMEM)
    hbm = pl.BlockSpec(memory_space=pl.ANY)
    return pl.pallas_call(
        ends_kernel,
        out_shape=(
            S((1, batch, tb, width), bf16), S((1, batch, tb, width), f32),
            S((1, 3, block, kq), f32), S((1, kq, block), f32),
            S((1, block, kq), f32), S((1, block, kq), f32), S((1, block, 2 * kc), f32),
            S((1, block, 2 * kc), f32), S((heads, 1, hot.shape[2]), f32), S((3, 1, share), f32),
        ),
        in_specs=[hbm, hbm, hbm, vmem, vmem],
        out_specs=(hbm, hbm) + (vmem,) * 8,
        scratch_shapes=[
            pltpu.VMEM((batch, tb, width), bf16), pltpu.VMEM((batch, tb, width), f32),
            pltpu.VMEM((batch, tb, width), bf16), pltpu.VMEM(fin.shape, f32), D((batch + 2,)), D((batch,)),
        ],
        compiler_params=pltpu.CompilerParams(vmem_limit_bytes=64 * 2**20 - 65536),
        name="ends",
    )(sec, ing, fin, small, hot)


def local(
    section_input, lengths, norm_gain, attn_in, attn_out, cross_first, cross_second,
    ffn_in, ffn_out, rel_bias, out_grad,
):
    enc = lax.axis_index("pipe") == 0
    tb, width = section_input.shape[2:]
    seq = tb * lax.axis_size("tensor")
    kq = attn_out.shape[1]
    data = lax.axis_size("dp")
    at_data = lax.axis_index("dp")
    direct = data <= 4 and (width // data) % 16 == 0
    heads = kq // DK

    offsets = list(range(seq)) + [0] + list(range(-seq + 1, 0))
    both = [np.array(bucket_list(offsets, ways)) for ways in (True, False)]
    hot = np.stack([np.arange(NB)[:, None] == spots[None] for spots in both])
    turned = [seq - 1 - m for m in range(2 * seq)]
    hot_m = np.stack(
        [np.arange(NB)[:, None] == np.array(bucket_list(turned, ways)) for ways in (True, False)]
    )

    def across(w):
        return jnp.swapaxes(w, -1, -2)

    sec, ing, zs, _, fin, small, _, _, _ = run_sections(
        section_input[0], out_grad[0], across(attn_in[0]), attn_out[0], across(cross_first[0]),
        across(cross_second[0]), ffn_in[0], ffn_out[0], jnp.swapaxes(norm_gain, 0, 1),
        lengths.T, rel_bias[0].T, jnp.asarray(hot, bf16), direct,
    )
    share = width // (data * lax.axis_size("tensor"))
    if direct:
        by_data = jnp.asarray(hot_m.reshape(2, data, NB // data, 2 * seq), bf16)
        sec, ing, w_in, w_out, c_1, c_2, f_1, f_2, bias, gains = ends(
            sec, ing, fin, small, by_data, share, heads
        )
        return (
            sec, ing, w_in, w_out, c_1, c_2, f_1, across(f_2),
            jnp.transpose(bias, (1, 2, 0)), jnp.swapaxes(gains, 0, 1),
        )

    packed = zs.reshape(7, data, width // data, 2 * kq)
    shard = lax.psum_scatter(packed, "dp", scatter_dimension=1, tiled=False).astype(f32)
    hot_m = jnp.where(enc, jnp.asarray(hot_m[0], f32), jnp.asarray(hot_m[1], f32))
    bsum = jnp.einsum("bm,hm->bh", hot_m, small[8 : 8 + heads], precision=lax.Precision.HIGHEST)
    bias_grad = lax.psum_scatter(bsum, "dp", scatter_dimension=0, tiled=True)
    gains = lax.psum(small[:3, :width], "dp")
    at = (at_data * lax.axis_size("tensor") + lax.axis_index("tensor")) * share
    gain_grad = lax.dynamic_slice_in_dim(gains, at, share, 1)

    def first_of(u):
        return jnp.concatenate([shard[u, :, :PAIR], shard[u, :, PAIR : PAIR + DK]], 1)

    def second_of(u):
        return jnp.concatenate([shard[u, :, 2 * PAIR :], shard[u, :, PAIR + DK : 2 * PAIR]], 1)

    return (
        sec[None],
        ing[None].astype(f32),
        jnp.stack([first_of(5), second_of(5), first_of(6)])[None],
        second_of(6).T[None],
        first_of(4)[None],
        second_of(4)[None],
        jnp.concatenate([shard[0], shard[1]], 1)[None],
        jnp.concatenate([shard[2], shard[3]], 1).T[None],
        bias_grad[None],
        gain_grad[None],
    )


def solution(mesh):
    placed = (
        P("pipe", "dp", "tensor", None),
        P("dp", None),
        P("pipe", None, None),
        P("pipe", None, None, "tensor"),
        P("pipe", "tensor", None),
        P("pipe", None, "tensor"),
        P("pipe", None, "tensor"),
        P("pipe", None, "tensor"),
        P("pipe", "tensor", None),
        P("pipe", None, "tensor"),
        P("pipe", "dp", "tensor", None),
    )
    return jax.shard_map(
        local,
        mesh=mesh,
        in_specs=placed,
        out_specs=(
            P("pipe", "dp", "tensor", None),
            P("pipe", "dp", "tensor", None),
            P("pipe", None, "dp", "tensor"),
            P("pipe", "tensor", "dp"),
            P("pipe", "dp", "tensor"),
            P("pipe", "dp", "tensor"),
            P("pipe", "dp", "tensor"),
            P("pipe", "tensor", "dp"),
            P("pipe", "dp", "tensor"),
            P("pipe", None, ("dp", "tensor")),
        ),
        check_vma=False,
    )
```

```python
import math
from functools import partial

import jax
import jax.numpy as jnp
import numpy as np
from jax import lax
from jax.experimental import pallas as pl
from jax.experimental.pallas import tpu as pltpu
from jax.sharding import PartitionSpec as P

NB = 32
MAX_DIST = 128
DK = 64
EPS = 1e-06
MASKED = -1000000000.0
MESH = pl.DeviceIdType.MESH
bf16, f32 = jnp.bfloat16, jnp.float32
PAIR = 128
G_IN, G_MID, G_FFN, G_DFFN, G_DMID, G_DATT = range(6)
S_ATT, S_MID, S_FFN, S_DMEM, S_DFFN, S_DMID, S_DIN = range(7)


def bucket_list(offsets, both_ways):
    half = NB // 2 if both_ways else NB
    exact = half // 2
    out = []
    for r in offsets:
        base = half if both_ways and r > 0 else 0
        n = abs(r) if both_ways else max(-r, 0)
        if n < exact:
            out.append(base + n)
        else:
            at = exact + math.floor(
                math.log(n / exact) / math.log(MAX_DIST / exact) * (half - exact)
            )
            out.append(base + min(half - 1, at))
    return out


def nt(a, b):
    return lax.dot_general(a, b, (((1,), (1,)), ((), ())), preferred_element_type=f32)


def nn(a, b):
    return lax.dot_general(a, b, (((1,), (0,)), ((), ())), preferred_element_type=f32)


def tn(a, b):
    return lax.dot_general(a, b, (((0,), (0,)), ((), ())), preferred_element_type=f32)


W_Q, W_K, W_V, W_O, W_C1, W_C2 = range(6)
W_F1, W_F2, WEIGHTS = range(6, 10), range(10, 14), 14


def section_kernel(
    xin, cin, w_in, w_out, c_1, c_2, f_1, f_2, gain_ref, len_ref, table_ref, hot_ref,
    sec_out, ing_out, zs, zr, fin_out, small_out, gown, ysend, yrecv,
    wqkv, wo, w1, w2, wf1, wf2, bias,
    xr, cot, out_rows,
    fin, qkv, ctx, lse, h1, fatt, mid, kvs, kvr,
    r2, ffnf, fffn, dctx, rsa, rss, rsr, diag, small, small_c, small_y, small_z,
    lsem, xs, xg, ts, tg, ys, yg, zps, zpg, gs, gr, ss, sr, ps, pr, os, og, us, ug, vs, vg, ms, mg,
    *, direct,
):
    ex, _, tb, width = xr.shape
    fmid = fatt
    rows = 2 * tb
    kq = wo.shape[0] // 2
    kc = wo.shape[0]
    fq = wf1.shape[2]
    fc = 2 * fq
    seq = 2 * rows
    heads = kc // DK
    pairs = kc // PAIR
    own_heads = heads // 2

    tensor = lax.axis_index("tensor")
    pipe = lax.axis_index("pipe")
    data = lax.axis_index("dp")
    count = lax.axis_size("dp")
    core = lax.rem(tensor, 2)
    side = tensor // 2
    parity = lax.rem(data, 2)
    partner = {"tensor": tensor + 1 - 2 * core}
    peer = {"tensor": lax.rem(tensor + 2, 4)}
    near = {"dp": data + 1 - 2 * parity}
    other = {"pipe": 1 - pipe}

    def away(step):
        return lax.rem(data + step, count)

    barrier = pltpu.get_barrier_semaphore()
    met = [partner, peer, other]
    met += [{"dp": away(i)} for i in range(1, count)] if direct else [near]
    for device in met:
        pl.semaphore_signal(barrier, 1, device_id=device, device_id_type=MESH)

    def remote(src, dst, send, recv, device):
        return pltpu.make_async_remote_copy(
            src, dst, send, recv, device_id=device, device_id_type=MESH
        )

    def own_copies():
        pairs_of = [(w_in.at[i], wqkv.at[pl.ds(i * kc, kq)]) for i in range(3)]
        pairs_of += [(w, home_of.at[pl.ds(0, kq)]) for w, home_of in ((w_out, wo), (c_1, w1), (c_2, w2))]
        pairs_of += [(f_1, wf1.at[0]), (f_2, wf2.at[0])]
        for e in range(ex):
            pairs_of.append((xin.at[side * ex + e], xr.at[e, side]))
        for e in range(ex):
            pairs_of.append((cin.at[side * ex + e], cot.at[e, side]))
        return [pltpu.make_async_copy(p, q, lsem.at[i]) for i, (p, q) in enumerate(pairs_of)]

    def x_copy(e):
        return remote(xin.at[(1 - side) * ex + e], xr.at[e, side], xs.at[0, e], xg.at[0, e], peer)

    def cot_copy(e):
        return remote(cin.at[(1 - side) * ex + e], cot.at[e, side], xs.at[1, e], xg.at[1, e], peer)

    def diag_copy():
        return remote(diag.at[0], diag.at[1], ts.at[0], tg.at[0], peer)

    half_kq, part_fq = kq // 2, wf1.shape[1] // 8

    def rows_at(first, n):
        return pl.ds(pl.multiple_of(first, 16), n)

    def small_ref(i):
        return (wqkv, i * kc + kq) if i < 3 else ((wo, w1, w2)[i - 3], kq)

    def big_rows(i, part):
        return rows_at((2 * ((i - W_F1[0]) % 4) + part) * part_fq, part_fq)

    def home(i, part):
        if i >= W_F1[0]:
            return (wf1, wf2)[(i - W_F1[0]) // 4].at[1, big_rows(i, part)]
        ref, first = small_ref(i)
        return ref.at[rows_at(first + part * half_kq, half_kq)]

    def w_copies(i):
        if i >= W_F1[0]:
            src = (f_1, f_2)[(i - W_F1[0]) // 4].at[big_rows(i, parity)]
            return [remote(src, home(i, parity), ys.at[i, 0], yg.at[i, 0], peer)]
        src = w_in.at[i] if i < 3 else (w_out, c_1, c_2)[i - 3]
        ref, first = small_ref(i)
        long, short = DK, half_kq - DK
        froms = (jnp.where(parity == 0, kq - DK, short), jnp.where(parity == 0, 0, DK + short))
        out = []
        for j, (at, n, skip) in enumerate(((froms[0], long, 0), (froms[1], short, long))):
            dst = ref.at[rows_at(first + parity * half_kq + skip, n)]
            out.append(remote(src.at[rows_at(at, n)], dst, ys.at[i, j], yg.at[i, j], peer))
        return out

    def w_start(order):
        for i in order:
            for cp in w_copies(i):
                cp.start()

    def w_pass(i):
        return remote(home(i, parity), home(i, parity), zps.at[i], zpg.at[i], near)

    def w_on(i):
        for cp in w_copies(i):
            cp.wait_recv()
        w_pass(i).start()

    def w_done(i):
        w_pass(i).wait()

    copies = own_copies()
    for cp in copies:
        cp.start()
    values = nn(table_ref[...], hot_ref[pipe])
    at_m = lax.broadcasted_iota(jnp.int32, (1, 2 * seq), 1)
    hidden = jnp.logical_and(jnp.logical_and(at_m > 0, at_m < seq), pipe == 1)
    diag[0, 0:own_heads] = jnp.where(hidden, MASKED, values)
    diag[0, own_heads:] = jnp.zeros((8 - own_heads, 2 * seq), f32)
    pl.semaphore_wait(barrier, len(met))
    diag_copy().start()
    x_copy(0).start()
    w_start((W_Q, W_K, W_V, W_O))

    @pl.when(pipe == 0)
    def _():
        w_start((*W_F1, *W_F2, W_C1, W_C2))

    for e in range(1, ex):
        x_copy(e).start()

    @pl.when(pipe == 1)
    def _():
        w_start((W_C1, W_C2, *W_F2, *W_F1))

    for e in range(ex):
        cot_copy(e).start()
    small[...] = jnp.zeros_like(small)
    diag_copy().wait()
    local_order = [(0, h) for h in range(own_heads)] + [(1, (h + 2) % 3) for h in range(own_heads)]
    for h, (from_side, at) in enumerate(local_order):
        wide = jnp.broadcast_to(diag[from_side, at : at + 1, :], (seq, 2 * seq))
        bias[h] = pltpu.roll(wide, 0, 1, stride=1, stride_axis=0)[:, :seq].astype(bf16)
    for i in (W_Q, W_K, W_V):
        w_on(i)
    for cp in copies:
        cp.wait()
    w_on(W_O)
    for i in (W_Q, W_K, W_V):
        w_done(i)
    wqkv[0:kc] = wqkv[0:kc] * jnp.asarray(0.125, bf16)

    lane = lax.broadcasted_iota(jnp.int32, (1, PAIR), 1)
    half_f = [jnp.where(lane // DK == hh, 1.0, 0.0) for hh in range(2)]
    half_b = [m.astype(bf16) for m in half_f]
    key_at = lax.broadcasted_iota(jnp.int32, (1, seq), 1)

    def key_mask(length):
        return jnp.where(key_at < length, 0.0, MASKED)

    def gather_copy(kind, buf, e):
        return remote(
            buf.at[e, :, core], buf.at[e, :, core], gs.at[kind, e], gr.at[kind, e], partner
        )

    def gather_start(kind, buf, e, value):
        buf[e, :, core] = value.reshape(2, tb, width)
        gather_copy(kind, buf, e).start()

    def gather_use(kind, buf, e, fn):
        def body(i, _):
            ch = lax.rem(core + i, 2)

            @pl.when(i == 1)
            def _():
                gather_copy(kind, buf, e).wait()

            fn(buf[e, :, ch].reshape(rows, width), ch)
            return 0

        lax.fori_loop(0, 2, body, 0)

    def scatter_copy(kind, e, slot):
        return remote(rss.at[slot], rsr.at[slot], ss.at[kind, e], sr.at[kind, e], partner)

    def scatter_send(kind, e, slot, value):
        rss[slot] = value.astype(bf16)
        scatter_copy(kind, e, slot).start()

    def scatter_start(kind, e, slot, fn):
        def body(i, _):
            ch = lax.rem(core + 1 + i, 2)
            rsa[...] = fn(ch)

            @pl.when(i == 0)
            def _():
                scatter_send(kind, e, slot, rsa[...])

            return 0

        lax.fori_loop(0, 2, body, 0)

    def scatter_end(kind, e, slot):
        scatter_copy(kind, e, slot).wait()
        return rsr[slot].astype(f32)

    def scatter(kind, e, slot, fn):
        scatter_start(kind, e, slot, fn)
        return scatter_end(kind, e, slot) + rsa[...]

    def norm(v, row):
        inv = lax.rsqrt(jnp.mean(v * v, axis=-1, keepdims=True) + EPS)
        return (v * inv * gain_ref[row]).astype(bf16)

    def norm_back(v, row, grad):
        inv = lax.rsqrt(jnp.mean(v * v, axis=-1, keepdims=True) + EPS)
        unit = v * inv
        small[pl.ds(row, 1), 0:width] += jnp.sum(grad * unit, axis=0, keepdims=True)
        gg = grad * gain_ref[row]
        return inv * (gg - unit * jnp.mean(gg * unit, axis=-1, keepdims=True))

    def attend(ready, load_q, load_k, load_v, length, use_bias, store_ctx, lse_ref):
        mask = key_mask(length)

        def body(p, _):
            ready(p)
            k, v = load_k(p), load_v(p)
            for yb in range(2):
                q = load_q(yb, p)
                total = scale = None
                lse_t = lse_ref[yb]
                for hh in range(2):
                    h = 2 * p + hh
                    s = nt(q * half_b[hh], k) + mask
                    if use_bias:
                        s = s + bias[h, pl.ds(yb * rows, rows), :].astype(f32)
                    top = jnp.max(s, axis=-1, keepdims=True)
                    w = jnp.exp(s - top)
                    den = jnp.sum(w, axis=-1, keepdims=True)
                    part = nn(w.astype(bf16), v * half_b[hh])
                    total = part if total is None else total + part
                    inv = (1.0 / den) * half_f[hh]
                    scale = inv if scale is None else scale + inv
                    lse_t = jnp.where(lane == h, top + jnp.log(den), lse_t)
                store_ctx(yb, p, (total * scale).astype(bf16))
                lse_ref[yb] = lse_t
            return 0

        lax.fori_loop(0, pairs, body, 0)

    def attend_back(
        load_q, load_k, load_v, load_do, load_o, lse_ref, length, dsacc, store_dq, store_dk, store_dv
    ):
        mask = key_mask(length)

        def body(p, _):
            k, v = load_k(p), load_v(p)
            dk = dv = None
            for yb in range(2):
                q, do = load_q(yb, p), load_do(yb, p)
                both = do.astype(f32) * load_o(yb, p).astype(f32)
                lse_t = lse_ref[yb]
                dq = None
                for hh in range(2):
                    h = 2 * p + hh
                    qm, dom = q * half_b[hh], do * half_b[hh]
                    lse_c = jnp.sum(jnp.where(lane == h, lse_t, 0.0), axis=-1, keepdims=True)
                    delta = jnp.sum(both * half_f[hh], axis=-1, keepdims=True)
                    s = nt(qm, k) + mask
                    if dsacc is not None:
                        s = s + bias[h, pl.ds(yb * rows, rows), :].astype(f32)
                    w = jnp.exp(s - lse_c)
                    ds = w * (nt(dom, v) - delta)
                    wb, db = w.astype(bf16), ds.astype(bf16)
                    if dsacc is not None:
                        at = pl.ds(yb * rows, rows)
                        dsacc[h, at, :] = (dsacc[h, at, :].astype(f32) + ds).astype(bf16)
                    dvp, dkp, dqp = tn(wb, dom), tn(db, qm), nn(db, k * half_b[hh])
                    dv = dvp if dv is None else dv + dvp
                    dk = dkp if dk is None else dk + dkp
                    dq = dqp if dq is None else dq + dqp
                store_dq(yb, p, dq.astype(bf16))
            store_dk(p, dk.astype(bf16))
            store_dv(p, dv.astype(bf16))
            return 0

        lax.fori_loop(0, pairs, body, 0)

    def block_of(ref, *at):
        def lanes_at(first, p):
            return pl.ds(pl.multiple_of(first + p * PAIR, PAIR), PAIR)

        def load_rows(first=0):
            return lambda yb, p: ref[(*at, yb, slice(None), slice(None), lanes_at(first, p))].reshape(rows, PAIR)

        def load_all(first=0):
            return lambda p: ref[(*at, slice(None), slice(None), slice(None), lanes_at(first, p))].reshape(seq, PAIR)

        def store_rows(first=0):
            def store(yb, p, value):
                ref[(*at, yb, slice(None), slice(None), lanes_at(first, p))] = value.reshape(2, tb, PAIR)

            return store

        def store_all(first=0):
            def store(p, value):
                ref[(*at, slice(None), slice(None), slice(None), lanes_at(first, p))] = value.reshape(2, 2, tb, PAIR)

            return store

        return load_rows, load_all, store_rows, store_all

    def pair_of(ref, e, i):
        def load(p):
            return ref[e, p, i].reshape(seq, PAIR)

        def store(p, value):
            ref[e, p, i] = value.reshape(2, 2, tb, PAIR)

        return load, store

    def in_rows(e):
        return xr[e].reshape(rows, width).astype(f32)

    def cot_rows(e):
        return cot[e].reshape(rows, width)

    def half_rows(ref, e, ch, count):
        return ref[e, :, ch].reshape(rows, count)

    def self_forward(e, slot, length, middle=None):
        x_copy(e).wait()
        gather_start(G_IN, fin, e, norm(in_rows(e), 0))

        def project(a, ch):
            qkv[e, :, ch] = nt(a, wqkv[...]).astype(bf16).reshape(2, tb, 3 * kc)

        gather_use(G_IN, fin, e, project)
        lr, la, _, _ = block_of(qkv, e)
        _, _, store_ctx, _ = block_of(ctx, e)

        def ready(p):
            pass

        attend(ready, lr(), la(kc), la(2 * kc), length, True, store_ctx(), lse.at[e])

        @pl.when(e == 0)
        def _():
            w_done(W_O)

        if middle is not None:
            middle()

        h1[e] = in_rows(e) + scatter(
            S_ATT, e, slot, lambda ch: nn(half_rows(ctx, e, ch, kc), wo[...])
        )

    def ffn_expand(e, src, act, dg, has_grad):
        gather_start(G_FFN, ffnf, e, norm(src[e], 2))

        def expand(a, ch):
            for i in range(2):
                pre = nn(a, wf1[i])
                sq = pre * pre
                th = jnp.tanh(0.7978845608028654 * pre * (1.0 + 0.044715 * sq))
                gate = 0.5 + 0.5 * th
                slope = gate + (0.5 * 0.7978845608028654) * pre * (1.0 - th * th) * (
                    1.0 + (3 * 0.044715) * sq
                )
                lanes = pl.ds(i * fq, fq)
                act[e, :, ch, :, lanes] = (pre * gate).astype(bf16).reshape(2, tb, fq)
                if has_grad:
                    slope = slope * dg[e, :, ch, :, lanes].reshape(rows, fq).astype(f32)
                dg[e, :, ch, :, lanes] = slope.astype(bf16).reshape(2, tb, fq)

        gather_use(G_FFN, ffnf, e, expand)

    def ffn_out_part(e, act):
        return lambda ch: nn(half_rows(act, e, ch, fc), wf2[...].reshape(fc, width))

    def ffn_in_part(e, dg):
        def part(ch):
            both = half_rows(dg, e, ch, fc)
            return nt(both[:, :fq], wf1[0]) + nt(both[:, fq:], wf1[1])

        return part

    def ffn_contract(e, dg, has_slope):
        def contract(a, ch):
            for i in range(2):
                lanes = pl.ds(i * fq, fq)
                dact = nt(a, wf2[i])
                if has_slope:
                    dact = dact * dg[e, :, ch, :, lanes].reshape(rows, fq).astype(f32)
                dg[e, :, ch, :, lanes] = dact.astype(bf16).reshape(2, tb, fq)

        gather_use(G_DFFN, fffn, e, contract)

    def context_grad(kind, buf, e, w):
        def project(a, ch):
            dctx[0, :, ch] = nt(a, w[...]).astype(bf16).reshape(2, tb, kc)

        gather_use(kind, buf, e, project)

    def self_back(e, slot, length, dsacc, between=None):
        gather_start(G_DATT, fatt, e, r2[e].astype(bf16))
        context_grad(G_DATT, fatt, e, wo)
        if between is not None:
            between()
        lr, la, sr_, sa_ = block_of(qkv, e)
        ldo = block_of(dctx, 0)[0]
        lo = block_of(ctx, e)[0]
        attend_back(
            lr(), la(kc), la(2 * kc), ldo(), lo(), lse.at[e], length, dsacc,
            sr_(), sa_(kc), sa_(2 * kc),
        )
        dn = scatter(S_DIN, e, slot, lambda ch: nn(half_rows(qkv, e, ch, 3 * kc), wqkv[...]))
        hand_out(1, e, (r2[e] + norm_back(in_rows(e), 0, dn)).astype(bf16), e == ex - 1)

    def out_copies(kind, e):
        at, out = side * ex + e, (sec_out, ing_out)[kind]
        return (
            pltpu.make_async_copy(out_rows.at[e, side], out.at[at], lsem.at[8 + kind * ex + e]),
            remote(out_rows.at[e, 1 - side], out.at[at], os.at[kind, e], og.at[kind, e], peer),
        )

    def hand_out(kind, e, value, later=False):
        if kind == 1:
            for cp in out_copies(0, e):
                cp.wait()
        out_rows[e] = value.reshape(2, tb, width)

        def start():
            for cp in out_copies(kind, e):
                cp.start()

        pl.when(jnp.logical_not(later))(start)

    def pass_copy(e, p):
        return remote(kvs.at[e, p], kvr.at[e, p], ps.at[e, p], pr.at[e, p], other)

    def y_copy(u):
        return remote(ysend.at[u], yrecv.at[u], us.at[u], ug.at[u], peer)

    def all_rows(ref, lanes):
        n = lanes.size
        return ref[:, :, :, :, lanes].reshape(ex * seq, n)

    half = width // 2

    def lanes_of(r):
        return pl.ds(pl.multiple_of(r * half, PAIR), half)

    def stage_copy(gst, r, i, dst, u):
        return pltpu.make_async_copy(
            gst.at[r, :, pl.ds(i * kc, kc)], dst.at[u, lanes_of(r)], lsem.at[2 * r + i]
        )

    def drain(gst, r):
        for i in range(2):
            stage_copy(gst, r, i, gown, 0).wait()

    def ffn_grads(u, src, feed_ref, gst, pending):
        def to(dst, first, wait, sent):
            def body(r, _):
                if wait:
                    drain(gst, r)
                if sent:

                    @pl.when(r == 1)
                    def _():
                        for i in range(2):
                            y_copy(u + i).start()

                rhs = all_rows(feed_ref, pl.ds(first, fq))
                gst[r] = tn(all_rows(src, lanes_of(r)), rhs).astype(bf16)
                for i in range(2):
                    stage_copy(gst, r, i, dst, u + i).start()
                return 0

            lax.fori_loop(0, 2, body, 0)

        to(ysend, fq, pending, False)
        to(gown, 0, True, True)

    def pair_grads(u, lhs_a, load_a, lhs_b, load_b, scale, gst, pending):
        def body(r, _):
            if pending:
                drain(gst, r)
            a = tn(all_rows(lhs_a, lanes_of(r)), load_a())
            if scale is not None:
                a = a * scale
            b = tn(all_rows(lhs_b, lanes_of(r)), load_b())
            low = lane < DK
            a1, b1 = a[:, PAIR : 2 * PAIR], b[:, PAIR : 2 * PAIR]
            mix_own = jnp.where(low, a1, pltpu.roll(b1, DK, 1))
            mix_peer = jnp.where(low, pltpu.roll(a1, DK, 1), b1)
            for j, part in enumerate(
                (a[:, :PAIR], mix_own, b[:, :PAIR], a[:, 2 * PAIR :], mix_peer, b[:, 2 * PAIR :])
            ):
                gst[r, :, j * PAIR : (j + 1) * PAIR] = part.astype(bf16)
            for i, dst in enumerate((gown, ysend)):
                stage_copy(gst, r, i, dst, u).start()
            return 0

        lax.fori_loop(0, 2, body, 0)
        for r in range(2):
            drain(gst, r)
        y_copy(u).start()

    def z_copy(u, step):
        block = width // count
        at = away(step)
        return remote(
            zs.at[u, pl.ds(pl.multiple_of(at * block, 16), block)], zr.at[u, step - 1],
            vs.at[u, step - 1], vg.at[u, step - 1], {"dp": at},
        )

    def pump(u, gst):
        y_copy(u).wait_recv()
        loads, stores = [], []
        for r in range(2):
            own, came = gst.at[r, :, pl.ds(0, kc)], gst.at[r, :, pl.ds(kc, kc)]
            loads.append(pltpu.make_async_copy(gown.at[u, lanes_of(r)], own, lsem.at[4 + r]))
            loads.append(pltpu.make_async_copy(yrecv.at[u, lanes_of(r)], came, lsem.at[6 + r]))
            stores.append(pltpu.make_async_copy(own, zs.at[u, lanes_of(r)], lsem.at[4 + r]))
        for cp in loads:
            cp.start()
        for r in range(2):
            for cp in loads[2 * r : 2 * r + 2]:
                cp.wait()
            gst[r, :, 0:kc] = (
                gst[r, :, 0:kc].astype(f32) + gst[r, :, kc : 2 * kc].astype(f32)
            ).astype(bf16)
            stores[r].start()
        for cp in stores:
            cp.wait()
        if direct:
            for step in range(1, count):
                z_copy(u, step).start()

    def finish(u, va, vf):
        block = width // count
        for step in range(1, count):
            z_copy(u, step).wait()
        mine = pl.ds(pl.multiple_of(data * block, 16), block)
        cps = [pltpu.make_async_copy(zs.at[u, mine], va.at[pl.ds(0, block)], lsem.at[0])]
        for step in range(1, count):
            cps.append(
                pltpu.make_async_copy(
                    zr.at[u, step - 1], va.at[pl.ds(step * block, block)], lsem.at[step]
                )
            )
        for cp in cps:
            cp.start()
        for cp in cps:
            cp.wait()
        total = va[0:block].astype(f32)
        for step in range(1, count):
            total = total + va[step * block : (step + 1) * block].astype(f32)
        vf[...] = total
        cp = pltpu.make_async_copy(vf, fin_out.at[u], lsem.at[0])
        cp.start()
        cp.wait()

    def small_near():
        first = remote(small.at[pl.ds(0, 8)], small_c, ms.at[0], mg.at[0], partner)
        first.start()
        first.wait()
        small[0:8] += small_c[...]
        small_peer().start()

    def small_peer():
        return remote(small, small_y, ms.at[1], mg.at[1], peer)

    def small_far():
        return [
            remote(small, small_z.at[i - 1], ms.at[1 + i], mg.at[1 + i], {"dp": away(i)})
            for i in range(1, count)
        ]

    def small_middle():
        small_peer().wait()
        small[0:8] += small_y[0:8]
        for h in range(own_heads):
            at = 8 + own_heads + (h + 1) % 3
            small[8 + h : 9 + h] += small_y[at : at + 1]
        if direct:
            for cp in small_far():
                cp.start()

    def small_end():
        total = small[...]
        if direct:
            for cp in small_far():
                cp.wait()
            for i in range(1, count):
                total = total + small_z[i - 1]
        small_out[...] = total

    def bias_grads(dsacc):
        at_r = lax.broadcasted_iota(jnp.int32, (seq, seq), 0)
        at_c = lax.broadcasted_iota(jnp.int32, (seq, seq), 1)
        flip = jnp.where(at_r + at_c == seq - 1, 1.0, 0.0).astype(bf16)

        def body(h, _):
            reverse = nn(dsacc[h], flip)
            wide = jnp.concatenate([reverse, jnp.zeros((seq, seq), f32)], axis=1)
            wide = pltpu.roll(wide, 0, 1, stride=1, stride_axis=0)
            small[pl.ds(8 + h, 1), :] = jnp.sum(wide, axis=0, keepdims=True)
            return 0

        lax.fori_loop(0, heads, body, 0)

    def loop(fn):
        def body(e, _):
            fn(e)
            return 0

        lax.fori_loop(0, ex, body, 0)

    def last_grads(dsacc, gst, between, small_first):
        def small_now():
            bias_grads(dsacc)
            small_near()

        lanes = [pl.ds(i * kc, kc) for i in range(3)]
        if small_first:
            small_now()
            between()
        pair_grads(
            5, fin, lambda: all_rows(qkv, lanes[0]), fin, lambda: all_rows(qkv, lanes[1]),
            0.125, gst, False,
        )
        pair_grads(
            6, fin, lambda: all_rows(qkv, lanes[2]), fatt, lambda: all_rows(ctx, lanes[0]),
            None, gst, False,
        )
        if not small_first:
            between()
            small_now()
        for cp in out_copies(1, ex - 1):
            cp.start()

    def collect(order, done, gst, small_first):
        def run(va, vf):
            n = len(order)
            ended = 0
            for k in range(done, n):
                if direct:
                    while ended <= k - 3:
                        finish(order[ended], va, vf)
                        ended += 1
                if k == n - 1 and small_first:
                    small_middle()
                pump(order[k], gst)
            if not small_first:
                small_middle()
            if direct:
                while ended < n:
                    finish(order[ended], va, vf)
                    ended += 1
            small_end()
            for u in order:
                y_copy(u).wait_send()
            for e in range(ex):
                for cp in out_copies(1, e):
                    cp.wait()

        V = pltpu.VMEM
        pl.run_scoped(run, V((width, kc), bf16), V((width // count, kc), f32))

    def begun():
        for i in range(WEIGHTS):
            for cp in w_copies(i):
                cp.wait_send()
        for e in range(ex):
            cot_copy(e).wait_send()

    V = pltpu.VMEM
    feed = V((ex, 2, 2, tb, fc), bf16)
    grad_stage = V((2, half, 2 * kc), bf16)
    score_sums = V((heads, seq, seq), bf16)
    last = ex - 1

    def pass_all(e, fn):
        for p in range(pairs):
            fn(pass_copy(e, p))

    def wide(ref, e, i, ch):
        return jnp.concatenate([ref[e, p, i, :, ch].reshape(rows, PAIR) for p in range(pairs)], 1)

    @pl.when(pipe == 0)
    def _():
        def own_length(e):
            return len_ref[0, side * ex + e]

        def keys(i):
            return lambda: jnp.concatenate(
                [kvr[:, p, i].reshape(ex * seq, PAIR) for p in range(pairs)], 1
            )

        def run(act, dg, dsacc, gst):
            def ahead(e):
                def middle():
                    pl.when(e == 0)(lambda: w_on(W_F1[0]))

                self_forward(e, 0, own_length(e), middle)

                @pl.when(e == 0)
                def _():
                    for i in (*W_F1[1:], *W_F2[:2]):
                        w_on(i)
                    for i in W_F1:
                        w_done(i)

                ffn_expand(e, h1, act, dg, False)

                @pl.when(e == 0)
                def _():
                    for i in W_F2[2:]:
                        w_on(i)
                    for i in W_F2:
                        w_done(i)
                    for i in (W_C1, W_C2):
                        w_on(i)

                r2[e] = h1[e] + scatter(S_FFN, e, 1, ffn_out_part(e, act))
                memory = norm(r2[e], 1)
                gather_start(G_MID, mid, e, memory)
                hand_out(0, e, memory)

                @pl.when(e == 0)
                def _():
                    for i in (W_C1, W_C2):
                        w_done(i)

                def project(a, ch):
                    for i, w in enumerate((w1, w2)):
                        out = nt(a, w[...]).astype(bf16)
                        for p in range(pairs):
                            kvs[e, p, i, :, ch] = out[:, p * PAIR : (p + 1) * PAIR].reshape(
                                2, tb, PAIR
                            )

                gather_use(G_MID, mid, e, project)
                pass_all(e, lambda cp: cp.start())

            def back(e):
                pass_all(e, lambda cp: cp.wait())
                cot_copy(e).wait_recv()

                def partial_sum(ch):
                    return nn(wide(kvr, e, 0, ch), w1[...]) + nn(wide(kvr, e, 1, ch), w2[...])

                scatter_start(S_DMEM, e, 1, partial_sum)

                @pl.when(e == last)
                def _():
                    pair_grads(4, mid, keys(0), mid, keys(1), None, gst, False)

                dmem = cot_rows(e).astype(f32) + (scatter_end(S_DMEM, e, 1) + rsa[...])
                r2[e] = norm_back(r2[e], 1, dmem)
                gather_start(G_DFFN, fffn, e, r2[e].astype(bf16))
                ffn_contract(e, dg, True)
                scatter_start(S_DFFN, e, 0, ffn_in_part(e, dg))

                @pl.when(e == last)
                def _():
                    ffn_grads(2, fffn, act, gst, False)

                dn = scatter_end(S_DFFN, e, 0) + rsa[...]
                r2[e] += norm_back(h1[e], 2, dn)

                @pl.when(e == last)
                def _():
                    for r in range(2):
                        drain(gst, r)
                    pump(4, gst)
                    ffn_grads(0, ffnf, dg, gst, False)
                    for r in range(2):
                        drain(gst, r)

                self_back(
                    e, 0, own_length(e), dsacc, lambda: pl.when(e == last)(lambda: pump(2, gst))
                )

            loop(ahead)
            dsacc[...] = jnp.zeros_like(dsacc)
            begun()
            loop(back)

        def outer(dsacc, gst):
            pl.run_scoped(lambda act, dg: run(act, dg, dsacc, gst), feed, feed)
            pump(3, gst)
            last_grads(dsacc, gst, lambda: pump(0, gst), True)
            collect((4, 2, 3, 0, 1, 5, 6), 4, gst, True)

        pl.run_scoped(outer, score_sums, grad_stage)

    @pl.when(pipe == 1)
    def _():
        def own_length(e):
            return len_ref[1, side * ex + e]

        def run(act, dg, cq, cctx, clse, gst):
            def first(e):
                self_forward(e, lax.rem(e, 2), own_length(e))
                gather_start(G_MID, mid, e, norm(h1[e], 1))

            def second(e):
                def project(a, ch):
                    cq[e, :, ch] = nt(a, w1[...]).astype(bf16).reshape(2, tb, kc)

                gather_use(G_MID, mid, e, project)

            def third(e):
                cot_copy(e).wait_recv()
                gather_start(G_DFFN, fffn, e, cot_rows(e))

            def there_and_back(e):
                lq, _, sq, _ = block_of(cq, e)
                (lk, _), (lv, _) = pair_of(kvr, e, 0), pair_of(kvr, e, 1)
                lc, _, sc, _ = block_of(cctx, e)
                source_length = len_ref[0, side * ex + e]
                attend(
                    lambda p: pass_copy(e, p).wait_recv(), lq(), lk, lv, source_length, False,
                    sc(), clse,
                )
                r2[e] = h1[e] + scatter(
                    S_MID, e, 1, lambda ch: nn(half_rows(cctx, e, ch, kc), w2[...])
                )
                ffn_expand(e, r2, act, dg, True)
                scatter_start(S_DFFN, e, 0, ffn_in_part(e, dg))
                scatter_send(S_FFN, e, 2, ffn_out_part(e, act)(1 - core))
                dn = scatter_end(S_DFFN, e, 0) + rsa[...]
                h2 = r2[e]
                grad = cot_rows(e).astype(f32) + norm_back(h2, 2, dn)
                rsa[...] = h2
                r2[e] = grad
                gather_start(G_DMID, fmid, e, grad.astype(bf16))
                out = rsa[...] + ffn_out_part(e, act)(core)
                hand_out(0, e, (out + scatter_end(S_FFN, e, 2)).astype(bf16))
                context_grad(G_DMID, fmid, e, w2)
                ldo = block_of(dctx, 0)[0]
                sk, sv = pair_of(kvs, e, 0)[1], pair_of(kvs, e, 1)[1]

                def store_values(p, value):
                    sv(p, value)
                    pass_copy(e, p).start()

                attend_back(
                    lq(), lk, lv, ldo(), lc(), clse, source_length, None, sq(), sk, store_values
                )


            def finish_cross(e):
                dn = scatter(S_DMID, e, lax.rem(e, 2), lambda ch: nn(half_rows(cq, e, ch, kc), w1[...]))
                r2[e] += norm_back(h1[e], 1, dn)

            loop(first)
            for i in (W_C1, W_C2, *W_F2[:2]):
                w_on(i)
            for i in (W_C1, W_C2):
                w_done(i)
            w1[...] = w1[...] * jnp.asarray(0.125, bf16)
            loop(second)
            for i in (*W_F2[2:], *W_F1):
                w_on(i)
            loop(third)
            for i in W_F2:
                w_done(i)
            loop(lambda e: ffn_contract(e, dg, False))
            for i in W_F1:
                w_done(i)
            begun()
            loop(there_and_back)
            ffn_grads(2, fffn, act, gst, False)
            ffn_grads(0, ffnf, dg, gst, True)
            lanes = pl.ds(0, kc)
            pair_grads(
                4, mid, lambda: all_rows(cq, lanes), fmid, lambda: all_rows(cctx, lanes),
                0.125, gst, True,
            )
            pump(2, gst)
            loop(finish_cross)

        pl.run_scoped(
            run, feed, feed, V((ex, 2, 2, tb, kc), bf16), V((ex, 2, 2, tb, kc), bf16),
            V((2, rows, PAIR), f32), grad_stage,
        )

        def outer(dsacc, gst):
            dsacc[...] = jnp.zeros_like(dsacc)

            def body(e):
                def between():
                    pl.when(e == 0)(lambda: pump(3, gst))
                    pl.when(e == last)(lambda: pump(4, gst))

                self_back(e, 1 - lax.rem(e, 2), own_length(e), dsacc, between)
                pl.when(e < last)(lambda: pump(e, gst))

            loop(body)
            loop(lambda e: pass_all(e, lambda cp: cp.wait_send()))
            last_grads(dsacc, gst, lambda: None, False)
            collect((2, 3, 0, 1, 4, 5, 6), 5, gst, False)

        pl.run_scoped(outer, score_sums, grad_stage)


def run_sections(x, cot, w_in, w_out, c_1, c_2, f_1, f_2, gains, lens, table, hot, direct):
    batch, tb, width = x.shape
    ex = batch // 2
    rows, seq = 2 * tb, 4 * tb
    kq, fq = w_out.shape[0], f_1.shape[1]
    kc, fc = 2 * kq, 2 * fq
    heads = kc // DK
    count = lax.axis_size("dp")
    vmem = pl.BlockSpec(memory_space=pltpu.VMEM)
    hbm = pl.BlockSpec(memory_space=pl.ANY)
    smem = pl.BlockSpec(memory_space=pltpu.SMEM)
    full = (ex, 2, 2, tb)
    units = (7, width, kc)
    V = pltpu.VMEM
    D = pltpu.SemaphoreType.DMA
    S = jax.ShapeDtypeStruct
    scratch = [
        V((3 * kc, width), bf16), V((kc, width), bf16), V((kc, width), bf16), V((kc, width), bf16),
        V((2, width, fq), bf16), V((2, fq, width), bf16), V((heads, seq, seq), bf16),
        V((ex, 2, tb, width), bf16), V((ex, 2, tb, width), bf16),
        V((ex, 2, tb, width), bf16),
        V((*full, width), bf16),
        V((*full, 3 * kc), bf16),
        V((*full, kc), bf16),
        V((ex, 2, rows, PAIR), f32),
        V((ex, rows, width), f32),
        V((*full, width), bf16),
        V((*full, width), bf16),
        V((ex, kc // PAIR, 2, 2, 2, tb, PAIR), bf16),
        V((ex, kc // PAIR, 2, 2, 2, tb, PAIR), bf16),
        V((ex, rows, width), f32),
        V((*full, width), bf16),
        V((*full, width), bf16),
        V((1, 2, 2, tb, kc), bf16),
        V((rows, width), f32),
        V((3, rows, width), bf16),
        V((3, rows, width), bf16),
        V((2, 8, 2 * seq), f32),
        V((16, 2 * seq), f32), V((8, 2 * seq), f32), V((16, 2 * seq), f32),
        V((max(1, count - 1) if direct else 1, 16, 2 * seq), f32),
        D((8 + 2 * ex,)),
        D((2, ex)), D((2, ex)), D((1,)), D((1,)), D((WEIGHTS, 2)), D((WEIGHTS, 2)), D((WEIGHTS,)), D((WEIGHTS,)),
        D((6, ex)), D((6, ex)), D((7, ex)), D((7, ex)), D((ex, kc // PAIR)), D((ex, kc // PAIR)),
        D((2, ex)), D((2, ex)), D((7,)), D((7,)), D((7, 3)), D((7, 3)), D((5,)), D((5,)),
    ]
    slots = count - 1 if direct else 1
    return pl.pallas_call(
        partial(section_kernel, direct=direct),
        out_shape=(
            S((batch, tb, width), bf16),
            S((batch, tb, width), bf16),
            S(units, bf16),
            S((7, slots, width // count if direct else 16, kc), bf16),
            S((7, width // count if direct else 8, kc), f32),
            S((16, 2 * seq), f32),
            S(units, bf16),
            S(units, bf16),
            S(units, bf16),
        ),
        in_specs=[hbm] * 8 + [vmem, smem, vmem, vmem],
        out_specs=(hbm, hbm, hbm, hbm, hbm, vmem, hbm, hbm, hbm),
        scratch_shapes=scratch,
        compiler_params=pltpu.CompilerParams(
            collective_id=0, has_side_effects=True, vmem_limit_bytes=64 * 2**20 - 65536
        ),
        name="sections",
    )(x, cot, w_in, w_out, c_1, c_2, f_1, f_2, gains, lens, table, hot)


def ends_kernel(
    sec, ing, fin_hbm, small, hot_ref,
    o_sec, o_ing, o_in, o_out, o_c1, o_c2, o_f1, o_f2, o_bias, o_gain,
    low_rows, high_rows, out_rows, fin, lsem, ssem,
):
    batch = ing.shape[0]
    whole_in = pltpu.make_async_copy(sec, out_rows, lsem.at[batch])
    whole = pltpu.make_async_copy(out_rows, o_sec.at[0], lsem.at[batch])
    sums_in = pltpu.make_async_copy(fin_hbm, fin, lsem.at[batch + 1])
    loads = [pltpu.make_async_copy(ing.at[e], low_rows.at[e], lsem.at[e]) for e in range(batch)]
    stores = [
        pltpu.make_async_copy(high_rows.at[e], o_ing.at[0, e], ssem.at[e]) for e in range(batch)
    ]
    for cp in loads:
        cp.start()
    sums_in.start()
    whole_in.start()
    for e in range(batch):
        loads[e].wait()
        high_rows[e] = low_rows[e].astype(f32)
        stores[e].start()
    whole_in.wait()
    whole.start()
    sums_in.wait()

    def first(u):
        return jnp.concatenate([fin[u, :, :PAIR], fin[u, :, PAIR : PAIR + DK]], 1)

    def second(u):
        return jnp.concatenate([fin[u, :, 2 * PAIR :], fin[u, :, PAIR + DK : 2 * PAIR]], 1)

    o_in[0, 0], o_in[0, 1], o_in[0, 2] = first(5), second(5), first(6)
    o_out[0] = second(6).T
    o_c1[0], o_c2[0] = first(4), second(4)
    kc = fin.shape[2]
    for i in range(2):
        o_f1[0, :, i * kc : (i + 1) * kc] = fin[i]
        o_f2[0, :, i * kc : (i + 1) * kc] = fin[2 + i]
    sums = small[8:16, :]
    high = sums.astype(bf16)
    rest = sums - high.astype(f32)
    middle = rest.astype(bf16)
    low = (rest - middle.astype(f32)).astype(bf16)
    hot = hot_ref[lax.axis_index("pipe"), lax.axis_index("dp")]
    bias = nt(high, hot) + nt(middle, hot) + nt(low, hot)
    for h in range(o_bias.shape[0]):
        o_bias[h] = bias[h : h + 1]
    share = o_gain.shape[2]
    at = (lax.axis_index("dp") * lax.axis_size("tensor") + lax.axis_index("tensor")) * share
    moved = pltpu.roll(small[0:8, :], lax.rem(small.shape[1] - at, small.shape[1]), 1)
    for i in range(3):
        o_gain[i] = moved[i : i + 1, :share]
    whole.wait()
    for cp in stores:
        cp.wait()


def ends(sec, ing, fin, small, hot, share, heads):
    batch, tb, width = ing.shape
    _, block, kc = fin.shape
    kq = kc // 2
    S = jax.ShapeDtypeStruct
    D = pltpu.SemaphoreType.DMA
    vmem = pl.BlockSpec(memory_space=pltpu.VMEM)
    hbm = pl.BlockSpec(memory_space=pl.ANY)
    return pl.pallas_call(
        ends_kernel,
        out_shape=(
            S((1, batch, tb, width), bf16), S((1, batch, tb, width), f32),
            S((1, 3, block, kq), f32), S((1, kq, block), f32),
            S((1, block, kq), f32), S((1, block, kq), f32), S((1, block, 2 * kc), f32),
            S((1, block, 2 * kc), f32), S((heads, 1, hot.shape[2]), f32), S((3, 1, share), f32),
        ),
        in_specs=[hbm, hbm, hbm, vmem, vmem],
        out_specs=(hbm, hbm) + (vmem,) * 8,
        scratch_shapes=[
            pltpu.VMEM((batch, tb, width), bf16), pltpu.VMEM((batch, tb, width), f32),
            pltpu.VMEM((batch, tb, width), bf16), pltpu.VMEM(fin.shape, f32), D((batch + 2,)), D((batch,)),
        ],
        compiler_params=pltpu.CompilerParams(vmem_limit_bytes=64 * 2**20 - 65536),
        name="ends",
    )(sec, ing, fin, small, hot)


def local(
    section_input, lengths, norm_gain, attn_in, attn_out, cross_first, cross_second,
    ffn_in, ffn_out, rel_bias, out_grad,
):
    enc = lax.axis_index("pipe") == 0
    tb, width = section_input.shape[2:]
    seq = tb * lax.axis_size("tensor")
    kq = attn_out.shape[1]
    data = lax.axis_size("dp")
    at_data = lax.axis_index("dp")
    direct = data <= 4 and (width // data) % 16 == 0
    heads = kq // DK

    offsets = list(range(seq)) + [0] + list(range(-seq + 1, 0))
    both = [np.array(bucket_list(offsets, ways)) for ways in (True, False)]
    hot = np.stack([np.arange(NB)[:, None] == spots[None] for spots in both])
    turned = [seq - 1 - m for m in range(2 * seq)]
    hot_m = np.stack(
        [np.arange(NB)[:, None] == np.array(bucket_list(turned, ways)) for ways in (True, False)]
    )

    def across(w):
        return jnp.swapaxes(w, -1, -2)

    sec, ing, zs, _, fin, small, _, _, _ = run_sections(
        section_input[0], out_grad[0], across(attn_in[0]), attn_out[0], across(cross_first[0]),
        across(cross_second[0]), ffn_in[0], ffn_out[0], jnp.swapaxes(norm_gain, 0, 1),
        lengths.T, rel_bias[0].T, jnp.asarray(hot, bf16), direct,
    )
    share = width // (data * lax.axis_size("tensor"))
    if direct:
        by_data = jnp.asarray(hot_m.reshape(2, data, NB // data, 2 * seq), bf16)
        sec, ing, w_in, w_out, c_1, c_2, f_1, f_2, bias, gains = ends(
            sec, ing, fin, small, by_data, share, heads
        )
        return (
            sec, ing, w_in, w_out, c_1, c_2, f_1, across(f_2),
            jnp.transpose(bias, (1, 2, 0)), jnp.swapaxes(gains, 0, 1),
        )

    packed = zs.reshape(7, data, width // data, 2 * kq)
    shard = lax.psum_scatter(packed, "dp", scatter_dimension=1, tiled=False).astype(f32)
    hot_m = jnp.where(enc, jnp.asarray(hot_m[0], f32), jnp.asarray(hot_m[1], f32))
    bsum = jnp.einsum("bm,hm->bh", hot_m, small[8 : 8 + heads], precision=lax.Precision.HIGHEST)
    bias_grad = lax.psum_scatter(bsum, "dp", scatter_dimension=0, tiled=True)
    gains = lax.psum(small[:3, :width], "dp")
    at = (at_data * lax.axis_size("tensor") + lax.axis_index("tensor")) * share
    gain_grad = lax.dynamic_slice_in_dim(gains, at, share, 1)

    def first_of(u):
        return jnp.concatenate([shard[u, :, :PAIR], shard[u, :, PAIR : PAIR + DK]], 1)

    def second_of(u):
        return jnp.concatenate([shard[u, :, 2 * PAIR :], shard[u, :, PAIR + DK : 2 * PAIR]], 1)

    return (
        sec[None],
        ing[None].astype(f32),
        jnp.stack([first_of(5), second_of(5), first_of(6)])[None],
        second_of(6).T[None],
        first_of(4)[None],
        second_of(4)[None],
        jnp.concatenate([shard[0], shard[1]], 1)[None],
        jnp.concatenate([shard[2], shard[3]], 1).T[None],
        bias_grad[None],
        gain_grad[None],
    )


def solution(mesh):
    placed = (
        P("pipe", "dp", "tensor", None),
        P("dp", None),
        P("pipe", None, None),
        P("pipe", None, None, "tensor"),
        P("pipe", "tensor", None),
        P("pipe", None, "tensor"),
        P("pipe", None, "tensor"),
        P("pipe", None, "tensor"),
        P("pipe", "tensor", None),
        P("pipe", None, "tensor"),
        P("pipe", "dp", "tensor", None),
    )
    return jax.shard_map(
        local,
        mesh=mesh,
        in_specs=placed,
        out_specs=(
            P("pipe", "dp", "tensor", None),
            P("pipe", "dp", "tensor", None),
            P("pipe", None, "dp", "tensor"),
            P("pipe", "tensor", "dp"),
            P("pipe", "dp", "tensor"),
            P("pipe", "dp", "tensor"),
            P("pipe", "dp", "tensor"),
            P("pipe", "tensor", "dp"),
            P("pipe", "dp", "tensor"),
            P("pipe", None, ("dp", "tensor")),
        ),
        check_vma=False,
    )
```
